256 devices in a mesh: seq: 128 (over z, x, y), section: 2 (over core).
Axes of the slice: x: 4, y: 4, z: 8, core: 2. Of those that a mesh axis runs over, the one named last changes fastest.
Arguments:
- layer_input: bfloat16 [2, 16384, 512], P('section', 'seq'), may hold values from -6 to 6
- conv_out: bfloat16 [2, 2, 16384, 512], P('section', None, 'seq'), may hold values from -6 to 6
- filters: bfloat16 [2, 2, 16384, 512], P('section', None, 'seq'), may hold values from -1.1 to 1.1
- skip_gain: float32 [2, 2, 512], P('section'), may hold values from -4 to 4
- weight_in: bfloat16 [2, 512, 1536], P('section'), may hold values from -0.25 to 0.25
- weight_out: bfloat16 [2, 512, 512], P('section'), may hold values from -0.25 to 0.25
- grad_output: bfloat16 [16384, 512], P('seq'), may hold values from -18 to 18
Outputs:
- grad_input: bfloat16 [2, 16384, 512], P('section', 'seq')
- grad_filter: bfloat16 [2, 2, 16384, 512], P('section', None, 'seq')
- grad_skip: float32 [2, 2, 512], P('section')
The draws below stay inside these ranges and needn't reach their ends.
All inputs are finite; a program needn't handle non-finite values.
Results may differ from the reference program's by a relative error of at most 0.009.
Values may be sent and summed in bfloat16 or wider, within the bound.
No kernel may reach another device: no remote copies, remote signals or barrier semaphores. Data moves between devices by JAX's collectives and lax.ppermute only.
A program may use at most 128 MiB of HBM per device.

```python
import math
import jax
import jax.numpy as jnp
from jax import lax

D = 512
SEQUENCE_TOKENS = 16384
N_SECTION = 2


def draw_filters(key, part):
    key = jax.random.fold_in(key, 11)
    jitter_random_key, span_random_key, spike_random_key = jax.random.split(key, 3)
    full_shape = (N_SECTION, 2, SEQUENCE_TOKENS, D)
    noise_field = jnp.clip(jax.random.normal(jitter_random_key, full_shape, jnp.float32), -6.0, 6.0)
    lowest = 32.0
    highest = 4.0 * SEQUENCE_TOKENS
    spread = jax.random.uniform(span_random_key, (N_SECTION, 2, 1, D), jnp.float32)
    decay_length = jnp.exp(math.log(lowest) + spread * (math.log(highest) - math.log(lowest)))
    spike_events = jax.random.randint(spike_random_key, (N_SECTION, 2, 1, 1, 3), 1, SEQUENCE_TOKENS)
    delay_index = lax.broadcasted_iota(jnp.int32, (N_SECTION, 2, SEQUENCE_TOKENS, 1, 1), 2)
    check_passed = jnp.sum((delay_index >= spike_events).astype(jnp.float32), axis=4)
    lag_value = delay_index[:, :, :, :, 0].astype(jnp.float32)
    envelope = jnp.exp(-lag_value / decay_length + check_passed * math.log(0.6))
    filtered = noise_field * envelope / jnp.sqrt(jnp.minimum(decay_length, float(SEQUENCE_TOKENS)))
    return filtered.astype(jnp.bfloat16)


def draw_grad_output(key, part):
    key = jax.random.fold_in(key, 23)
    main_key = jax.random.fold_in(key, 0)
    position = lax.broadcasted_iota(jnp.float32, (SEQUENCE_TOKENS, D), 0) / SEQUENCE_TOKENS
    values = jnp.clip(jax.random.normal(main_key, (SEQUENCE_TOKENS, D), jnp.float32), -6.0, 6.0) * jnp.exp(position * math.log(3.0))
    return values.astype(jnp.bfloat16)


def shard_levels(stream_key, extent, pieces, smallest, top_value):
    def one(dim, shards_of):
        draws = jax.random.uniform(jax.random.fold_in(jax.random.fold_in(stream_key, 6), dim), (shards_of,), jnp.float32, smallest / len(pieces), top_value / len(pieces))
        return jnp.repeat(jnp.exp(draws), extent[dim] // shards_of).reshape((-1,) + (1,) * (len(extent) - dim - 1))

    level = one(*pieces[0])
    for cut in pieces[1:]:
        level = level * one(*cut)
    return level


def scatter_about(own_key, extent, scale, bound, cuts=(), held_as=jnp.bfloat16):
    drawn = jax.random.normal(own_key, extent, jnp.float32) * scale
    if len(cuts) > 0:
        drawn = shard_levels(own_key, extent, cuts, -0.22, 0.18) * drawn
    return jnp.clip(drawn, min=-bound, max=bound).astype(held_as)


def setup_inputs(seed: int = 0) -> dict:
    keys = jax.random.split(jax.random.key(seed), 8)
    return {
        "layer_input": scatter_about(keys[0], (N_SECTION, SEQUENCE_TOKENS, D), 1.0, 6.0, ((0, 2), (1, 128))),
        "conv_out": scatter_about(keys[1], (N_SECTION, 2, SEQUENCE_TOKENS, D), 1.0, 6.0, ((0, 2), (2, 128))),
        "filters": draw_filters(jax.random.fold_in(keys[7], 71), 0),
        "skip_gain": scatter_about(keys[3], (N_SECTION, 2, D), 1.0, 4.0, ((0, 2),), jnp.float32),
        "weight_in": scatter_about(keys[4], (N_SECTION, D, 3 * D), D ** -0.5, 0.25, ((0, 2),)),
        "weight_out": scatter_about(keys[5], (N_SECTION, D, D), D ** -0.5, 0.25, ((0, 2),)),
        "grad_output": draw_grad_output(jax.random.fold_in(keys[7], 71), 0),
    }


def spectrum(signal):
    return jnp.fft.rfft(signal, n=2 * SEQUENCE_TOKENS, axis=0)

def signal_of(values):
    return jnp.fft.irfft(values, n=2 * SEQUENCE_TOKENS, axis=0)[:SEQUENCE_TOKENS]

def layer_backward(saved_input, saved_conv, saved_filter, gains, in_matrix, out_matrix, incoming):
    projected = jnp.dot(saved_input, in_matrix, preferred_element_type=jnp.float32).astype(jnp.bfloat16)
    values = projected[:, :D].astype(jnp.float32)
    gate_one = projected[:, D:2 * D].astype(jnp.float32)
    gate_two = projected[:, 2 * D:].astype(jnp.float32)
    conv_one = saved_conv[0].astype(jnp.float32)
    conv_two = saved_conv[1].astype(jnp.float32)
    gated_mix = gate_one * conv_one
    grad_mix_two = lax.dot_general(incoming, out_matrix, (((1,), (1,)), ((), ())), preferred_element_type=jnp.float32)
    grad_gate_two = grad_mix_two * conv_two
    grad_conv_two = grad_mix_two * gate_two
    filter_one = spectrum(saved_filter[0].astype(jnp.float32))
    filter_two = spectrum(saved_filter[1].astype(jnp.float32))
    spec_two = spectrum(grad_conv_two)
    grad_mix_one = signal_of(jnp.conj(filter_two) * spec_two) + gains[1] * grad_conv_two
    grad_filter_two = signal_of(spec_two * jnp.conj(spectrum(gated_mix)))
    sum_two = lax.optimization_barrier(jnp.sum(grad_conv_two * gated_mix, axis=0))
    grad_gate_one = grad_mix_one * conv_one
    grad_conv_one = grad_mix_one * gate_one
    spec_one = spectrum(grad_conv_one)
    grad_values = signal_of(jnp.conj(filter_one) * spec_one) + gains[0] * grad_conv_one
    grad_filter_one = signal_of(spec_one * jnp.conj(spectrum(values)))
    sum_one = lax.optimization_barrier(jnp.sum(grad_conv_one * values, axis=0))
    grad_proj = jnp.concatenate([grad_values, grad_gate_one, grad_gate_two], axis=1).astype(jnp.bfloat16)
    result = incoming.astype(jnp.float32) + lax.dot_general(grad_proj, in_matrix, (((1,), (1,)), ((), ())), preferred_element_type=jnp.float32)
    rescale = 1.0 / math.sqrt(SEQUENCE_TOKENS)
    grad_filters = (jnp.stack([grad_filter_one, grad_filter_two]) * rescale).astype(jnp.bfloat16)
    grad_gains = jnp.stack([sum_one, sum_two]) * rescale
    return (result.astype(jnp.bfloat16), grad_filters, grad_gains)

def reference(layer_input, conv_out, filters, skip_gain, weight_in, weight_out, grad_output):
    late_layer = layer_backward(layer_input[1], conv_out[1], filters[1], skip_gain[1], weight_in[1], weight_out[1], grad_output)
    early_layer = layer_backward(layer_input[0], conv_out[0], filters[0], skip_gain[0], weight_in[0], weight_out[0], late_layer[0])
    grad_input = jnp.stack([early_layer[0], late_layer[0]])
    grad_filter = jnp.stack([early_layer[1], late_layer[1]])
    grad_skip = jnp.stack([early_layer[2], late_layer[2]])
    return (grad_input, grad_filter, grad_skip)
```

```python
import functools
import math

import jax
import jax.numpy as jnp
import ml_dtypes
import numpy as np
from jax import lax
from jax.experimental import pallas as pl
from jax.experimental.pallas import tpu as pltpu
from jax.sharding import PartitionSpec as P

BF = jnp.bfloat16
F32 = jnp.float32
VMEM_LIMIT = 48 * 1024 * 1024


def split_table(table, axis):
    high = table.astype(np.float32).astype(ml_dtypes.bfloat16)
    low = (table - high.astype(np.float64)).astype(np.float32).astype(ml_dtypes.bfloat16)
    return np.concatenate([high, low], axis=axis)


def transform_tables(blocks, width):
    period = 2 * blocks * width
    half = np.arange(blocks) + 0.5
    outer = 2.0 * np.pi * np.outer(half, np.arange(blocks)) / (2 * blocks)
    inner = 2.0 * np.pi * np.outer(np.arange(width), np.arange(width)) / width
    turn = 2.0 * np.pi * np.outer(half, np.arange(width)) / period
    cos_in, sin_in = np.cos(inner), np.sin(inner)
    outer_fwd = split_table(np.concatenate([np.cos(outer), -np.sin(outer)], 0), 1)
    inner_fwd = split_table(np.block([[cos_in, -sin_in], [sin_in, cos_in]]), 0)
    inner_inv = split_table(np.block([[cos_in, sin_in], [-sin_in, cos_in]]), 0)
    outer_inv = split_table(
        np.concatenate([np.cos(outer).T, -np.sin(outer).T], 1) * (2.0 / period), 1
    )
    turns = np.stack([np.cos(turn), np.sin(turn)]).astype(np.float32)
    return outer_fwd, inner_fwd, inner_inv, outer_inv, turns


def mm(left, right):
    return jnp.dot(left, right, preferred_element_type=F32)


def mm_t(left, right):
    return lax.dot_general(left, right, (((1,), (1,)), ((), ())), preferred_element_type=F32)


def to_spectrum(signals, outer, inner, turns):
    count = len(signals)
    size = signals[0].shape[0]
    width = signals[0].shape[1]
    data = jnp.concatenate([signal.astype(BF) for signal in signals], axis=1)
    mixed = mm(outer[...], jnp.concatenate([data, data], axis=0))
    turn_cos, turn_sin = turns[0], turns[1]
    rows = []
    for c in range(count):
        real = mixed[:size, c * width : (c + 1) * width]
        imag = mixed[size:, c * width : (c + 1) * width]
        rows.append(
            jnp.concatenate(
                [real * turn_cos + imag * turn_sin, imag * turn_cos - real * turn_sin], axis=1
            ).astype(BF)
        )
    turned = jnp.concatenate(rows, axis=0)
    return mm(jnp.concatenate([turned, turned], axis=1), inner[...])


def conj_times(left, right):
    width = left.shape[1] // 2
    left_real, left_imag = left[:, :width], left[:, width:]
    right_real, right_imag = right[:, :width], right[:, width:]
    return jnp.concatenate(
        [
            left_real * right_real + left_imag * right_imag,
            left_real * right_imag - left_imag * right_real,
        ],
        axis=1,
    )


def from_spectrum(product, inner, outer, turns):
    width = product.shape[1] // 2
    size = turns.shape[1]
    count = product.shape[0] // size
    data = product.astype(BF)
    mixed = mm(jnp.concatenate([data, data], axis=1), inner[...])
    turn_cos, turn_sin = turns[0], turns[1]
    reals, imags = [], []
    for c in range(count):
        real = mixed[c * size : (c + 1) * size, :width]
        imag = mixed[c * size : (c + 1) * size, width:]
        reals.append((real * turn_cos - imag * turn_sin).astype(BF))
        imags.append((imag * turn_cos + real * turn_sin).astype(BF))
    turned = jnp.concatenate(
        [jnp.concatenate(reals, axis=1), jnp.concatenate(imags, axis=1)], axis=0
    )
    result = mm(outer[...], jnp.concatenate([turned, turned], axis=0))
    return [result[:, c * width : (c + 1) * width] for c in range(count)]


def put_rows(scratch, value, first, stride):
    size = value.shape[0]
    for k in range(value.shape[1] // size):
        block = value[:, k * size : (k + 1) * size].astype(F32).T
        scratch[pl.ds(first + k, size, stride=stride), :] = block


def get_rows(scratch, first, stride, count):
    size = scratch.shape[1]
    return jnp.concatenate(
        [scratch[pl.ds(first + k, size, stride=stride), :].T for k in range(count)], axis=1
    )


def prepare_body(rows, conv, filt, w_in, w_out, inc, packed, gate_two_out, part_two_out, scratch):
    channels = rows.shape[1]
    per = channels // rows.shape[0]
    stride = 6 * per
    projected = mm(rows[...], w_in[...]).astype(BF)
    values = projected[:, :channels]
    gate_one = projected[:, channels : 2 * channels]
    gate_two = projected[:, 2 * channels :]
    mix_two = mm_t(inc[...], w_out[...])
    gate_two_out[...] = gate_two
    part_two_out[...] = (mix_two * conv[1].astype(F32)).astype(BF)
    put_rows(scratch, filt[0], 0, stride)
    put_rows(scratch, filt[1], per, stride)
    put_rows(scratch, values, 2 * per, stride)
    put_rows(scratch, gate_one, 3 * per, stride)
    put_rows(scratch, conv[0], 4 * per, stride)
    put_rows(scratch, mix_two * gate_two.astype(F32), 5 * per, stride)
    packed[...] = scratch[...].astype(BF)


def regrad_body(inc, w_out, gate_two, conv_two, packed, part_two_out, scratch):
    per = inc.shape[1] // inc.shape[0]
    mix_two = mm_t(inc[...], w_out[...])
    part_two_out[...] = (mix_two * conv_two[...].astype(F32)).astype(BF)
    put_rows(scratch, mix_two * gate_two[...].astype(F32), 0, per)
    packed[...] = scratch[...].astype(BF)


def early_body(
    per, gains, data, outer_fwd, inner_fwd, inner_inv, outer_inv, turns, packed, filt_out, known, out
):
    size = data.shape[1]
    known[...] = data[...].astype(F32)

    def signals(s):
        return [known[pl.ds(s * per + k, size, stride=6 * per), :] for k in range(per)]

    grad_two = signals(5)
    filt_two = to_spectrum(signals(1), outer_fwd, inner_fwd, turns)
    filt_out[1] = filt_two
    spec_two = to_spectrum(grad_two, outer_fwd, inner_fwd, turns)
    mixed = from_spectrum(conj_times(filt_two, spec_two), inner_inv, outer_inv, turns)
    mix_one = [mixed[k] + gains[1, k] * grad_two[k] for k in range(per)]
    conv_one, gate_one = signals(4), signals(3)
    for k in range(per):
        out[pl.ds(per + k, size, stride=2 * per), :] = mix_one[k] * conv_one[k]
    grad_one = [mix_one[k] * gate_one[k] for k in range(per)]
    filt_one = to_spectrum(signals(0), outer_fwd, inner_fwd, turns)
    filt_out[0] = filt_one
    spec_one = to_spectrum(grad_one, outer_fwd, inner_fwd, turns)
    mixed = from_spectrum(conj_times(filt_one, spec_one), inner_inv, outer_inv, turns)
    for k in range(per):
        out[pl.ds(k, size, stride=2 * per), :] = mixed[k] + gains[0, k] * grad_one[k]
    packed[...] = out[...].astype(BF)


def known_body(per, data, outer_fwd, inner_fwd, turns, spec_out, known):
    size = data.shape[1]
    known[...] = data[...].astype(F32)

    def signals(s):
        return [known[pl.ds(s * per + k, size, stride=6 * per), :] for k in range(per)]

    spec_out[0] = to_spectrum(signals(2), outer_fwd, inner_fwd, turns)
    gated = [gate * conv for gate, conv in zip(signals(3), signals(4))]
    spec_out[1] = to_spectrum(gated, outer_fwd, inner_fwd, turns)


def late_body(
    per,
    gains,
    data,
    fresh,
    filt,
    spec,
    outer_fwd,
    inner_fwd,
    inner_inv,
    outer_inv,
    turns,
    packed,
    known,
    fresh_known,
    out,
):
    size = data.shape[1]
    rows = out.shape[0] // size
    known[...] = data[...].astype(F32)
    fresh_known[...] = fresh[...].astype(F32)

    def signals(s):
        return [known[pl.ds(s * per + k, size, stride=6 * per), :] for k in range(per)]

    def send(s, values):
        for k in range(per):
            out[pl.ds(s * per + k, size, stride=rows), :] = values[k]

    grad_two = [fresh_known[pl.ds(k, size, stride=per), :] for k in range(per)]
    spec_two = to_spectrum(grad_two, outer_fwd, inner_fwd, turns)
    mixed = from_spectrum(conj_times(filt[1], spec_two), inner_inv, outer_inv, turns)
    send(3, from_spectrum(conj_times(spec[1], spec_two), inner_inv, outer_inv, turns))
    mix_one = [mixed[k] + gains[1, k] * grad_two[k] for k in range(per)]
    conv_one, gate_one = signals(4), signals(3)
    send(1, [mix_one[k] * conv_one[k] for k in range(per)])
    grad_one = [mix_one[k] * gate_one[k] for k in range(per)]
    spec_one = to_spectrum(grad_one, outer_fwd, inner_fwd, turns)
    mixed = from_spectrum(conj_times(filt[0], spec_one), inner_inv, outer_inv, turns)
    send(2, from_spectrum(conj_times(spec[0], spec_one), inner_inv, outer_inv, turns))
    send(0, [mixed[k] + gains[0, k] * grad_one[k] for k in range(per)])
    values = signals(2)
    lane = lax.broadcasted_iota(jnp.int32, (1, size), 1)
    skip_row = jnp.zeros((1, size), F32)
    for k in range(per):
        for w, term in ((0, grad_one[k] * values[k]), (1, grad_two[k] * (gate_one[k] * conv_one[k]))):
            total = jnp.sum(jnp.sum(term, axis=0, keepdims=True), axis=1, keepdims=True)
            high = total.astype(BF).astype(F32)
            skip_row = jnp.where(lane == w * per + k, high, skip_row)
            skip_row = jnp.where(lane == (2 + w) * per + k, total - high, skip_row)
    out[pl.ds(4 * per, size, stride=rows), :] = jnp.broadcast_to(skip_row, (size, size))
    for r in range(4 * per + 1, rows):
        out[pl.ds(r, size, stride=rows), :] = jnp.zeros((size, size), F32)
    packed[...] = out[...].astype(BF)


def input_grad(inc, values, gate_one, part_two, w_in):
    proj = jnp.concatenate([values.astype(BF), gate_one.astype(BF), part_two], axis=1)
    return (inc.astype(F32) + mm_t(proj, w_in)).astype(BF)


def hand_body(per, data, part_two, inc, w_in, result, scratch):
    scratch[...] = data[...].astype(F32)
    values = get_rows(scratch, 0, 2 * per, per)
    gate_one = get_rows(scratch, per, 2 * per, per)
    result[...] = input_grad(inc[...], values, gate_one, part_two[...], w_in[...])


def finish_body(per, rescale, data, part_two, inc, w_in, result, filt_grads, skip_grads, scratch):
    size = data.shape[1]
    stride = data.shape[0] // size
    scratch[...] = data[...].astype(F32)
    values = get_rows(scratch, 0, stride, per)
    gate_one = get_rows(scratch, per, stride, per)
    result[...] = input_grad(inc[...], values, gate_one, part_two[...], w_in[...])
    filt_grads[0] = (get_rows(scratch, 2 * per, stride, per) * rescale).astype(BF)
    filt_grads[1] = (get_rows(scratch, 3 * per, stride, per) * rescale).astype(BF)
    sums = scratch[pl.ds(4 * per, size, stride=stride), :].T
    sums = (sums[: 2 * per] + sums[2 * per : 4 * per]) * rescale
    for w in range(2):
        for k in range(per):
            row = w * per + k
            skip_grads[pl.ds(w, 1), pl.ds(k * size, size)] = sums[row : row + 1]


def call(body, out_shapes, scratch, *operands, smem=0):
    specs = [
        pl.BlockSpec(memory_space=pltpu.SMEM if i < smem else pltpu.VMEM)
        for i in range(len(operands))
    ]
    return pl.pallas_call(
        body,
        out_shape=[jax.ShapeDtypeStruct(shape, dtype) for shape, dtype in out_shapes],
        in_specs=specs,
        out_specs=[pl.BlockSpec(memory_space=pltpu.VMEM) for _ in out_shapes],
        scratch_shapes=[pltpu.VMEM(shape, F32) for shape in scratch],
        compiler_params=pltpu.CompilerParams(vmem_limit_bytes=VMEM_LIMIT),
    )(*operands)


def exchange(rows):
    return lax.all_to_all(rows, "seq", split_axis=0, concat_axis=0, tiled=True)


def on_device(layer_input, conv_out, filters, skip_gain, weight_in, weight_out, grad_output):
    tokens, channels = grad_output.shape
    parts = lax.axis_size("seq")
    per = channels // parts
    w_in, w_out, conv = weight_in[0], weight_out[0], conv_out[0]
    outer_fwd, inner_fwd, inner_inv, outer_inv, turns = transform_tables(parts, tokens)
    is_late = lax.axis_index("section") == 1
    own = lax.dynamic_slice_in_dim(
        skip_gain[0].reshape(2, per, parts), lax.axis_index("seq"), 1, axis=2
    )[:, :, 0]
    token_rows = ((tokens, channels), BF)
    spectra = ((2, per * parts, 2 * tokens), F32)

    packed, gate_two, part_two = call(
        prepare_body,
        [((parts * 6 * per, tokens), BF), token_rows, token_rows],
        [(parts * 6 * per, tokens)],
        layer_input[0], conv, filters[0], w_in, w_out, grad_output,
    )
    data = exchange(packed)
    packed, filt = call(
        functools.partial(early_body, per),
        [((parts * 2 * per, tokens), BF), spectra],
        [(parts * 6 * per, tokens), (parts * 2 * per, tokens)],
        own, data, outer_fwd, inner_fwd, inner_inv, outer_inv, turns,
        smem=1,
    )
    back = exchange(packed)
    (spec,) = call(
        functools.partial(known_body, per),
        [spectra],
        [(parts * 6 * per, tokens)],
        data, outer_fwd, inner_fwd, turns,
    )
    (late,) = call(
        functools.partial(hand_body, per),
        [token_rows],
        [(parts * 2 * per, tokens)],
        back, part_two, grad_output, w_in,
    )
    handed = lax.ppermute(late, "section", [(1, 0)])
    incoming = jnp.where(is_late, grad_output, handed)
    packed, part_two = call(
        regrad_body,
        [((parts * per, tokens), BF), token_rows],
        [(parts * per, tokens)],
        incoming, w_out, gate_two, conv[1],
    )
    fresh = exchange(packed)
    out_rows = 8 * ((4 * per + 1 + 7) // 8)
    (packed,) = call(
        functools.partial(late_body, per),
        [((parts * out_rows, tokens), BF)],
        [(parts * 6 * per, tokens), (parts * per, tokens), (parts * out_rows, tokens)],
        own, data, fresh, filt, spec, outer_fwd, inner_fwd, inner_inv, outer_inv, turns,
        smem=1,
    )
    back = exchange(packed)
    grad_rows, filter_grads, skip_grads = call(
        functools.partial(finish_body, per, 1.0 / math.sqrt(parts * tokens)),
        [token_rows, ((2, tokens, channels), BF), ((2, channels), F32)],
        [(parts * out_rows, tokens)],
        back, part_two, incoming, w_in,
    )
    return (grad_rows[None], filter_grads[None], skip_grads[None])


def solution(mesh):
    in_specs = (
        P("section", "seq", None),
        P("section", None, "seq", None),
        P("section", None, "seq", None),
        P("section", None, None),
        P("section", None, None),
        P("section", None, None),
        P("seq", None),
    )
    out_specs = (
        P("section", "seq", None),
        P("section", None, "seq", None),
        P("section", None, None),
    )
    return jax.shard_map(
        on_device, mesh=mesh, in_specs=in_specs, out_specs=out_specs, check_vma=False
    )
```

```python
import functools
import math

import jax
import jax.numpy as jnp
import ml_dtypes
import numpy as np
from jax import lax
from jax.experimental import pallas as pl
from jax.experimental.pallas import tpu as pltpu
from jax.sharding import PartitionSpec as P

BF = jnp.bfloat16
F32 = jnp.float32
VMEM_LIMIT = 20 * 1024 * 1024


def split_table(table, axis):
    high = table.astype(np.float32).astype(ml_dtypes.bfloat16)
    low = (table - high.astype(np.float64)).astype(np.float32).astype(ml_dtypes.bfloat16)
    return np.concatenate([high, low], axis=axis)


def transform_tables(blocks, width):
    period = 2 * blocks * width
    half = np.arange(blocks) + 0.5
    outer = 2.0 * np.pi * np.outer(half, np.arange(blocks)) / (2 * blocks)
    inner = 2.0 * np.pi * np.outer(np.arange(width), np.arange(width)) / width
    turn = 2.0 * np.pi * np.outer(half, np.arange(width)) / period
    cos_in, sin_in = np.cos(inner), np.sin(inner)
    outer_fwd = split_table(np.concatenate([np.cos(outer), -np.sin(outer)], 0), 1)
    inner_fwd = split_table(np.block([[cos_in, -sin_in], [sin_in, cos_in]]), 0)
    inner_inv = split_table(np.block([[cos_in, sin_in], [-sin_in, cos_in]]), 0)
    outer_inv = split_table(
        np.concatenate([np.cos(outer).T, -np.sin(outer).T], 1) * (2.0 / period), 1
    )
    turns = np.stack([np.cos(turn), np.sin(turn)]).astype(np.float32)
    return outer_fwd, inner_fwd, inner_inv, outer_inv, turns


def mm(left, right):
    return jnp.dot(left, right, preferred_element_type=F32)


def mm_t(left, right):
    return lax.dot_general(left, right, (((1,), (1,)), ((), ())), preferred_element_type=F32)


def to_spectrum(signals, outer, inner, turns):
    count = len(signals)
    size = signals[0].shape[0]
    width = signals[0].shape[1]
    data = jnp.concatenate([signal.astype(BF) for signal in signals], axis=1)
    mixed = mm(outer[...], jnp.concatenate([data, data], axis=0))
    turn_cos, turn_sin = turns[0], turns[1]
    rows = []
    for c in range(count):
        real = mixed[:size, c * width : (c + 1) * width]
        imag = mixed[size:, c * width : (c + 1) * width]
        rows.append(
            jnp.concatenate(
                [real * turn_cos + imag * turn_sin, imag * turn_cos - real * turn_sin], axis=1
            ).astype(BF)
        )
    turned = jnp.concatenate(rows, axis=0)
    return mm(jnp.concatenate([turned, turned], axis=1), inner[...])


def conj_times(left, right):
    width = left.shape[1] // 2
    left_real, left_imag = left[:, :width], left[:, width:]
    right_real, right_imag = right[:, :width], right[:, width:]
    return jnp.concatenate(
        [
            left_real * right_real + left_imag * right_imag,
            left_real * right_imag - left_imag * right_real,
        ],
        axis=1,
    )


def from_spectrum(product, inner, outer, turns):
    width = product.shape[1] // 2
    size = turns.shape[1]
    count = product.shape[0] // size
    data = product.astype(BF)
    mixed = mm(jnp.concatenate([data, data], axis=1), inner[...])
    turn_cos, turn_sin = turns[0], turns[1]
    reals, imags = [], []
    for c in range(count):
        real = mixed[c * size : (c + 1) * size, :width]
        imag = mixed[c * size : (c + 1) * size, width:]
        reals.append((real * turn_cos - imag * turn_sin).astype(BF))
        imags.append((imag * turn_cos + real * turn_sin).astype(BF))
    turned = jnp.concatenate(
        [jnp.concatenate(reals, axis=1), jnp.concatenate(imags, axis=1)], axis=0
    )
    result = mm(outer[...], jnp.concatenate([turned, turned], axis=0))
    return [result[:, c * width : (c + 1) * width] for c in range(count)]


def put_rows(scratch, value, first, stride):
    size = value.shape[0]
    for k in range(value.shape[1] // size):
        block = value[:, k * size : (k + 1) * size].astype(F32).T
        scratch[pl.ds(first + k, size, stride=stride), :] = block


def get_rows(scratch, first, stride, count):
    size = scratch.shape[1]
    return jnp.concatenate(
        [scratch[pl.ds(first + k, size, stride=stride), :].T for k in range(count)], axis=1
    )


def fetch(pairs, sems):
    copies = [
        pltpu.make_async_copy(source, target, sems.at[i])
        for i, (source, target) in enumerate(pairs)
    ]
    for copy in copies:
        copy.start()
    return copies


def prepare_body(
    rows_in,
    conv_in,
    filt_in,
    w_in_in,
    w_out_in,
    inc_in,
    packed_out,
    later_out,
    gate_two_out,
    part_two_out,
    rows,
    conv,
    filt,
    w_in,
    w_out,
    inc,
    first,
    second,
    packed,
    later,
    gate_two_kept,
    part_two_kept,
    sems,
    out_sems,
):
    channels = rows.shape[1]
    per = channels // rows.shape[0]
    got_filt, got_rows, got_w_in, got_inc, got_w_out, got_conv = fetch(
        [
            (filt_in, filt),
            (rows_in, rows),
            (w_in_in, w_in),
            (inc_in, inc),
            (w_out_in, w_out),
            (conv_in, conv),
        ],
        sems,
    )
    got_filt.wait()
    put_rows(first, filt[0], 0, 4 * per)
    put_rows(first, filt[1], per, 4 * per)
    got_rows.wait()
    got_w_in.wait()
    projected = mm(rows[...], w_in[...]).astype(BF)
    gate_one = projected[:, channels : 2 * channels]
    gate_two = projected[:, 2 * channels :]
    put_rows(first, gate_one, 2 * per, 4 * per)
    got_inc.wait()
    got_w_out.wait()
    mix_two = mm_t(inc[...], w_out[...])
    put_rows(first, mix_two * gate_two.astype(F32), 3 * per, 4 * per)
    packed[...] = first[...].astype(BF)
    sends = [pltpu.make_async_copy(packed, packed_out, out_sems.at[0])]
    sends[0].start()
    gate_two_kept[...] = gate_two
    got_conv.wait()
    part_two_kept[...] = (mix_two * conv[1].astype(F32)).astype(BF)
    put_rows(second, projected[:, :channels], 0, 2 * per)
    put_rows(second, gate_one.astype(F32) * conv[0].astype(F32), per, 2 * per)
    later[...] = second[...].astype(BF)
    for i, (source, target) in enumerate(
        [(gate_two_kept, gate_two_out), (part_two_kept, part_two_out), (later, later_out)]
    ):
        send = pltpu.make_async_copy(source, target, out_sems.at[1 + i])
        send.start()
        sends.append(send)
    for send in sends:
        send.wait()


def regrad_body(
    late,
    inc,
    done,
    w_out,
    gate_two_in,
    conv,
    later,
    packed,
    part_two_out,
    kept_out,
    part_two,
    gate_two,
    scratch,
    sems,
):
    per = inc.shape[1] // inc.shape[0]

    @pl.when(late[0] == 0)
    def _():
        gate, keep = fetch([(gate_two_in, gate_two), (inc, kept_out)], sems)
        mix_two = mm_t(inc[...], w_out[...])
        part_two[...] = (mix_two * conv[1].astype(F32)).astype(BF)
        part = pltpu.make_async_copy(part_two, part_two_out, sems.at[2])
        part.start()
        gate.wait()
        put_rows(scratch, mix_two * gate_two[...].astype(F32), 0, 2 * per)
        for k in range(per):
            empty = jnp.zeros((inc.shape[0], inc.shape[0]), F32)
            scratch[pl.ds(per + k, inc.shape[0], stride=2 * per), :] = empty
        packed[...] = scratch[...].astype(BF)
        keep.wait()
        part.wait()

    @pl.when(late[0] == 1)
    def _():
        part_two[...] = jnp.zeros_like(part_two)
        copies = fetch([(done, kept_out), (part_two, part_two_out), (later, packed)], sems)
        for copy in copies:
            copy.wait()


def signals(scratch, s, per):
    size = scratch.shape[1]
    stride = scratch.shape[0] // size
    return [scratch[pl.ds(s * per + k, size, stride=stride), :] for k in range(per)]


def send_rows(scratch, s, values):
    size = scratch.shape[1]
    stride = scratch.shape[0] // size
    for k, value in enumerate(values):
        scratch[pl.ds(s * len(values) + k, size, stride=stride), :] = value


def early_body(
    per,
    late,
    gains,
    data,
    later,
    outer_fwd,
    inner_fwd,
    inner_inv,
    outer_inv,
    turns,
    packed,
    spec_out,
    grad_out,
    known,
    out,
    spec,
    grad,
    sems,
):
    size = data.shape[1]

    @pl.when(late[0] == 1)
    def _():
        known[...] = data[...].astype(F32)
        filt_two = to_spectrum(signals(known, 1, per), outer_fwd, inner_fwd, turns)
        grad_two = signals(known, 3, per)
        spec_two = to_spectrum(grad_two, outer_fwd, inner_fwd, turns)
        spec[1] = spec_two
        mixed = from_spectrum(conj_times(filt_two, spec_two), inner_inv, outer_inv, turns)
        mix_one = [mixed[k] + gains[1, k] * grad_two[k] for k in range(per)]
        send_rows(out, 1, mix_one)
        gate_one = signals(known, 2, per)
        grad_one = [mix_one[k] * gate_one[k] for k in range(per)]
        for k in range(per):
            grad[pl.ds(k * size, size), :] = grad_one[k]
        filt_one = to_spectrum(signals(known, 0, per), outer_fwd, inner_fwd, turns)
        spec_one = to_spectrum(grad_one, outer_fwd, inner_fwd, turns)
        spec[0] = spec_one
        copies = fetch([(spec, spec_out), (grad, grad_out)], sems)
        mixed = from_spectrum(conj_times(filt_one, spec_one), inner_inv, outer_inv, turns)
        send_rows(out, 0, [mixed[k] + gains[0, k] * grad_one[k] for k in range(per)])
        packed[...] = out[...].astype(BF)
        for copy in copies:
            copy.wait()

    @pl.when(late[0] == 0)
    def _():
        known[...] = data[...].astype(F32)
        grad[...] = jnp.zeros_like(grad)
        spec[0] = to_spectrum(signals(known, 0, per), outer_fwd, inner_fwd, turns)
        spec[1] = to_spectrum(signals(known, 1, per), outer_fwd, inner_fwd, turns)
        copies = fetch([(spec, spec_out), (grad, grad_out), (later, packed)], sems)
        for copy in copies:
            copy.wait()


def known_body(per, data, outer_fwd, inner_fwd, turns, spec_out, known):
    known[...] = data[...].astype(F32)
    spec_out[0] = to_spectrum(signals(known, 0, per), outer_fwd, inner_fwd, turns)
    spec_out[1] = to_spectrum(signals(known, 1, per), outer_fwd, inner_fwd, turns)


def skip_rows(per, grads, others, out):
    size = out.shape[1]
    rows = out.shape[0] // size
    lane = lax.broadcasted_iota(jnp.int32, (1, size), 1)
    skip_row = jnp.zeros((1, size), F32)
    for w in range(2):
        for k in range(per):
            term = grads[w][k] * others[w][k]
            total = jnp.sum(jnp.sum(term, axis=0, keepdims=True), axis=1, keepdims=True)
            high = total.astype(BF).astype(F32)
            skip_row = jnp.where(lane == w * per + k, high, skip_row)
            skip_row = jnp.where(lane == (2 + w) * per + k, total - high, skip_row)
    out[pl.ds(4 * per, size, stride=rows), :] = jnp.broadcast_to(skip_row, (size, size))
    for r in range(4 * per + 1, rows):
        out[pl.ds(r, size, stride=rows), :] = jnp.zeros((size, size), F32)


def late_body(
    per,
    late,
    gains,
    first,
    second,
    third,
    held_in,
    grad_in,
    spec,
    outer_fwd_in,
    inner_fwd_in,
    inner_inv_in,
    outer_inv_in,
    turns_in,
    packed,
    known,
    other,
    fresh,
    out,
    held,
    grad_held,
    outer_fwd,
    inner_fwd,
    inner_inv,
    outer_inv,
    turns,
    sems,
):
    size = first.shape[1]
    copies = fetch(
        [
            (outer_fwd_in, outer_fwd),
            (turns_in, turns),
            (inner_fwd_in, inner_fwd),
            (held_in, held),
            (inner_inv_in, inner_inv),
            (outer_inv_in, outer_inv),
            (grad_in, grad_held),
        ],
        sems,
    )
    fresh[...] = third[...].astype(F32)
    known[...] = first[...].astype(F32)
    for copy in copies:
        copy.wait()

    @pl.when(late[0] == 0)
    def _():
        other[...] = second[...].astype(F32)
        grad_two = signals(fresh, 0, per)
        spec_two = to_spectrum(grad_two, outer_fwd, inner_fwd, turns)
        mixed = from_spectrum(conj_times(held[1], spec_two), inner_inv, outer_inv, turns)
        send_rows(out, 3, from_spectrum(conj_times(spec[1], spec_two), inner_inv, outer_inv, turns))
        mix_one = [mixed[k] + gains[1, k] * grad_two[k] for k in range(per)]
        send_rows(out, 1, mix_one)
        gate_one = signals(known, 2, per)
        grad_one = [mix_one[k] * gate_one[k] for k in range(per)]
        spec_one = to_spectrum(grad_one, outer_fwd, inner_fwd, turns)
        mixed = from_spectrum(conj_times(held[0], spec_one), inner_inv, outer_inv, turns)
        send_rows(out, 2, from_spectrum(conj_times(spec[0], spec_one), inner_inv, outer_inv, turns))
        send_rows(out, 0, [mixed[k] + gains[0, k] * grad_one[k] for k in range(per)])
        skip_rows(
            per, (grad_one, grad_two), (signals(other, 0, per), signals(other, 1, per)), out
        )
        packed[...] = out[...].astype(BF)

    @pl.when(late[0] == 1)
    def _():
        values, gated = signals(fresh, 0, per), signals(fresh, 1, per)
        spec_one = to_spectrum(values, outer_fwd, inner_fwd, turns)
        spec_two = to_spectrum(gated, outer_fwd, inner_fwd, turns)
        send_rows(out, 2, from_spectrum(conj_times(spec_one, held[0]), inner_inv, outer_inv, turns))
        send_rows(out, 3, from_spectrum(conj_times(spec_two, held[1]), inner_inv, outer_inv, turns))
        empty = [jnp.zeros((size, size), F32)] * per
        send_rows(out, 0, empty)
        send_rows(out, 1, empty)
        grad_one = [grad_held[pl.ds(k * size, size), :] for k in range(per)]
        skip_rows(per, (grad_one, signals(known, 3, per)), (values, gated), out)
        packed[...] = out[...].astype(BF)


def input_grad(inc, values, mix_one, conv_one, part_two, w_in):
    gate_one = mix_one * conv_one.astype(F32)
    proj = jnp.concatenate([values.astype(BF), gate_one.astype(BF), part_two], axis=1)
    return (inc.astype(F32) + mm_t(proj, w_in)).astype(BF)


def hand_body(
    per, late, data, conv, part_two_in, inc_in, w_in, result, scratch, part_two, inc, sems
):
    @pl.when(late[0] == 1)
    def _():
        copies = fetch([(part_two_in, part_two), (inc_in, inc)], sems)
        scratch[...] = data[...].astype(F32)
        values = get_rows(scratch, 0, 2 * per, per)
        mix_one = get_rows(scratch, per, 2 * per, per)
        for copy in copies:
            copy.wait()
        result[...] = input_grad(inc[...], values, mix_one, conv[0], part_two[...], w_in[...])

    @pl.when(late[0] == 0)
    def _():
        result[...] = jnp.zeros_like(result)


def finish_body(
    per,
    rescale,
    late,
    data,
    conv,
    part_two,
    inc,
    w_in,
    result,
    filt_grads,
    skip_grads,
    scratch,
):
    size = data.shape[1]
    stride = data.shape[0] // size
    scratch[...] = data[...].astype(F32)

    @pl.when(late[0] == 0)
    def _():
        values = get_rows(scratch, 0, stride, per)
        mix_one = get_rows(scratch, per, stride, per)
        result[...] = input_grad(inc[...], values, mix_one, conv[0], part_two[...], w_in[...])

    @pl.when(late[0] == 1)
    def _():
        result[...] = inc[...]

    filt_grads[0] = (get_rows(scratch, 2 * per, stride, per) * rescale).astype(BF)
    filt_grads[1] = (get_rows(scratch, 3 * per, stride, per) * rescale).astype(BF)
    sums = scratch[pl.ds(4 * per, size, stride=stride), :].T
    sums = (sums[: 2 * per] + sums[2 * per : 4 * per]) * rescale
    for w in range(2):
        for k in range(per):
            row = w * per + k
            skip_grads[pl.ds(w, 1), pl.ds(k * size, size)] = sums[row : row + 1]


def call(body, out_shapes, scratch, *operands, smem=0, direct=(), direct_out=(), limit=VMEM_LIMIT):
    def space(i):
        if i < smem:
            return pltpu.SMEM
        return pltpu.HBM if i in direct else pltpu.VMEM

    return pl.pallas_call(
        body,
        out_shape=[
            (pltpu.HBM if i in direct_out else jax.ShapeDtypeStruct)(shape, dtype)
            for i, (shape, dtype) in enumerate(out_shapes)
        ],
        in_specs=[pl.BlockSpec(memory_space=space(i)) for i in range(len(operands))],
        out_specs=[
            pl.BlockSpec(memory_space=pltpu.HBM if i in direct_out else pltpu.VMEM)
            for i in range(len(out_shapes))
        ],
        scratch_shapes=[
            pltpu.VMEM(shape, F32) if isinstance(shape, tuple) else shape for shape in scratch
        ],
        compiler_params=pltpu.CompilerParams(vmem_limit_bytes=limit),
    )(
        *[
            pltpu.with_memory_space_constraint(x, pltpu.HBM) if i in direct else x
            for i, x in enumerate(operands)
        ]
    )


def exchange(rows, parts):
    per_part = rows.shape[0] // parts
    tile = math.gcd(per_part, 8)
    cut = rows.reshape(parts, per_part // tile, tile, rows.shape[1])
    return lax.all_to_all(cut, "seq", split_axis=0, concat_axis=0, tiled=True).reshape(rows.shape)


def on_device(layer_input, conv_out, filters, skip_gain, weight_in, weight_out, grad_output):
    tokens, channels = grad_output.shape
    parts = lax.axis_size("seq")
    per = channels // parts
    w_in, w_out, conv = weight_in[0], weight_out[0], conv_out[0]
    outer_fwd, inner_fwd, inner_inv, outer_inv, turns = transform_tables(parts, tokens)
    late = lax.axis_index("section").astype(jnp.int32).reshape(1)
    own = lax.dynamic_slice_in_dim(
        skip_gain[0].reshape(2, per, parts), lax.axis_index("seq"), 1, axis=2
    )[:, :, 0]

    def rows(count):
        return (parts * count, tokens)

    token_rows = ((tokens, channels), BF)
    spectra = ((2, per * parts, 2 * tokens), F32)

    packed, later, gate_two, part_two = call(
        prepare_body,
        [(rows(4 * per), BF), (rows(2 * per), BF), token_rows, token_rows],
        [
            pltpu.VMEM((tokens, channels), BF),
            pltpu.VMEM((2, tokens, channels), BF),
            pltpu.VMEM((2, tokens, channels), BF),
            pltpu.VMEM(w_in.shape, BF),
            pltpu.VMEM(w_out.shape, BF),
            pltpu.VMEM((tokens, channels), BF),
            rows(4 * per),
            rows(2 * per),
            pltpu.VMEM(rows(4 * per), BF),
            pltpu.VMEM(rows(2 * per), BF),
            pltpu.VMEM((tokens, channels), BF),
            pltpu.VMEM((tokens, channels), BF),
            pltpu.SemaphoreType.DMA((6,)),
            pltpu.SemaphoreType.DMA((4,)),
        ],
        layer_input[0], conv, filters[0], w_in, w_out, grad_output,
        direct=range(6), direct_out=range(4),
    )
    first = exchange(packed, parts)
    packed, held, grad_held = call(
        functools.partial(early_body, per),
        [(rows(2 * per), BF), spectra, (rows(per), F32)],
        [
            rows(4 * per), rows(2 * per), spectra[0], rows(per), pltpu.SemaphoreType.DMA((3,)),
        ],
        late, own, first, later, outer_fwd, inner_fwd, inner_inv, outer_inv, turns,
        smem=2, direct=(3,), direct_out=(1, 2),
    )
    second = exchange(packed, parts)
    (done,) = call(
        functools.partial(hand_body, per),
        [token_rows],
        [
            rows(2 * per), pltpu.VMEM((tokens, channels), BF), pltpu.VMEM((tokens, channels), BF),
            pltpu.SemaphoreType.DMA((2,)),
        ],
        late, second, conv, part_two, grad_output, w_in,
        smem=1, direct=(3, 4),
    )
    handed = lax.ppermute(done, "section", [(1, 0)])
    packed, part_two, kept = call(
        regrad_body,
        [(rows(2 * per), BF), token_rows, token_rows],
        [
            pltpu.VMEM((tokens, channels), BF), pltpu.VMEM((tokens, channels), BF), rows(2 * per),
            pltpu.SemaphoreType.DMA((3,)),
        ],
        late, handed, done, w_out, gate_two, conv, later,
        smem=1, direct=(4, 6), direct_out=(1, 2),
    )
    third = exchange(packed, parts)
    (spec,) = call(
        functools.partial(known_body, per),
        [spectra],
        [rows(2 * per)],
        second, outer_fwd, inner_fwd, turns,
    )
    out_rows = 4 * per + 2
    (packed,) = call(
        functools.partial(late_body, per),
        [(rows(out_rows), BF)],
        [
            rows(4 * per), rows(2 * per), rows(2 * per), rows(out_rows), spectra[0], rows(per),
            pltpu.VMEM(outer_fwd.shape, BF), pltpu.VMEM(inner_fwd.shape, BF),
            pltpu.VMEM(inner_inv.shape, BF), pltpu.VMEM(outer_inv.shape, BF),
            turns.shape, pltpu.SemaphoreType.DMA((7,)),
        ],
        late, own, first, second, third, held, grad_held, spec,
        outer_fwd, inner_fwd, inner_inv, outer_inv, turns,
        smem=2, direct=(5, 6, 8, 9, 10, 11, 12),
    )
    back = exchange(packed, parts)
    grad_rows, filter_grads, skip_grads = call(
        functools.partial(finish_body, per, 1.0 / math.sqrt(parts * tokens)),
        [token_rows, ((2, tokens, channels), BF), ((2, channels), F32)],
        [rows(out_rows)],
        late, back, conv, part_two, kept, w_in,
        smem=1,
    )
    return (grad_rows[None], filter_grads[None], skip_grads[None])


def solution(mesh):
    in_specs = (
        P("section", "seq", None),
        P("section", None, "seq", None),
        P("section", None, "seq", None),
        P("section", None, None),
        P("section", None, None),
        P("section", None, None),
        P("seq", None),
    )
    out_specs = (
        P("section", "seq", None),
        P("section", None, "seq", None),
        P("section", None, None),
    )
    return jax.shard_map(
        on_device, mesh=mesh, in_specs=in_specs, out_specs=out_specs, check_vma=False
    )
```

```python
import functools
import math

import jax
import jax.numpy as jnp
import ml_dtypes
import numpy as np
from jax import lax
from jax.experimental import pallas as pl
from jax.experimental.pallas import tpu as pltpu
from jax.sharding import PartitionSpec as P

BF = jnp.bfloat16
F32 = jnp.float32
VMEM_LIMIT = 20 * 1024 * 1024


def split_table(table, axis):
    high = table.astype(np.float32).astype(ml_dtypes.bfloat16)
    low = (table - high.astype(np.float64)).astype(np.float32).astype(ml_dtypes.bfloat16)
    return np.concatenate([high, low], axis=axis)


def transform_tables(blocks, width):
    period = 2 * blocks * width
    half = np.arange(blocks) + 0.5
    outer = 2.0 * np.pi * np.outer(half, np.arange(blocks)) / (2 * blocks)
    inner = 2.0 * np.pi * np.outer(np.arange(width), np.arange(width)) / width
    turn = 2.0 * np.pi * np.outer(half, np.arange(width)) / period
    cos_in, sin_in = np.cos(inner), np.sin(inner)
    outer_fwd = split_table(np.concatenate([np.cos(outer), -np.sin(outer)], 0), 1)
    inner_fwd = split_table(np.block([[cos_in, -sin_in], [sin_in, cos_in]]), 0)
    inner_inv = split_table(np.block([[cos_in, sin_in], [-sin_in, cos_in]]), 0)
    outer_inv = split_table(
        np.concatenate([np.cos(outer).T, -np.sin(outer).T], 1) * (2.0 / period), 1
    )
    turns = np.stack([np.cos(turn), np.sin(turn)]).astype(np.float32)
    return outer_fwd, inner_fwd, inner_inv, outer_inv, turns


def mm(left, right):
    return jnp.dot(left, right, preferred_element_type=F32)


def mm_t(left, right):
    return lax.dot_general(left, right, (((1,), (1,)), ((), ())), preferred_element_type=F32)


def to_spectrum(signals, outer, inner, turns):
    count = len(signals)
    size = signals[0].shape[0]
    width = signals[0].shape[1]
    data = jnp.concatenate([signal.astype(BF) for signal in signals], axis=1)
    mixed = mm(outer[...], jnp.concatenate([data, data], axis=0))
    turn_cos, turn_sin = turns[0], turns[1]
    rows = []
    for c in range(count):
        real = mixed[:size, c * width : (c + 1) * width]
        imag = mixed[size:, c * width : (c + 1) * width]
        rows.append(
            jnp.concatenate(
                [real * turn_cos + imag * turn_sin, imag * turn_cos - real * turn_sin], axis=1
            ).astype(BF)
        )
    turned = jnp.concatenate(rows, axis=0)
    return mm(jnp.concatenate([turned, turned], axis=1), inner[...])


def conj_times(left, right):
    width = left.shape[1] // 2
    left_real, left_imag = left[:, :width], left[:, width:]
    right_real, right_imag = right[:, :width], right[:, width:]
    return jnp.concatenate(
        [
            left_real * right_real + left_imag * right_imag,
            left_real * right_imag - left_imag * right_real,
        ],
        axis=1,
    )


def from_spectrum(product, inner, outer, turns):
    width = product.shape[1] // 2
    size = turns.shape[1]
    count = product.shape[0] // size
    data = product.astype(BF)
    mixed = mm(jnp.concatenate([data, data], axis=1), inner[...])
    turn_cos, turn_sin = turns[0], turns[1]
    reals, imags = [], []
    for c in range(count):
        real = mixed[c * size : (c + 1) * size, :width]
        imag = mixed[c * size : (c + 1) * size, width:]
        reals.append((real * turn_cos - imag * turn_sin).astype(BF))
        imags.append((imag * turn_cos + real * turn_sin).astype(BF))
    turned = jnp.concatenate(
        [jnp.concatenate(reals, axis=1), jnp.concatenate(imags, axis=1)], axis=0
    )
    result = mm(outer[...], jnp.concatenate([turned, turned], axis=0))
    return [result[:, c * width : (c + 1) * width] for c in range(count)]


def put_rows(scratch, value, first, stride):
    size = value.shape[0]
    for k in range(value.shape[1] // size):
        block = value[:, k * size : (k + 1) * size].astype(F32).T
        scratch[pl.ds(first + k, size, stride=stride), :] = block


def get_rows(scratch, first, stride, count):
    size = scratch.shape[1]
    return jnp.concatenate(
        [scratch[pl.ds(first + k, size, stride=stride), :].T for k in range(count)], axis=1
    )


def fetch(pairs, sems):
    copies = [
        pltpu.make_async_copy(source, target, sems.at[i])
        for i, (source, target) in enumerate(pairs)
    ]
    for copy in copies:
        copy.start()
    return copies


def half_of(ref, side):
    width = ref.shape[1] // 2
    return ref[:, side * width : (side + 1) * width]


def prepare_body(
    late,
    rows_in,
    conv_in,
    filt_in,
    w_in_in,
    w_out_in,
    inc_in,
    own_out,
    other_out,
    later_own_out,
    later_other_out,
    keep_out,
    send_out,
    rows,
    conv,
    filt,
    w_in,
    w_out,
    inc,
    first,
    second,
    packs,
    laters,
    pairs,
    sems,
    out_sems,
):
    mine = late[0]
    channels = rows.shape[1]
    per = channels // rows.shape[0] // 2
    got_filt, got_rows, got_w_in, got_inc, got_w_out, got_conv = fetch(
        [
            (filt_in, filt),
            (rows_in, rows),
            (w_in_in, w_in),
            (inc_in, inc),
            (w_out_in, w_out),
            (conv_in, conv),
        ],
        sems,
    )
    got_filt.wait()
    for side in range(2):
        put_rows(first.at[side], half_of(filt[0], side), 0, 4 * per)
        put_rows(first.at[side], half_of(filt[1], side), per, 4 * per)
    got_rows.wait()
    got_w_in.wait()
    projected = mm(rows[...], w_in[...]).astype(BF)
    values = projected[:, :channels]
    gate_one = projected[:, channels : 2 * channels]
    gate_two = projected[:, 2 * channels :]
    got_inc.wait()
    got_w_out.wait()
    mix_two = mm_t(inc[...], w_out[...])
    grad_two = mix_two * gate_two.astype(F32)
    for side in range(2):
        put_rows(first.at[side], half_of(gate_one, side), 2 * per, 4 * per)
        put_rows(first.at[side], half_of(grad_two, side), 3 * per, 4 * per)
        packs[side] = first[side].astype(BF)
    sends = fetch([(packs.at[1 - mine], other_out), (packs.at[mine], own_out)], out_sems)
    got_conv.wait()
    gated = gate_one.astype(F32) * conv[0].astype(F32)
    for side in range(2):
        put_rows(second.at[side], half_of(values, side), 0, 2 * per)
        put_rows(second.at[side], half_of(gated, side), per, 2 * per)
        laters[side] = second[side].astype(BF)

    @pl.when(mine == 1)
    def _():
        part_two = (mix_two * conv[1].astype(F32)).astype(BF)
        for side in range(2):
            pairs[side, 0] = half_of(part_two, side)
            pairs[side, 1] = half_of(conv[0], side)

    @pl.when(mine == 0)
    def _():
        for side in range(2):
            pairs[side, 0] = half_of(gate_two, side)
            pairs[side, 1] = half_of(conv[1], side)

    for i, (source, target) in enumerate(
        [
            (laters.at[1 - mine], later_other_out),
            (laters.at[mine], later_own_out),
            (pairs.at[1 - mine], send_out),
            (pairs.at[mine], keep_out),
        ]
    ):
        send = pltpu.make_async_copy(source, target, out_sems.at[2 + i])
        send.start()
        sends.append(send)
    for send in sends:
        send.wait()


def signals(scratch, s, per):
    size = scratch.shape[1]
    stride = scratch.shape[0] // size
    return [scratch[pl.ds(s * per + k, size, stride=stride), :] for k in range(per)]


def send_rows(scratch, s, values):
    size = scratch.shape[1]
    stride = scratch.shape[0] // size
    for k, value in enumerate(values):
        scratch[pl.ds(s * len(values) + k, size, stride=stride), :] = value


def early_body(
    per,
    late,
    gains,
    data,
    later_own,
    later_got,
    outer_fwd,
    inner_fwd,
    inner_inv,
    outer_inv,
    turns,
    packed,
    spec_out,
    grad_out,
    known,
    out,
    spec,
    grad,
    later,
    later_rows,
    sems,
):
    size = data.shape[1]
    mine = late[0]
    laters = fetch([(later_own, later.at[mine]), (later_got, later.at[1 - mine])], sems)
    known[...] = data[...].astype(F32)
    filt_two = to_spectrum(signals(known, 1, per), outer_fwd, inner_fwd, turns)
    grad_two = signals(known, 3, per)
    spec_two = to_spectrum(grad_two, outer_fwd, inner_fwd, turns)
    spec[1] = spec_two
    mixed = from_spectrum(conj_times(filt_two, spec_two), inner_inv, outer_inv, turns)
    mix_one = [mixed[k] + gains[1, k] * grad_two[k] for k in range(per)]
    send_rows(out, 1, mix_one)
    gate_one = signals(known, 2, per)
    grad_one = [mix_one[k] * gate_one[k] for k in range(per)]
    for k in range(per):
        grad[pl.ds(k * size, size), :] = grad_one[k]
    filt_one = to_spectrum(signals(known, 0, per), outer_fwd, inner_fwd, turns)
    spec_one = to_spectrum(grad_one, outer_fwd, inner_fwd, turns)
    spec[0] = spec_one
    copies = [
        pltpu.make_async_copy(spec, spec_out, sems.at[2]),
        pltpu.make_async_copy(grad, grad_out, sems.at[3]),
    ]
    for copy in copies:
        copy.start()
    for copy in laters:
        copy.wait()
    for layer in range(2):
        later_rows[...] = later[layer].astype(F32)
        for s in range(2):
            send_rows(out, 4 - 2 * layer + s, signals(later_rows, s, per))
    mixed = from_spectrum(conj_times(filt_one, spec_one), inner_inv, outer_inv, turns)
    send_rows(out, 0, [mixed[k] + gains[0, k] * grad_one[k] for k in range(per)])
    packed[...] = out[...].astype(BF)
    for copy in copies:
        copy.wait()


def skip_row(per, base, grads, others):
    size = grads[0][0].shape[1]
    lane = lax.broadcasted_iota(jnp.int32, (1, size), 1)
    row = jnp.zeros((1, size), F32)
    for w in range(2):
        for k in range(per):
            term = grads[w][k] * others[w][k]
            total = jnp.sum(jnp.sum(term, axis=0, keepdims=True), axis=1, keepdims=True)
            high = total.astype(BF).astype(F32)
            row = jnp.where(lane == base + w * per + k, high, row)
            row = jnp.where(lane == base + (2 + w) * per + k, total - high, row)
    return row


def known_body(
    per,
    first,
    second,
    held,
    grad_held,
    outer_fwd,
    inner_fwd,
    inner_inv,
    outer_inv,
    turns,
    spec_out,
    filt_out,
    skip_out,
    known,
    other,
):
    size = second.shape[1]
    known[...] = first[...].astype(F32)
    other[...] = second[...].astype(F32)
    for s in range(2):
        spec_out[s] = to_spectrum(signals(other, 4 + s, per), outer_fwd, inner_fwd, turns)
    values, gated = signals(other, 2, per), signals(other, 3, per)
    for s, signal in enumerate((values, gated)):
        spec = to_spectrum(signal, outer_fwd, inner_fwd, turns)
        grads = from_spectrum(conj_times(spec, held[s]), inner_inv, outer_inv, turns)
        for k in range(per):
            filt_out[pl.ds((s * per + k) * size, size), :] = grads[k]
    grad_one = [grad_held[pl.ds(k * size, size), :] for k in range(per)]
    row = skip_row(per, 4 * per, (grad_one, signals(known, 3, per)), (values, gated))
    skip_out[...] = jnp.broadcast_to(row, skip_out.shape)


def late_body(
    per,
    gains,
    second,
    third,
    spec,
    filt_held,
    skip_held,
    outer_fwd_in,
    inner_fwd_in,
    inner_inv_in,
    outer_inv_in,
    turns_in,
    packed,
    known,
    other,
    out,
    outer_fwd,
    inner_fwd,
    inner_inv,
    outer_inv,
    turns,
    sems,
):
    size = third.shape[1]
    got_outer, got_turns, got_inner, got_inner_inv, got_outer_inv = fetch(
        [
            (outer_fwd_in, outer_fwd),
            (turns_in, turns),
            (inner_fwd_in, inner_fwd),
            (inner_inv_in, inner_inv),
            (outer_inv_in, outer_inv),
        ],
        sems,
    )
    known[...] = third[...].astype(F32)
    other[...] = second[...].astype(F32)
    for s in range(2):
        send_rows(
            out, 4 + s, [filt_held[pl.ds((s * per + k) * size, size), :] for k in range(per)]
        )
    rows = out.shape[0] // size
    out[pl.ds(6 * per + 1, size, stride=rows), :] = jnp.zeros((size, size), F32)
    got_outer.wait()
    got_turns.wait()
    got_inner.wait()
    grad_two = signals(known, 3, per)
    spec_two = to_spectrum(grad_two, outer_fwd, inner_fwd, turns)
    filt_two = to_spectrum(signals(known, 1, per), outer_fwd, inner_fwd, turns)
    got_inner_inv.wait()
    got_outer_inv.wait()
    mixed = from_spectrum(conj_times(filt_two, spec_two), inner_inv, outer_inv, turns)
    filt_one = to_spectrum(signals(known, 0, per), outer_fwd, inner_fwd, turns)
    send_rows(out, 3, from_spectrum(conj_times(spec[1], spec_two), inner_inv, outer_inv, turns))
    mix_one = [mixed[k] + gains[1, k] * grad_two[k] for k in range(per)]
    send_rows(out, 1, mix_one)
    gate_one = signals(known, 2, per)
    grad_one = [mix_one[k] * gate_one[k] for k in range(per)]
    row = skip_row(
        per, 0, (grad_one, grad_two), (signals(other, 4, per), signals(other, 5, per))
    )
    row = row + skip_held[pl.ds(0, 1), :]
    out[pl.ds(6 * per, size, stride=rows), :] = jnp.broadcast_to(row, (size, size))
    spec_one = to_spectrum(grad_one, outer_fwd, inner_fwd, turns)
    mixed = from_spectrum(conj_times(filt_one, spec_one), inner_inv, outer_inv, turns)
    send_rows(out, 2, from_spectrum(conj_times(spec[0], spec_one), inner_inv, outer_inv, turns))
    send_rows(out, 0, [mixed[k] + gains[0, k] * grad_one[k] for k in range(per)])
    packed[...] = out[...].astype(BF)


def hand_body(
    per,
    late,
    data,
    pair_keep,
    pair_got,
    w_own,
    w_got,
    partial,
    scratch,
    pair,
    w_in,
    sems,
):
    mine = late[0]
    half = pair.shape[2]

    def copies(side):
        pairs, weights = (pair_keep, w_own) if side == 1 else (pair_got, w_got)
        moves = [(pairs, pair)]
        for b in range(3):
            columns = pl.ds((2 * b + side) * half, half)
            moves.append((weights.at[:, columns], w_in.at[:, pl.ds(b * half, half)]))
        return [pltpu.make_async_copy(a, b, sems.at[i]) for i, (a, b) in enumerate(moves)]

    for side in range(2):

        @pl.when(mine == side)
        def _():
            for copy in copies(side):
                copy.start()

    scratch[...] = data[...].astype(F32)
    values = get_rows(scratch, 0, 6 * per, per).astype(BF)
    mix_one = get_rows(scratch, per, 6 * per, per)
    for side in range(2):

        @pl.when(mine == side)
        def _():
            for copy in copies(side):
                copy.wait()

    gate_one = (mix_one * pair[1].astype(F32)).astype(BF)
    partial[...] = mm_t(jnp.concatenate([values, gate_one, pair[0]], axis=1), w_in[...])


def regrad_body(
    per,
    late,
    inc,
    part_own,
    part_got,
    pair_keep,
    pair_got,
    w_own,
    w_got,
    pack_own,
    pack_got,
    packed,
    kept_out,
    part_two_out,
    scratch,
    pair,
    w_out,
    pack,
    kept,
    part_two,
    sems,
    out_sems,
):
    mine = late[0]
    half = pair.shape[2]

    def copies(side):
        if side == 0:
            moves = [(w_own, w_out), (pair_keep, pair), (pack_own, pack)]
        else:
            moves = [(w_got, w_out), (pair_got, pair), (pack_got, pack)]
        moves[0] = (moves[0][0].at[pl.ds(side * half, half), :], w_out)
        return [pltpu.make_async_copy(a, b, sems.at[i]) for i, (a, b) in enumerate(moves)]

    for side in range(2):

        @pl.when(mine == side)
        def _():
            for copy in copies(side):
                copy.start()

    result = (inc[...].astype(F32) + (part_own[...] + part_got[...])).astype(BF)
    kept[...] = result
    keep = pltpu.make_async_copy(kept, kept_out, out_sems.at[0])
    keep.start()
    for side in range(2):

        @pl.when(mine == side)
        def _():
            for copy in copies(side):
                copy.wait()

    mix_two = mm_t(result, w_out[...])
    part_two[...] = (mix_two * pair[1].astype(F32)).astype(BF)
    part = pltpu.make_async_copy(part_two, part_two_out, out_sems.at[1])
    part.start()
    scratch[...] = pack[...].astype(F32)
    put_rows(scratch, mix_two * pair[0].astype(F32), 3 * per, 4 * per)
    packed[...] = scratch[...].astype(BF)
    keep.wait()
    part.wait()


def finish_body(
    per,
    rescale,
    late,
    own,
    got,
    conv,
    part_own,
    part_got,
    inc,
    w_in,
    result,
    filt_grads,
    skip_grads,
    sides,
):
    mine = late[0]
    size = own.shape[1]
    half = per * size
    stride = own.shape[0] // size
    sides[mine] = own[...].astype(F32)
    sides[1 - mine] = got[...].astype(F32)

    def both(s):
        return jnp.concatenate(
            [get_rows(sides.at[side], s * per, stride, per) for side in range(2)], axis=1
        )

    def filter_and_skip(layer):
        filt_grads[0] = (both(2 + 2 * layer) * rescale).astype(BF)
        filt_grads[1] = (both(3 + 2 * layer) * rescale).astype(BF)
        for side in range(2):
            sums = sides[side, pl.ds(6 * per, size, stride=stride), :].T
            base = 4 * layer * per
            sums = (sums[base : base + 2 * per] + sums[base + 2 * per : base + 4 * per]) * rescale
            for w in range(2):
                for k in range(per):
                    row = w * per + k
                    skip_grads[pl.ds(w, 1), pl.ds(side * half + k * size, size)] = sums[
                        row : row + 1
                    ]

    @pl.when(mine == 0)
    def _():
        gate_one = both(1) * conv[0].astype(F32)
        proj = jnp.concatenate(
            [both(0).astype(BF), gate_one.astype(BF), part_own[...], part_got[...]], axis=1
        )
        result[...] = (inc[...].astype(F32) + mm_t(proj, w_in[...])).astype(BF)
        filter_and_skip(0)

    @pl.when(mine == 1)
    def _():
        result[...] = inc[...]
        filter_and_skip(1)


def call(body, out_shapes, scratch, *operands, smem=0, direct=(), direct_out=(), limit=VMEM_LIMIT):
    def space(i):
        if i < smem:
            return pltpu.SMEM
        return pltpu.HBM if i in direct else pltpu.VMEM

    return pl.pallas_call(
        body,
        out_shape=[
            (pltpu.HBM if i in direct_out else jax.ShapeDtypeStruct)(shape, dtype)
            for i, (shape, dtype) in enumerate(out_shapes)
        ],
        in_specs=[pl.BlockSpec(memory_space=space(i)) for i in range(len(operands))],
        out_specs=[
            pl.BlockSpec(memory_space=pltpu.HBM if i in direct_out else pltpu.VMEM)
            for i in range(len(out_shapes))
        ],
        scratch_shapes=[
            pltpu.VMEM(shape, F32) if isinstance(shape, tuple) else shape for shape in scratch
        ],
        compiler_params=pltpu.CompilerParams(vmem_limit_bytes=limit),
    )(
        *[
            pltpu.with_memory_space_constraint(x, pltpu.HBM) if i in direct else x
            for i, x in enumerate(operands)
        ]
    )


def exchange(rows, parts):
    per_part = rows.shape[0] // parts
    tile = math.gcd(per_part, 8)
    cut = rows.reshape(parts, per_part // tile, tile, rows.shape[1])
    return lax.all_to_all(cut, "seq", split_axis=0, concat_axis=0, tiled=True).reshape(rows.shape)


def on_device(layer_input, conv_out, filters, skip_gain, weight_in, weight_out, grad_output):
    tokens, channels = grad_output.shape
    parts = lax.axis_size("seq")
    per = channels // parts // 2
    half = channels // 2
    w_in, w_out, conv = weight_in[0], weight_out[0], conv_out[0]
    tables = transform_tables(parts, tokens)
    outer_fwd, inner_fwd, inner_inv, outer_inv, turns = tables
    section = lax.axis_index("section").astype(jnp.int32)
    late = section.reshape(1)

    def rows(count):
        return (parts * count, tokens)

    def vmem(*shape):
        return pltpu.VMEM(shape, BF)

    def sems(count):
        return pltpu.SemaphoreType.DMA((count,))

    def swap(value, pairs=((0, 1), (1, 0))):
        return lax.ppermute(value, "section", pairs)

    spectra = (2, per * parts, 2 * tokens)
    pair = ((2, tokens, half), BF)

    pack_own, pack_other, later_own, later_other, pair_keep, pair_send = call(
        prepare_body,
        [(rows(4 * per), BF)] * 2 + [(rows(2 * per), BF)] * 2 + [pair] * 2,
        [
            vmem(tokens, channels),
            vmem(2, tokens, channels),
            vmem(2, tokens, channels),
            vmem(*w_in.shape),
            vmem(*w_out.shape),
            vmem(tokens, channels),
            (2, *rows(4 * per)),
            (2, *rows(2 * per)),
            vmem(2, *rows(4 * per)),
            vmem(2, *rows(2 * per)),
            vmem(2, *pair[0]),
            sems(6),
            sems(6),
        ],
        late, layer_input[0], conv, filters[0], w_in, w_out, grad_output,
        smem=1, direct=range(1, 7), direct_out=range(6),
    )
    pack_got = swap(pack_other)
    packed = jnp.where(section == 1, pack_own, pack_got)
    first = exchange(packed, parts)

    later_got = swap(later_other)
    gains_got = swap(skip_gain[0])
    pair_got = swap(pair_send)
    w_in_got = swap(w_in, ((1, 0),))
    w_out_got = swap(w_out, ((0, 1),))

    def own_channels(gains):
        return lax.dynamic_slice(
            gains.reshape(2, 2 * per, parts), (0, section * per, lax.axis_index("seq")), (2, per, 1)
        )[:, :, 0]

    gains_early = own_channels(jnp.where(section == 1, skip_gain[0], gains_got))
    gains_late = own_channels(jnp.where(section == 1, gains_got, skip_gain[0]))

    packed, held, grad_held = call(
        functools.partial(early_body, per),
        [(rows(6 * per), BF), (spectra, F32), (rows(per), F32)],
        [
            rows(4 * per), rows(6 * per), spectra, rows(per), vmem(2, *rows(2 * per)),
            rows(2 * per), sems(4),
        ],
        late, gains_early, first, later_own, later_got, *tables,
        smem=2, direct=(3, 4), direct_out=(1, 2),
    )
    second = exchange(packed, parts)
    (partial,) = call(
        functools.partial(hand_body, per),
        [((tokens, channels), F32)],
        [rows(6 * per), vmem(2, tokens, half), vmem(channels, 3 * half), sems(4)],
        late, second, pair_keep, pair_got, w_in, w_in_got,
        smem=1, direct=(2, 3, 4, 5),
    )
    partial_got = swap(partial)
    packed, kept, part_two = call(
        functools.partial(regrad_body, per),
        [(rows(4 * per), BF), ((tokens, channels), BF), ((tokens, half), BF)],
        [
            rows(4 * per), vmem(2, tokens, half), vmem(half, channels), vmem(*rows(4 * per)),
            vmem(tokens, channels), vmem(tokens, half), sems(3), sems(2),
        ],
        late, grad_output, partial, partial_got, pair_keep, pair_got, w_out, w_out_got,
        pack_own, pack_got,
        smem=1, direct=range(4, 10), direct_out=(1, 2),
    )
    third = exchange(packed, parts)
    part_two_got = swap(part_two)
    spec, filt_held, skip_held = call(
        functools.partial(known_body, per),
        [(spectra, F32), (rows(2 * per), F32), ((8, tokens), F32)],
        [rows(4 * per), rows(6 * per)],
        first, second, held, grad_held, *tables,
    )
    out_rows = 6 * per + 2
    (packed,) = call(
        functools.partial(late_body, per),
        [(rows(out_rows), BF)],
        [
            rows(4 * per), rows(6 * per), rows(out_rows),
            vmem(*outer_fwd.shape), vmem(*inner_fwd.shape), vmem(*inner_inv.shape),
            vmem(*outer_inv.shape), turns.shape, sems(5),
        ],
        gains_late, second, third, spec, filt_held, skip_held, *tables,
        smem=1, direct=range(6, 11),
    )
    back = exchange(packed, parts)
    back_got = swap(back)
    grad_rows, filter_grads, skip_grads = call(
        functools.partial(finish_body, per, 1.0 / math.sqrt(parts * tokens)),
        [((tokens, channels), BF), ((2, tokens, channels), BF), ((2, channels), F32)],
        [(2, *rows(out_rows))],
        late, back, back_got, conv, part_two, part_two_got, kept, w_in,
        smem=1,
    )
    return (grad_rows[None], filter_grads[None], skip_grads[None])


def solution(mesh):
    in_specs = (
        P("section", "seq", None),
        P("section", None, "seq", None),
        P("section", None, "seq", None),
        P("section", None, None),
        P("section", None, None),
        P("section", None, None),
        P("seq", None),
    )
    out_specs = (
        P("section", "seq", None),
        P("section", None, "seq", None),
        P("section", None, None),
    )
    return jax.shard_map(
        on_device, mesh=mesh, in_specs=in_specs, out_specs=out_specs, check_vma=False
    )
```

```python
import functools
import math

import jax
import jax.numpy as jnp
import ml_dtypes
import numpy as np
from jax import lax
from jax.experimental import pallas as pl
from jax.experimental.pallas import tpu as pltpu
from jax.sharding import PartitionSpec as P

BF = jnp.bfloat16
F32 = jnp.float32
VMEM_LIMIT = 20 * 1024 * 1024


def split_table(table, axis):
    high = table.astype(np.float32).astype(ml_dtypes.bfloat16)
    low = (table - high.astype(np.float64)).astype(np.float32).astype(ml_dtypes.bfloat16)
    return np.concatenate([high, low], axis=axis)


def transform_tables(blocks, width):
    period = 2 * blocks * width
    half = np.arange(blocks) + 0.5
    outer = 2.0 * np.pi * np.outer(half, np.arange(blocks)) / (2 * blocks)
    inner = 2.0 * np.pi * np.outer(np.arange(width), np.arange(width)) / width
    turn = 2.0 * np.pi * np.outer(half, np.arange(width)) / period
    cos_in, sin_in = np.cos(inner), np.sin(inner)
    outer_fwd = split_table(np.concatenate([np.cos(outer), -np.sin(outer)], 0), 1)
    inner_fwd = split_table(np.block([[cos_in, -sin_in], [sin_in, cos_in]]), 0)
    inner_inv = split_table(np.block([[cos_in, sin_in], [-sin_in, cos_in]]), 0)
    outer_inv = split_table(
        np.concatenate([np.cos(outer).T, -np.sin(outer).T], 1) * (2.0 / period), 1
    )
    turns = np.stack([np.cos(turn), np.sin(turn)]).astype(np.float32)
    return outer_fwd, inner_fwd, inner_inv, outer_inv, turns


def mm(left, right):
    return jnp.dot(left, right, preferred_element_type=F32)


def mm_t(left, right):
    return lax.dot_general(left, right, (((1,), (1,)), ((), ())), preferred_element_type=F32)


def to_spectrum(signals, outer, inner, turns):
    count = len(signals)
    size = signals[0].shape[0]
    width = signals[0].shape[1]
    data = jnp.concatenate([signal.astype(BF) for signal in signals], axis=1)
    mixed = mm(outer[...], jnp.concatenate([data, data], axis=0))
    turn_cos, turn_sin = turns[0], turns[1]
    rows = []
    for c in range(count):
        real = mixed[:size, c * width : (c + 1) * width]
        imag = mixed[size:, c * width : (c + 1) * width]
        rows.append(
            jnp.concatenate(
                [real * turn_cos + imag * turn_sin, imag * turn_cos - real * turn_sin], axis=1
            ).astype(BF)
        )
    turned = jnp.concatenate(rows, axis=0)
    return mm(jnp.concatenate([turned, turned], axis=1), inner[...])


def conj_times(left, right):
    width = left.shape[1] // 2
    left_real, left_imag = left[:, :width], left[:, width:]
    right_real, right_imag = right[:, :width], right[:, width:]
    return jnp.concatenate(
        [
            left_real * right_real + left_imag * right_imag,
            left_real * right_imag - left_imag * right_real,
        ],
        axis=1,
    )


def from_spectrum(product, inner, outer, turns):
    width = product.shape[1] // 2
    size = turns.shape[1]
    count = product.shape[0] // size
    data = product.astype(BF)
    mixed = mm(jnp.concatenate([data, data], axis=1), inner[...])
    turn_cos, turn_sin = turns[0], turns[1]
    reals, imags = [], []
    for c in range(count):
        real = mixed[c * size : (c + 1) * size, :width]
        imag = mixed[c * size : (c + 1) * size, width:]
        reals.append((real * turn_cos - imag * turn_sin).astype(BF))
        imags.append((imag * turn_cos + real * turn_sin).astype(BF))
    turned = jnp.concatenate(
        [jnp.concatenate(reals, axis=1), jnp.concatenate(imags, axis=1)], axis=0
    )
    result = mm(outer[...], jnp.concatenate([turned, turned], axis=0))
    return [result[:, c * width : (c + 1) * width] for c in range(count)]


def put_rows(scratch, value, first, stride):
    size = value.shape[0]
    for k in range(value.shape[1] // size):
        block = value[:, k * size : (k + 1) * size].astype(F32).T
        scratch[pl.ds(first + k, size, stride=stride), :] = block


def get_rows(scratch, first, stride, count):
    size = scratch.shape[1]
    return jnp.concatenate(
        [scratch[pl.ds(first + k, size, stride=stride), :].T for k in range(count)], axis=1
    )


def fetch(pairs, sems):
    copies = [
        pltpu.make_async_copy(source, target, sems.at[i])
        for i, (source, target) in enumerate(pairs)
    ]
    for copy in copies:
        copy.start()
    return copies


def prepare_body(
    rows_in,
    conv_in,
    filt_in,
    w_in_in,
    w_out_in,
    inc_in,
    packed_out,
    later_out,
    gate_two_out,
    part_two_out,
    rows,
    conv,
    filt,
    w_in,
    w_out,
    inc,
    first,
    second,
    later,
    gate_two_kept,
    part_two_kept,
    sems,
    out_sems,
):
    channels = rows.shape[1]
    per = channels // rows.shape[0]
    got_filt, got_rows, got_w_in, got_inc, got_w_out, got_conv = fetch(
        [
            (filt_in, filt),
            (rows_in, rows),
            (w_in_in, w_in),
            (inc_in, inc),
            (w_out_in, w_out),
            (conv_in, conv),
        ],
        sems,
    )
    got_filt.wait()
    put_rows(first, filt[0], 0, 4 * per)
    put_rows(first, filt[1], per, 4 * per)
    got_rows.wait()
    got_w_in.wait()
    projected = mm(rows[...], w_in[...]).astype(BF)
    gate_one = projected[:, channels : 2 * channels]
    gate_two = projected[:, 2 * channels :]
    put_rows(first, gate_one, 2 * per, 4 * per)
    got_inc.wait()
    got_w_out.wait()
    mix_two = mm_t(inc[...], w_out[...])
    put_rows(first, mix_two * gate_two.astype(F32), 3 * per, 4 * per)
    packed_out[...] = first[...].astype(BF)
    sends = []
    gate_two_kept[...] = gate_two
    got_conv.wait()
    part_two_kept[...] = (mix_two * conv[1].astype(F32)).astype(BF)
    put_rows(second, projected[:, :channels], 0, 2 * per)
    put_rows(second, gate_one.astype(F32) * conv[0].astype(F32), per, 2 * per)
    later[...] = second[...].astype(BF)
    for i, (source, target) in enumerate(
        [(gate_two_kept, gate_two_out), (part_two_kept, part_two_out), (later, later_out)]
    ):
        send = pltpu.make_async_copy(source, target, out_sems.at[i])
        send.start()
        sends.append(send)
    for send in sends:
        send.wait()


def regrad_body(
    late,
    inc,
    done,
    w_out,
    gate_two_in,
    conv,
    later,
    packed,
    part_two_out,
    kept_out,
    part_two,
    gate_two,
    scratch,
    sems,
):
    per = inc.shape[1] // inc.shape[0]

    @pl.when(late[0] == 0)
    def _():
        gate, keep = fetch([(gate_two_in, gate_two), (inc, kept_out)], sems)
        mix_two = mm_t(inc[...], w_out[...])
        part_two[...] = (mix_two * conv[1].astype(F32)).astype(BF)
        part = pltpu.make_async_copy(part_two, part_two_out, sems.at[2])
        part.start()
        gate.wait()
        put_rows(scratch, mix_two * gate_two[...].astype(F32), 0, 2 * per)
        for k in range(per):
            empty = jnp.zeros((inc.shape[0], inc.shape[0]), F32)
            scratch[pl.ds(per + k, inc.shape[0], stride=2 * per), :] = empty
        packed[...] = scratch[...].astype(BF)
        keep.wait()
        part.wait()

    @pl.when(late[0] == 1)
    def _():
        part_two[...] = jnp.zeros_like(part_two)
        copies = fetch([(done, kept_out), (part_two, part_two_out), (later, packed)], sems)
        for copy in copies:
            copy.wait()


def signals(scratch, s, per):
    size = scratch.shape[1]
    stride = scratch.shape[0] // size
    return [scratch[pl.ds(s * per + k, size, stride=stride), :] for k in range(per)]


def send_rows(scratch, s, values):
    size = scratch.shape[1]
    stride = scratch.shape[0] // size
    for k, value in enumerate(values):
        scratch[pl.ds(s * len(values) + k, size, stride=stride), :] = value


def early_body(
    per,
    late,
    gains,
    data,
    later,
    outer_fwd,
    inner_fwd,
    inner_inv,
    outer_inv,
    turns,
    packed,
    spec_out,
    grad_out,
    known,
    out,
    spec,
    grad,
    sems,
):
    size = data.shape[1]

    @pl.when(late[0] == 1)
    def _():
        known[...] = data[...].astype(F32)
        filt_two = to_spectrum(signals(known, 1, per), outer_fwd, inner_fwd, turns)
        grad_two = signals(known, 3, per)
        spec_two = to_spectrum(grad_two, outer_fwd, inner_fwd, turns)
        spec[1] = spec_two
        mixed = from_spectrum(conj_times(filt_two, spec_two), inner_inv, outer_inv, turns)
        mix_one = [mixed[k] + gains[1, k] * grad_two[k] for k in range(per)]
        send_rows(out, 1, mix_one)
        gate_one = signals(known, 2, per)
        grad_one = [mix_one[k] * gate_one[k] for k in range(per)]
        for k in range(per):
            grad[pl.ds(k * size, size), :] = grad_one[k]
        filt_one = to_spectrum(signals(known, 0, per), outer_fwd, inner_fwd, turns)
        spec_one = to_spectrum(grad_one, outer_fwd, inner_fwd, turns)
        spec[0] = spec_one
        copies = fetch([(spec, spec_out), (grad, grad_out)], sems)
        mixed = from_spectrum(conj_times(filt_one, spec_one), inner_inv, outer_inv, turns)
        send_rows(out, 0, [mixed[k] + gains[0, k] * grad_one[k] for k in range(per)])
        packed[...] = out[...].astype(BF)
        for copy in copies:
            copy.wait()

    @pl.when(late[0] == 0)
    def _():
        known[...] = data[...].astype(F32)
        grad[...] = jnp.zeros_like(grad)
        spec[0] = to_spectrum(signals(known, 0, per), outer_fwd, inner_fwd, turns)
        spec[1] = to_spectrum(signals(known, 1, per), outer_fwd, inner_fwd, turns)
        copies = fetch([(spec, spec_out), (grad, grad_out), (later, packed)], sems)
        for copy in copies:
            copy.wait()


def skip_rows(per, grads, others, out):
    size = out.shape[1]
    rows = out.shape[0] // size
    lane = lax.broadcasted_iota(jnp.int32, (1, size), 1)
    skip_row = jnp.zeros((1, size), F32)
    for w in range(2):
        for k in range(per):
            term = grads[w][k] * others[w][k]
            total = jnp.sum(jnp.sum(term, axis=0, keepdims=True), axis=1, keepdims=True)
            high = total.astype(BF).astype(F32)
            skip_row = jnp.where(lane == w * per + k, high, skip_row)
            skip_row = jnp.where(lane == (2 + w) * per + k, total - high, skip_row)
    out[pl.ds(4 * per, size, stride=rows), :] = jnp.broadcast_to(skip_row, (size, size))
    for r in range(4 * per + 1, rows):
        out[pl.ds(r, size, stride=rows), :] = jnp.zeros((size, size), F32)


def late_body(
    per,
    late,
    gains,
    first,
    second,
    third,
    held_in,
    grad_in,
    spec_in,
    outer_fwd,
    inner_fwd,
    inner_inv,
    outer_inv,
    turns,
    packed,
    known,
    other,
    fresh,
    out,
    held,
    grad_held,
    spec,
    sems,
):
    size = first.shape[1]
    copies = fetch([(held_in, held), (spec_in, spec), (grad_in, grad_held)], sems)
    fresh[...] = third[...].astype(F32)
    known[...] = first[...].astype(F32)

    @pl.when(late[0] == 0)
    def _():
        grad_two = signals(fresh, 0, per)
        spec_two = to_spectrum(grad_two, outer_fwd, inner_fwd, turns)
        for copy in copies:
            copy.wait()
        mixed = from_spectrum(conj_times(held[1], spec_two), inner_inv, outer_inv, turns)
        send_rows(out, 3, from_spectrum(conj_times(spec[1], spec_two), inner_inv, outer_inv, turns))
        mix_one = [mixed[k] + gains[1, k] * grad_two[k] for k in range(per)]
        send_rows(out, 1, mix_one)
        gate_one = signals(known, 2, per)
        grad_one = [mix_one[k] * gate_one[k] for k in range(per)]
        spec_one = to_spectrum(grad_one, outer_fwd, inner_fwd, turns)
        mixed = from_spectrum(conj_times(held[0], spec_one), inner_inv, outer_inv, turns)
        send_rows(out, 2, from_spectrum(conj_times(spec[0], spec_one), inner_inv, outer_inv, turns))
        send_rows(out, 0, [mixed[k] + gains[0, k] * grad_one[k] for k in range(per)])
        other[...] = second[...].astype(F32)
        skip_rows(
            per, (grad_one, grad_two), (signals(other, 0, per), signals(other, 1, per)), out
        )
        packed[...] = out[...].astype(BF)

    @pl.when(late[0] == 1)
    def _():
        values, gated = signals(fresh, 0, per), signals(fresh, 1, per)
        spec_one = to_spectrum(values, outer_fwd, inner_fwd, turns)
        spec_two = to_spectrum(gated, outer_fwd, inner_fwd, turns)
        for copy in copies:
            copy.wait()
        send_rows(out, 2, from_spectrum(conj_times(spec_one, held[0]), inner_inv, outer_inv, turns))
        send_rows(out, 3, from_spectrum(conj_times(spec_two, held[1]), inner_inv, outer_inv, turns))
        empty = [jnp.zeros((size, size), F32)] * per
        send_rows(out, 0, empty)
        send_rows(out, 1, empty)
        grad_one = [grad_held[pl.ds(k * size, size), :] for k in range(per)]
        skip_rows(per, (grad_one, signals(known, 3, per)), (values, gated), out)
        packed[...] = out[...].astype(BF)


def input_grad(inc, values, mix_one, conv_one, part_two, w_in):
    gate_one = mix_one * conv_one.astype(F32)
    proj = jnp.concatenate([values.astype(BF), gate_one.astype(BF), part_two], axis=1)
    return (inc.astype(F32) + mm_t(proj, w_in)).astype(BF)


def hand_body(
    per,
    late,
    data,
    conv,
    part_two_in,
    inc_in,
    w_in,
    outer_fwd,
    inner_fwd,
    turns,
    result,
    spec_out,
    scratch,
    part_two,
    inc,
    spec,
    sems,
):
    @pl.when(late[0] == 1)
    def _():
        copies = fetch([(part_two_in, part_two), (inc_in, inc)], sems)
        scratch[...] = data[...].astype(F32)
        values = get_rows(scratch, 0, 2 * per, per)
        mix_one = get_rows(scratch, per, 2 * per, per)
        for copy in copies:
            copy.wait()
        result[...] = input_grad(inc[...], values, mix_one, conv[0], part_two[...], w_in[...])

    @pl.when(late[0] == 0)
    def _():
        scratch[...] = data[...].astype(F32)
        copies = []
        for s in range(2):
            spec[s] = to_spectrum(signals(scratch, s, per), outer_fwd, inner_fwd, turns)
            copies.append(pltpu.make_async_copy(spec.at[s], spec_out.at[s], sems.at[s]))
            copies[s].start()
        result[...] = jnp.zeros_like(result)
        for copy in copies:
            copy.wait()


def finish_body(
    per,
    rescale,
    late,
    data,
    conv,
    part_two,
    inc,
    w_in,
    result,
    filt_grads,
    skip_grads,
    scratch,
):
    size = data.shape[1]
    stride = data.shape[0] // size
    scratch[...] = data[...].astype(F32)

    @pl.when(late[0] == 0)
    def _():
        values = get_rows(scratch, 0, stride, per)
        mix_one = get_rows(scratch, per, stride, per)
        result[...] = input_grad(inc[...], values, mix_one, conv[0], part_two[...], w_in[...])

    @pl.when(late[0] == 1)
    def _():
        result[...] = inc[...]

    filt_grads[0] = (get_rows(scratch, 2 * per, stride, per) * rescale).astype(BF)
    filt_grads[1] = (get_rows(scratch, 3 * per, stride, per) * rescale).astype(BF)
    sums = scratch[pl.ds(4 * per, size, stride=stride), :].T
    sums = (sums[: 2 * per] + sums[2 * per : 4 * per]) * rescale
    for w in range(2):
        for k in range(per):
            row = w * per + k
            skip_grads[pl.ds(w, 1), pl.ds(k * size, size)] = sums[row : row + 1]


def call(body, out_shapes, scratch, *operands, smem=0, direct=(), direct_out=(), limit=VMEM_LIMIT):
    def space(i):
        if i < smem:
            return pltpu.SMEM
        return pltpu.HBM if i in direct else pltpu.VMEM

    return pl.pallas_call(
        body,
        out_shape=[
            (pltpu.HBM if i in direct_out else jax.ShapeDtypeStruct)(shape, dtype)
            for i, (shape, dtype) in enumerate(out_shapes)
        ],
        in_specs=[pl.BlockSpec(memory_space=space(i)) for i in range(len(operands))],
        out_specs=[
            pl.BlockSpec(memory_space=pltpu.HBM if i in direct_out else pltpu.VMEM)
            for i in range(len(out_shapes))
        ],
        scratch_shapes=[
            pltpu.VMEM(shape, F32) if isinstance(shape, tuple) else shape for shape in scratch
        ],
        compiler_params=pltpu.CompilerParams(vmem_limit_bytes=limit),
    )(
        *[
            pltpu.with_memory_space_constraint(x, pltpu.HBM) if i in direct else x
            for i, x in enumerate(operands)
        ]
    )


def exchange(rows, parts):
    per_part = rows.shape[0] // parts
    tile = math.gcd(per_part, 8)
    cut = rows.reshape(parts, per_part // tile, tile, rows.shape[1])
    return lax.all_to_all(cut, "seq", split_axis=0, concat_axis=0, tiled=True).reshape(rows.shape)


def on_device(layer_input, conv_out, filters, skip_gain, weight_in, weight_out, grad_output):
    tokens, channels = grad_output.shape
    parts = lax.axis_size("seq")
    per = channels // parts
    w_in, w_out, conv = weight_in[0], weight_out[0], conv_out[0]
    outer_fwd, inner_fwd, inner_inv, outer_inv, turns = transform_tables(parts, tokens)
    late = lax.axis_index("section").astype(jnp.int32).reshape(1)
    own = lax.dynamic_slice_in_dim(
        skip_gain[0].reshape(2, per, parts), lax.axis_index("seq"), 1, axis=2
    )[:, :, 0]

    def rows(count):
        return (parts * count, tokens)

    token_rows = ((tokens, channels), BF)
    spectra = ((2, per * parts, 2 * tokens), F32)

    packed, later, gate_two, part_two = call(
        prepare_body,
        [(rows(4 * per), BF), (rows(2 * per), BF), token_rows, token_rows],
        [
            pltpu.VMEM((tokens, channels), BF),
            pltpu.VMEM((2, tokens, channels), BF),
            pltpu.VMEM((2, tokens, channels), BF),
            pltpu.VMEM(w_in.shape, BF),
            pltpu.VMEM(w_out.shape, BF),
            pltpu.VMEM((tokens, channels), BF),
            rows(4 * per),
            rows(2 * per),
            pltpu.VMEM(rows(2 * per), BF),
            pltpu.VMEM((tokens, channels), BF),
            pltpu.VMEM((tokens, channels), BF),
            pltpu.SemaphoreType.DMA((6,)),
            pltpu.SemaphoreType.DMA((3,)),
        ],
        layer_input[0], conv, filters[0], w_in, w_out, grad_output,
        direct=range(6), direct_out=range(1, 4),
    )
    packed, own, late = lax.optimization_barrier((packed, own, late))
    first = exchange(packed, parts)
    packed, held, grad_held = call(
        functools.partial(early_body, per),
        [(rows(2 * per), BF), spectra, (rows(per), F32)],
        [
            rows(4 * per), rows(2 * per), spectra[0], rows(per), pltpu.SemaphoreType.DMA((3,)),
        ],
        late, own, first, later, outer_fwd, inner_fwd, inner_inv, outer_inv, turns,
        smem=2, direct=(3,), direct_out=(1, 2),
    )
    second = exchange(packed, parts)
    done, spec = call(
        functools.partial(hand_body, per),
        [token_rows, spectra],
        [
            rows(2 * per), pltpu.VMEM((tokens, channels), BF), pltpu.VMEM((tokens, channels), BF),
            spectra[0], pltpu.SemaphoreType.DMA((2,)),
        ],
        late, second, conv, part_two, grad_output, w_in, outer_fwd, inner_fwd, turns,
        smem=1, direct=(3, 4), direct_out=(1,),
    )
    handed = lax.ppermute(done, "section", [(1, 0)])
    packed, part_two, kept = call(
        regrad_body,
        [(rows(2 * per), BF), token_rows, token_rows],
        [
            pltpu.VMEM((tokens, channels), BF), pltpu.VMEM((tokens, channels), BF), rows(2 * per),
            pltpu.SemaphoreType.DMA((3,)),
        ],
        late, handed, done, w_out, gate_two, conv, later,
        smem=1, direct=(4, 6), direct_out=(1, 2),
    )
    third = exchange(packed, parts)
    out_rows = 4 * per + 2
    (packed,) = call(
        functools.partial(late_body, per),
        [(rows(out_rows), BF)],
        [
            rows(4 * per), rows(2 * per), rows(2 * per), rows(out_rows), spectra[0], rows(per),
            spectra[0],
pltpu.SemaphoreType.DMA((3,)),
        ],
        late, own, first, second, third, held, grad_held, spec,
        outer_fwd, inner_fwd, inner_inv, outer_inv, turns,
        smem=2, direct=range(5, 8),
    )
    back = exchange(packed, parts)
    grad_rows, filter_grads, skip_grads = call(
        functools.partial(finish_body, per, 1.0 / math.sqrt(parts * tokens)),
        [token_rows, ((2, tokens, channels), BF), ((2, channels), F32)],
        [rows(out_rows)],
        late, back, conv, part_two, kept, w_in,
        smem=1,
    )
    return (grad_rows[None], filter_grads[None], skip_grads[None])


def solution(mesh):
    in_specs = (
        P("section", "seq", None),
        P("section", None, "seq", None),
        P("section", None, "seq", None),
        P("section", None, None),
        P("section", None, None),
        P("section", None, None),
        P("seq", None),
    )
    out_specs = (
        P("section", "seq", None),
        P("section", None, "seq", None),
        P("section", None, None),
    )
    return jax.shard_map(
        on_device, mesh=mesh, in_specs=in_specs, out_specs=out_specs, check_vma=False
    )
```

```python
import functools
import math

import jax
import jax.numpy as jnp
import ml_dtypes
import numpy as np
from jax import lax
from jax.experimental import pallas as pl
from jax.experimental.pallas import tpu as pltpu
from jax.sharding import PartitionSpec as P

BF = jnp.bfloat16
F32 = jnp.float32
VMEM_LIMIT = 20 * 1024 * 1024


def split_table(table, axis):
    high = table.astype(np.float32).astype(ml_dtypes.bfloat16)
    low = (table - high.astype(np.float64)).astype(np.float32).astype(ml_dtypes.bfloat16)
    return np.concatenate([high, low], axis=axis)


def transform_tables(blocks, width):
    period = 2 * blocks * width
    half = np.arange(blocks) + 0.5
    outer = 2.0 * np.pi * np.outer(half, np.arange(blocks)) / (2 * blocks)
    inner = 2.0 * np.pi * np.outer(np.arange(width), np.arange(width)) / width
    turn = 2.0 * np.pi * np.outer(half, np.arange(width)) / period
    cos_in, sin_in = np.cos(inner), np.sin(inner)
    outer_fwd = split_table(np.concatenate([np.cos(outer), -np.sin(outer)], 0), 1)
    inner_fwd = split_table(np.block([[cos_in, -sin_in], [sin_in, cos_in]]), 0)
    inner_inv = split_table(np.block([[cos_in, sin_in], [-sin_in, cos_in]]), 0)
    outer_inv = split_table(
        np.concatenate([np.cos(outer).T, -np.sin(outer).T], 1) * (2.0 / period), 1
    )
    turns = np.stack([np.cos(turn), np.sin(turn)]).astype(np.float32)
    return outer_fwd, inner_fwd, inner_inv, outer_inv, turns


def mm(left, right):
    return jnp.dot(left, right, preferred_element_type=F32)


def mm_t(left, right):
    return lax.dot_general(left, right, (((1,), (1,)), ((), ())), preferred_element_type=F32)


def to_spectrum(signals, outer, inner, turns):
    count = len(signals)
    size = signals[0].shape[0]
    width = signals[0].shape[1]
    data = jnp.concatenate([signal.astype(BF) for signal in signals], axis=1)
    mixed = mm(outer[...], jnp.concatenate([data, data], axis=0))
    turn_cos, turn_sin = turns[0], turns[1]
    rows = []
    for c in range(count):
        real = mixed[:size, c * width : (c + 1) * width]
        imag = mixed[size:, c * width : (c + 1) * width]
        rows.append(
            jnp.concatenate(
                [real * turn_cos + imag * turn_sin, imag * turn_cos - real * turn_sin], axis=1
            ).astype(BF)
        )
    turned = jnp.concatenate(rows, axis=0)
    return mm(jnp.concatenate([turned, turned], axis=1), inner[...])


def conj_times(left, right):
    width = left.shape[1] // 2
    left_real, left_imag = left[:, :width], left[:, width:]
    right_real, right_imag = right[:, :width], right[:, width:]
    return jnp.concatenate(
        [
            left_real * right_real + left_imag * right_imag,
            left_real * right_imag - left_imag * right_real,
        ],
        axis=1,
    )


def from_spectrum(product, inner, outer, turns):
    width = product.shape[1] // 2
    size = turns.shape[1]
    count = product.shape[0] // size
    data = product.astype(BF)
    mixed = mm(jnp.concatenate([data, data], axis=1), inner[...])
    turn_cos, turn_sin = turns[0], turns[1]
    reals, imags = [], []
    for c in range(count):
        real = mixed[c * size : (c + 1) * size, :width]
        imag = mixed[c * size : (c + 1) * size, width:]
        reals.append((real * turn_cos - imag * turn_sin).astype(BF))
        imags.append((imag * turn_cos + real * turn_sin).astype(BF))
    turned = jnp.concatenate(
        [jnp.concatenate(reals, axis=1), jnp.concatenate(imags, axis=1)], axis=0
    )
    result = mm(outer[...], jnp.concatenate([turned, turned], axis=0))
    return [result[:, c * width : (c + 1) * width] for c in range(count)]


def put_rows(scratch, value, first, stride):
    size = value.shape[0]
    for k in range(value.shape[1] // size):
        block = value[:, k * size : (k + 1) * size].astype(BF).T
        scratch[pl.ds(first + k, size, stride=stride), :] = block.astype(F32)


def get_rows(scratch, first, stride, count):
    size = scratch.shape[1]
    return jnp.concatenate(
        [scratch[pl.ds(first + k, size, stride=stride), :].astype(BF).T for k in range(count)],
        axis=1,
    )


def fetch(pairs, sems):
    copies = [
        pltpu.make_async_copy(source, target, sems.at[i])
        for i, (source, target) in enumerate(pairs)
    ]
    for copy in copies:
        copy.start()
    return copies


def prepare_body(
    rows_in,
    conv_in,
    filt_in,
    w_in_in,
    w_out_in,
    inc_in,
    packed_out,
    later_out,
    gate_two_out,
    part_two_out,
    rows,
    conv,
    filt,
    w_in,
    w_out,
    inc,
    first,
    second,
    later,
    gate_two_kept,
    part_two_kept,
    sems,
    out_sems,
):
    channels = rows.shape[1]
    per = channels // rows.shape[0]
    got_filt, got_rows, got_w_in, got_inc, got_w_out, got_conv = fetch(
        [
            (filt_in, filt),
            (rows_in, rows),
            (w_in_in, w_in),
            (inc_in, inc),
            (w_out_in, w_out),
            (conv_in, conv),
        ],
        sems,
    )
    got_filt.wait()
    put_rows(first, filt[0], 0, 4 * per)
    put_rows(first, filt[1], per, 4 * per)
    got_rows.wait()
    got_w_in.wait()
    projected = mm(rows[...], w_in[...]).astype(BF)
    gate_one = projected[:, channels : 2 * channels]
    gate_two = projected[:, 2 * channels :]
    put_rows(first, gate_one, 2 * per, 4 * per)
    got_inc.wait()
    got_w_out.wait()
    mix_two = mm_t(inc[...], w_out[...])
    put_rows(first, mix_two * gate_two.astype(F32), 3 * per, 4 * per)
    packed_out[...] = first[...].astype(BF)
    sends = []
    gate_two_kept[...] = gate_two
    got_conv.wait()
    part_two_kept[...] = (mix_two * conv[1].astype(F32)).astype(BF)
    put_rows(second, projected[:, :channels], 0, 2 * per)
    put_rows(second, gate_one.astype(F32) * conv[0].astype(F32), per, 2 * per)
    later[...] = second[...].astype(BF)
    for i, (source, target) in enumerate(
        [(gate_two_kept, gate_two_out), (part_two_kept, part_two_out), (later, later_out)]
    ):
        send = pltpu.make_async_copy(source, target, out_sems.at[i])
        send.start()
        sends.append(send)
    for send in sends:
        send.wait()


def regrad_body(
    late,
    inc,
    done,
    w_out,
    gate_two_in,
    conv,
    later,
    packed,
    part_two_out,
    kept_out,
    part_two,
    gate_two,
    scratch,
    sems,
):
    per = inc.shape[1] // inc.shape[0]

    @pl.when(late[0] == 0)
    def _():
        gate, keep = fetch([(gate_two_in, gate_two), (inc, kept_out)], sems)
        mix_two = mm_t(inc[...], w_out[...])
        part_two[...] = (mix_two * conv[1].astype(F32)).astype(BF)
        part = pltpu.make_async_copy(part_two, part_two_out, sems.at[2])
        part.start()
        gate.wait()
        put_rows(scratch, mix_two * gate_two[...].astype(F32), 0, 2 * per)
        for k in range(per):
            empty = jnp.zeros((inc.shape[0], inc.shape[0]), F32)
            scratch[pl.ds(per + k, inc.shape[0], stride=2 * per), :] = empty
        packed[...] = scratch[...].astype(BF)
        keep.wait()
        part.wait()

    @pl.when(late[0] == 1)
    def _():
        part_two[...] = jnp.zeros_like(part_two)
        copies = fetch([(done, kept_out), (part_two, part_two_out), (later, packed)], sems)
        for copy in copies:
            copy.wait()


def signals(scratch, s, per):
    size = scratch.shape[1]
    stride = scratch.shape[0] // size
    return [scratch[pl.ds(s * per + k, size, stride=stride), :] for k in range(per)]


def send_rows(scratch, s, values):
    size = scratch.shape[1]
    stride = scratch.shape[0] // size
    for k, value in enumerate(values):
        scratch[pl.ds(s * len(values) + k, size, stride=stride), :] = value


def early_body(
    per,
    late,
    place,
    gains,
    data,
    later,
    outer_fwd,
    inner_fwd,
    inner_inv,
    outer_inv,
    turns,
    packed,
    spec_out,
    grad_out,
    known,
    out,
    spec,
    grad,
    sems,
):
    size = data.shape[1]

    @pl.when(late[0] == 1)
    def _():
        known[...] = data[...].astype(F32)
        filt_two = to_spectrum(signals(known, 1, per), outer_fwd, inner_fwd, turns)
        grad_two = signals(known, 3, per)
        spec_two = to_spectrum(grad_two, outer_fwd, inner_fwd, turns)
        spec[1] = spec_two
        mixed = from_spectrum(conj_times(filt_two, spec_two), inner_inv, outer_inv, turns)
        mix_one = [mixed[k] + gains[1, k * size + place[0]] * grad_two[k] for k in range(per)]
        send_rows(out, 1, mix_one)
        gate_one = signals(known, 2, per)
        grad_one = [mix_one[k] * gate_one[k] for k in range(per)]
        for k in range(per):
            grad[pl.ds(k * size, size), :] = grad_one[k]
        filt_one = to_spectrum(signals(known, 0, per), outer_fwd, inner_fwd, turns)
        spec_one = to_spectrum(grad_one, outer_fwd, inner_fwd, turns)
        spec[0] = spec_one
        copies = fetch([(spec, spec_out), (grad, grad_out)], sems)
        mixed = from_spectrum(conj_times(filt_one, spec_one), inner_inv, outer_inv, turns)
        send_rows(out, 0, [mixed[k] + gains[0, k * size + place[0]] * grad_one[k] for k in range(per)])
        packed[...] = out[...].astype(BF)
        for copy in copies:
            copy.wait()

    @pl.when(late[0] == 0)
    def _():
        known[...] = data[...].astype(F32)
        grad[...] = jnp.zeros_like(grad)
        spec[0] = to_spectrum(signals(known, 0, per), outer_fwd, inner_fwd, turns)
        spec[1] = to_spectrum(signals(known, 1, per), outer_fwd, inner_fwd, turns)
        copies = fetch([(spec, spec_out), (grad, grad_out), (later, packed)], sems)
        for copy in copies:
            copy.wait()


def skip_rows(per, grads, others, out):
    size = out.shape[1]
    rows = out.shape[0] // size
    lane = lax.broadcasted_iota(jnp.int32, (1, size), 1)
    skip_row = jnp.zeros((1, size), F32)
    for w in range(2):
        for k in range(per):
            term = grads[w][k] * others[w][k]
            total = jnp.sum(jnp.sum(term, axis=0, keepdims=True), axis=1, keepdims=True)
            high = total.astype(BF).astype(F32)
            skip_row = jnp.where(lane == w * per + k, high, skip_row)
            skip_row = jnp.where(lane == (2 + w) * per + k, total - high, skip_row)
    out[pl.ds(4 * per, size, stride=rows), :] = jnp.broadcast_to(skip_row, (size, size))
    for r in range(4 * per + 1, rows):
        out[pl.ds(r, size, stride=rows), :] = jnp.zeros((size, size), F32)


def late_body(
    per,
    late,
    place,
    gains,
    first,
    second,
    third,
    held_in,
    grad_in,
    spec_in,
    outer_fwd,
    inner_fwd,
    inner_inv,
    outer_inv,
    turns,
    packed,
    known,
    other,
    fresh,
    out,
    held,
    grad_held,
    spec,
    sems,
):
    size = first.shape[1]
    copies = fetch([(held_in, held), (spec_in, spec), (grad_in, grad_held)], sems)
    fresh[...] = third[...].astype(F32)
    known[...] = first[...].astype(F32)

    @pl.when(late[0] == 0)
    def _():
        grad_two = signals(fresh, 0, per)
        spec_two = to_spectrum(grad_two, outer_fwd, inner_fwd, turns)
        for copy in copies:
            copy.wait()
        mixed = from_spectrum(conj_times(held[1], spec_two), inner_inv, outer_inv, turns)
        send_rows(out, 3, from_spectrum(conj_times(spec[1], spec_two), inner_inv, outer_inv, turns))
        mix_one = [mixed[k] + gains[1, k * size + place[0]] * grad_two[k] for k in range(per)]
        send_rows(out, 1, mix_one)
        gate_one = signals(known, 2, per)
        grad_one = [mix_one[k] * gate_one[k] for k in range(per)]
        spec_one = to_spectrum(grad_one, outer_fwd, inner_fwd, turns)
        mixed = from_spectrum(conj_times(held[0], spec_one), inner_inv, outer_inv, turns)
        send_rows(out, 2, from_spectrum(conj_times(spec[0], spec_one), inner_inv, outer_inv, turns))
        send_rows(out, 0, [mixed[k] + gains[0, k * size + place[0]] * grad_one[k] for k in range(per)])
        other[...] = second[...].astype(F32)
        skip_rows(
            per, (grad_one, grad_two), (signals(other, 0, per), signals(other, 1, per)), out
        )
        packed[...] = out[...].astype(BF)

    @pl.when(late[0] == 1)
    def _():
        values, gated = signals(fresh, 0, per), signals(fresh, 1, per)
        spec_one = to_spectrum(values, outer_fwd, inner_fwd, turns)
        spec_two = to_spectrum(gated, outer_fwd, inner_fwd, turns)
        for copy in copies:
            copy.wait()
        send_rows(out, 2, from_spectrum(conj_times(spec_one, held[0]), inner_inv, outer_inv, turns))
        send_rows(out, 3, from_spectrum(conj_times(spec_two, held[1]), inner_inv, outer_inv, turns))
        empty = [jnp.zeros((size, size), F32)] * per
        send_rows(out, 0, empty)
        send_rows(out, 1, empty)
        grad_one = [grad_held[pl.ds(k * size, size), :] for k in range(per)]
        skip_rows(per, (grad_one, signals(known, 3, per)), (values, gated), out)
        packed[...] = out[...].astype(BF)


def input_grad(inc, values, mix_one, conv_one, part_two, w_in):
    gate_one = mix_one.astype(F32) * conv_one.astype(F32)
    proj = jnp.concatenate([values.astype(BF), gate_one.astype(BF), part_two], axis=1)
    return (inc.astype(F32) + mm_t(proj, w_in)).astype(BF)


def hand_body(
    per,
    late,
    data,
    conv,
    part_two_in,
    inc_in,
    w_in,
    outer_fwd,
    inner_fwd,
    turns,
    result,
    spec_out,
    scratch,
    part_two,
    inc,
    spec,
    sems,
):
    @pl.when(late[0] == 1)
    def _():
        copies = fetch([(part_two_in, part_two), (inc_in, inc)], sems)
        scratch[...] = data[...].astype(F32)
        values = get_rows(scratch, 0, 2 * per, per)
        mix_one = get_rows(scratch, per, 2 * per, per)
        for copy in copies:
            copy.wait()
        result[...] = input_grad(inc[...], values, mix_one, conv[0], part_two[...], w_in[...])

    @pl.when(late[0] == 0)
    def _():
        scratch[...] = data[...].astype(F32)
        copies = []
        for s in range(2):
            spec[s] = to_spectrum(signals(scratch, s, per), outer_fwd, inner_fwd, turns)
            copies.append(pltpu.make_async_copy(spec.at[s], spec_out.at[s], sems.at[s]))
            copies[s].start()
        result[...] = jnp.zeros_like(result)
        for copy in copies:
            copy.wait()


def finish_body(
    per,
    rescale,
    late,
    data,
    conv,
    part_two,
    inc,
    w_in,
    result,
    filt_grads,
    skip_grads,
    scratch,
):
    size = data.shape[1]
    stride = data.shape[0] // size
    scratch[...] = data[...].astype(F32)

    @pl.when(late[0] == 0)
    def _():
        values = get_rows(scratch, 0, stride, per)
        mix_one = get_rows(scratch, per, stride, per)
        result[...] = input_grad(inc[...], values, mix_one, conv[0], part_two[...], w_in[...])

    @pl.when(late[0] == 1)
    def _():
        result[...] = inc[...]

    filt_grads[0] = (get_rows(scratch, 2 * per, stride, per).astype(F32) * rescale).astype(BF)
    filt_grads[1] = (get_rows(scratch, 3 * per, stride, per).astype(F32) * rescale).astype(BF)
    sums = scratch[pl.ds(4 * per, size, stride=stride), :].T
    sums = (sums[: 2 * per] + sums[2 * per : 4 * per]) * rescale
    for w in range(2):
        for k in range(per):
            row = w * per + k
            skip_grads[pl.ds(w, 1), pl.ds(k * size, size)] = sums[row : row + 1]


def call(body, out_shapes, scratch, *operands, smem=0, direct=(), direct_out=(), limit=VMEM_LIMIT):
    def space(i):
        if i < smem:
            return pltpu.SMEM
        return pltpu.HBM if i in direct else pltpu.VMEM

    return pl.pallas_call(
        body,
        out_shape=[
            (pltpu.HBM if i in direct_out else jax.ShapeDtypeStruct)(shape, dtype)
            for i, (shape, dtype) in enumerate(out_shapes)
        ],
        in_specs=[pl.BlockSpec(memory_space=space(i)) for i in range(len(operands))],
        out_specs=[
            pl.BlockSpec(memory_space=pltpu.HBM if i in direct_out else pltpu.VMEM)
            for i in range(len(out_shapes))
        ],
        scratch_shapes=[
            pltpu.VMEM(shape, F32) if isinstance(shape, tuple) else shape for shape in scratch
        ],
        compiler_params=pltpu.CompilerParams(vmem_limit_bytes=limit),
    )(
        *[
            pltpu.with_memory_space_constraint(x, pltpu.HBM) if i in direct else x
            for i, x in enumerate(operands)
        ]
    )


def exchange(rows, parts):
    per_part = rows.shape[0] // parts
    tile = math.gcd(per_part, 2)
    cut = rows.reshape(parts, per_part // tile, tile, rows.shape[1])
    return lax.all_to_all(cut, "seq", split_axis=0, concat_axis=0, tiled=True).reshape(rows.shape)


def on_device(layer_input, conv_out, filters, skip_gain, weight_in, weight_out, grad_output):
    tokens, channels = grad_output.shape
    parts = lax.axis_size("seq")
    per = channels // parts
    w_in, w_out, conv = weight_in[0], weight_out[0], conv_out[0]
    outer_fwd, inner_fwd, inner_inv, outer_inv, turns = transform_tables(parts, tokens)
    late = lax.axis_index("section").astype(jnp.int32).reshape(1)
    place = lax.axis_index("seq").astype(jnp.int32).reshape(1)

    def rows(count):
        return (parts * count, tokens)

    token_rows = ((tokens, channels), BF)
    spectra = ((2, per * parts, 2 * tokens), F32)

    packed, later, gate_two, part_two = call(
        prepare_body,
        [(rows(4 * per), BF), (rows(2 * per), BF), token_rows, token_rows],
        [
            pltpu.VMEM((tokens, channels), BF),
            pltpu.VMEM((2, tokens, channels), BF),
            pltpu.VMEM((2, tokens, channels), BF),
            pltpu.VMEM(w_in.shape, BF),
            pltpu.VMEM(w_out.shape, BF),
            pltpu.VMEM((tokens, channels), BF),
            rows(4 * per),
            rows(2 * per),
            pltpu.VMEM(rows(2 * per), BF),
            pltpu.VMEM((tokens, channels), BF),
            pltpu.VMEM((tokens, channels), BF),
            pltpu.SemaphoreType.DMA((6,)),
            pltpu.SemaphoreType.DMA((3,)),
        ],
        layer_input[0], conv, filters[0], w_in, w_out, grad_output,
        direct=range(6), direct_out=range(1, 4),
    )
    packed, late, place = lax.optimization_barrier((packed, late, place))
    first = exchange(packed, parts)
    packed, held, grad_held = call(
        functools.partial(early_body, per),
        [(rows(2 * per), BF), spectra, (rows(per), F32)],
        [
            rows(4 * per), rows(2 * per), spectra[0], rows(per), pltpu.SemaphoreType.DMA((3,)),
        ],
        late, place, skip_gain[0], first, later, outer_fwd, inner_fwd, inner_inv, outer_inv, turns,
        smem=3, direct=(4,), direct_out=(1, 2),
    )
    second = exchange(packed, parts)
    done, spec = call(
        functools.partial(hand_body, per),
        [token_rows, spectra],
        [
            rows(2 * per), pltpu.VMEM((tokens, channels), BF), pltpu.VMEM((tokens, channels), BF),
            spectra[0], pltpu.SemaphoreType.DMA((2,)),
        ],
        late, second, conv, part_two, grad_output, w_in, outer_fwd, inner_fwd, turns,
        smem=1, direct=(3, 4), direct_out=(1,),
    )
    handed = lax.ppermute(done, "section", [(0, 1), (1, 0)])
    packed, part_two, kept = call(
        regrad_body,
        [(rows(2 * per), BF), token_rows, token_rows],
        [
            pltpu.VMEM((tokens, channels), BF), pltpu.VMEM((tokens, channels), BF), rows(2 * per),
            pltpu.SemaphoreType.DMA((3,)),
        ],
        late, handed, done, w_out, gate_two, conv, later,
        smem=1, direct=(4, 6), direct_out=(1, 2),
    )
    third = exchange(packed, parts)
    out_rows = 4 * per + 2
    (packed,) = call(
        functools.partial(late_body, per),
        [(rows(out_rows), BF)],
        [
            rows(4 * per), rows(2 * per), rows(2 * per), rows(out_rows), spectra[0], rows(per),
            spectra[0],
pltpu.SemaphoreType.DMA((3,)),
        ],
        late, place, skip_gain[0], first, second, third, held, grad_held, spec,
        outer_fwd, inner_fwd, inner_inv, outer_inv, turns,
        smem=3, direct=range(6, 9),
    )
    back = exchange(packed, parts)
    grad_rows, filter_grads, skip_grads = call(
        functools.partial(finish_body, per, 1.0 / math.sqrt(parts * tokens)),
        [token_rows, ((2, tokens, channels), BF), ((2, channels), F32)],
        [rows(out_rows)],
        late, back, conv, part_two, kept, w_in,
        smem=1,
    )
    return (grad_rows[None], filter_grads[None], skip_grads[None])


def solution(mesh):
    in_specs = (
        P("section", "seq", None),
        P("section", None, "seq", None),
        P("section", None, "seq", None),
        P("section", None, None),
        P("section", None, None),
        P("section", None, None),
        P("seq", None),
    )
    out_specs = (
        P("section", "seq", None),
        P("section", None, "seq", None),
        P("section", None, None),
    )
    return jax.shard_map(
        on_device, mesh=mesh, in_specs=in_specs, out_specs=out_specs, check_vma=False
    )
```

```python
import functools
import math

import jax
import jax.numpy as jnp
import ml_dtypes
import numpy as np
from jax import lax
from jax.experimental import pallas as pl
from jax.experimental.pallas import tpu as pltpu
from jax.sharding import PartitionSpec as P

BF = jnp.bfloat16
F32 = jnp.float32
VMEM_LIMIT = 20 * 1024 * 1024


def split_table(table, axis):
    high = table.astype(np.float32).astype(ml_dtypes.bfloat16)
    low = (table - high.astype(np.float64)).astype(np.float32).astype(ml_dtypes.bfloat16)
    return np.concatenate([high, low], axis=axis)


def transform_tables(blocks, width):
    period = 2 * blocks * width
    half = np.arange(blocks) + 0.5
    outer = 2.0 * np.pi * np.outer(half, np.arange(blocks)) / (2 * blocks)
    inner = 2.0 * np.pi * np.outer(np.arange(width), np.arange(width)) / width
    turn = 2.0 * np.pi * np.outer(half, np.arange(width)) / period
    cos_in, sin_in = np.cos(inner), np.sin(inner)
    outer_fwd = split_table(np.concatenate([np.cos(outer), -np.sin(outer)], 0), 1)
    inner_fwd = split_table(np.block([[cos_in, -sin_in], [sin_in, cos_in]]), 0)
    inner_inv = split_table(np.block([[cos_in, sin_in], [-sin_in, cos_in]]), 0)
    outer_inv = split_table(
        np.concatenate([np.cos(outer).T, -np.sin(outer).T], 1) * (2.0 / period), 1
    )
    turns = np.stack([np.cos(turn), np.sin(turn)]).astype(np.float32)
    return outer_fwd, inner_fwd, inner_inv, outer_inv, turns


def mm(left, right):
    return jnp.dot(left, right, preferred_element_type=F32)


def mm_t(left, right):
    return lax.dot_general(left, right, (((1,), (1,)), ((), ())), preferred_element_type=F32)


def to_spectrum(signals, outer, inner, turns):
    count = len(signals)
    size = signals[0].shape[0]
    width = signals[0].shape[1]
    data = jnp.concatenate([signal.astype(BF) for signal in signals], axis=1)
    mixed = mm(outer[...], jnp.concatenate([data, data], axis=0))
    turn_cos, turn_sin = turns[0], turns[1]
    rows = []
    for c in range(count):
        real = mixed[:size, c * width : (c + 1) * width]
        imag = mixed[size:, c * width : (c + 1) * width]
        rows.append(
            jnp.concatenate(
                [real * turn_cos + imag * turn_sin, imag * turn_cos - real * turn_sin], axis=1
            ).astype(BF)
        )
    turned = jnp.concatenate(rows, axis=0)
    return mm(jnp.concatenate([turned, turned], axis=1), inner[...])


def conj_times(left, right):
    width = left.shape[1] // 2
    left_real, left_imag = left[:, :width], left[:, width:]
    right_real, right_imag = right[:, :width], right[:, width:]
    return jnp.concatenate(
        [
            left_real * right_real + left_imag * right_imag,
            left_real * right_imag - left_imag * right_real,
        ],
        axis=1,
    )


def from_spectrum(product, inner, outer, turns):
    width = product.shape[1] // 2
    size = turns.shape[1]
    count = product.shape[0] // size
    data = product.astype(BF)
    mixed = mm(jnp.concatenate([data, data], axis=1), inner[...])
    turn_cos, turn_sin = turns[0], turns[1]
    reals, imags = [], []
    for c in range(count):
        real = mixed[c * size : (c + 1) * size, :width]
        imag = mixed[c * size : (c + 1) * size, width:]
        reals.append((real * turn_cos - imag * turn_sin).astype(BF))
        imags.append((imag * turn_cos + real * turn_sin).astype(BF))
    turned = jnp.concatenate(
        [jnp.concatenate(reals, axis=1), jnp.concatenate(imags, axis=1)], axis=0
    )
    result = mm(outer[...], jnp.concatenate([turned, turned], axis=0))
    return [result[:, c * width : (c + 1) * width] for c in range(count)]


def put_rows(scratch, value, first, stride):
    size = value.shape[0]
    for k in range(value.shape[1] // size):
        block = value[:, k * size : (k + 1) * size].astype(BF).T
        scratch[pl.ds(first + k, size, stride=stride), :] = block.astype(F32)


def get_rows(scratch, first, stride, count):
    size = scratch.shape[1]
    return jnp.concatenate(
        [scratch[pl.ds(first + k, size, stride=stride), :].astype(BF).T for k in range(count)],
        axis=1,
    )


def fetch(pairs, sems):
    copies = [
        pltpu.make_async_copy(source, target, sems.at[i])
        for i, (source, target) in enumerate(pairs)
    ]
    for copy in copies:
        copy.start()
    return copies


def prepare_body(
    rows_in,
    conv_in,
    filt_in,
    w_in_in,
    w_out_in,
    inc_in,
    packed_out,
    later_out,
    gate_two_out,
    part_two_out,
    rows,
    conv,
    filt,
    w_in,
    w_out,
    inc,
    first,
    second,
    sems,
):
    channels = rows.shape[1]
    per = channels // rows.shape[0]
    got_filt, got_rows, got_w_in, got_inc, got_w_out, got_conv = fetch(
        [
            (filt_in, filt),
            (rows_in, rows),
            (w_in_in, w_in),
            (inc_in, inc),
            (w_out_in, w_out),
            (conv_in, conv),
        ],
        sems,
    )
    got_filt.wait()
    put_rows(first, filt[0], 0, 4 * per)
    put_rows(first, filt[1], per, 4 * per)
    got_rows.wait()
    got_w_in.wait()
    projected = mm(rows[...], w_in[...]).astype(BF)
    gate_one = projected[:, channels : 2 * channels]
    gate_two = projected[:, 2 * channels :]
    put_rows(first, gate_one, 2 * per, 4 * per)
    got_inc.wait()
    got_w_out.wait()
    mix_two = mm_t(inc[...], w_out[...])
    put_rows(first, mix_two * gate_two.astype(F32), 3 * per, 4 * per)
    packed_out[...] = first[...].astype(BF)
    gate_two_out[...] = gate_two
    got_conv.wait()
    part_two_out[...] = (mix_two * conv[1].astype(F32)).astype(BF)
    put_rows(second, projected[:, :channels], 0, 2 * per)
    put_rows(second, gate_one.astype(F32) * conv[0].astype(F32), per, 2 * per)
    later_out[...] = second[...].astype(BF)


def regrad_body(late, inc, done, w_out, gate_two, conv, later, packed, part_two, kept, scratch):
    size = inc.shape[0]
    per = inc.shape[1] // size

    @pl.when(late[0] == 0)
    def _():
        kept[...] = inc[...]
        mix_two = mm_t(inc[...], w_out[...])
        part_two[...] = (mix_two * conv[1].astype(F32)).astype(BF)
        put_rows(scratch, mix_two * gate_two[...].astype(F32), 0, 2 * per)
        for k in range(per):
            scratch[pl.ds(per + k, size, stride=2 * per), :] = jnp.zeros((size, size), F32)
        packed[...] = scratch[...].astype(BF)

    @pl.when(late[0] == 1)
    def _():
        kept[...] = done[...]
        part_two[...] = jnp.zeros_like(part_two)
        packed[...] = later[...]


def signals(scratch, s, per):
    size = scratch.shape[1]
    stride = scratch.shape[0] // size
    return [scratch[pl.ds(s * per + k, size, stride=stride), :] for k in range(per)]


def send_rows(scratch, s, values):
    size = scratch.shape[1]
    stride = scratch.shape[0] // size
    for k, value in enumerate(values):
        scratch[pl.ds(s * len(values) + k, size, stride=stride), :] = value


def early_body(
    per,
    late,
    place,
    gains,
    data,
    later,
    outer_fwd,
    inner_fwd,
    inner_inv,
    outer_inv,
    turns,
    packed,
    spec,
    grad,
    known,
    out,
):
    size = data.shape[1]

    @pl.when(late[0] == 1)
    def _():
        known[...] = data[...].astype(F32)
        filt_two = to_spectrum(signals(known, 1, per), outer_fwd, inner_fwd, turns)
        grad_two = signals(known, 3, per)
        spec_two = to_spectrum(grad_two, outer_fwd, inner_fwd, turns)
        spec[1] = spec_two
        mixed = from_spectrum(conj_times(filt_two, spec_two), inner_inv, outer_inv, turns)
        mix_one = [mixed[k] + gains[1, k * size + place[0]] * grad_two[k] for k in range(per)]
        send_rows(out, 1, mix_one)
        gate_one = signals(known, 2, per)
        grad_one = [mix_one[k] * gate_one[k] for k in range(per)]
        for k in range(per):
            grad[pl.ds(k * size, size), :] = grad_one[k]
        filt_one = to_spectrum(signals(known, 0, per), outer_fwd, inner_fwd, turns)
        spec_one = to_spectrum(grad_one, outer_fwd, inner_fwd, turns)
        spec[0] = spec_one
        mixed = from_spectrum(conj_times(filt_one, spec_one), inner_inv, outer_inv, turns)
        send_rows(out, 0, [mixed[k] + gains[0, k * size + place[0]] * grad_one[k] for k in range(per)])
        packed[...] = out[...].astype(BF)

    @pl.when(late[0] == 0)
    def _():
        packed[...] = later[...]
        known[...] = data[...].astype(F32)
        grad[...] = jnp.zeros_like(grad)
        spec[0] = to_spectrum(signals(known, 0, per), outer_fwd, inner_fwd, turns)
        spec[1] = to_spectrum(signals(known, 1, per), outer_fwd, inner_fwd, turns)


def skip_rows(per, grads, others, out):
    size = out.shape[1]
    rows = out.shape[0] // size
    lane = lax.broadcasted_iota(jnp.int32, (1, size), 1)
    skip_row = jnp.zeros((1, size), F32)
    for w in range(2):
        for k in range(per):
            term = grads[w][k] * others[w][k]
            total = jnp.sum(jnp.sum(term, axis=0, keepdims=True), axis=1, keepdims=True)
            high = total.astype(BF).astype(F32)
            skip_row = jnp.where(lane == w * per + k, high, skip_row)
            skip_row = jnp.where(lane == (2 + w) * per + k, total - high, skip_row)
    out[pl.ds(4 * per, size, stride=rows), :] = jnp.broadcast_to(skip_row, (size, size))
    for r in range(4 * per + 1, rows):
        out[pl.ds(r, size, stride=rows), :] = jnp.zeros((size, size), F32)


def late_body(
    per,
    late,
    place,
    gains,
    first,
    second,
    third,
    held,
    grad_held,
    spec,
    outer_fwd,
    inner_fwd,
    inner_inv,
    outer_inv,
    turns,
    packed,
    known,
    other,
    fresh,
    out,
):
    size = first.shape[1]
    fresh[...] = third[...].astype(F32)
    known[...] = first[...].astype(F32)

    @pl.when(late[0] == 0)
    def _():
        grad_two = signals(fresh, 0, per)
        spec_two = to_spectrum(grad_two, outer_fwd, inner_fwd, turns)
        mixed = from_spectrum(conj_times(held[1], spec_two), inner_inv, outer_inv, turns)
        send_rows(out, 3, from_spectrum(conj_times(spec[1], spec_two), inner_inv, outer_inv, turns))
        mix_one = [mixed[k] + gains[1, k * size + place[0]] * grad_two[k] for k in range(per)]
        send_rows(out, 1, mix_one)
        gate_one = signals(known, 2, per)
        grad_one = [mix_one[k] * gate_one[k] for k in range(per)]
        spec_one = to_spectrum(grad_one, outer_fwd, inner_fwd, turns)
        mixed = from_spectrum(conj_times(held[0], spec_one), inner_inv, outer_inv, turns)
        send_rows(out, 2, from_spectrum(conj_times(spec[0], spec_one), inner_inv, outer_inv, turns))
        send_rows(out, 0, [mixed[k] + gains[0, k * size + place[0]] * grad_one[k] for k in range(per)])
        other[...] = second[...].astype(F32)
        skip_rows(
            per, (grad_one, grad_two), (signals(other, 0, per), signals(other, 1, per)), out
        )
        packed[...] = out[...].astype(BF)

    @pl.when(late[0] == 1)
    def _():
        values, gated = signals(fresh, 0, per), signals(fresh, 1, per)
        spec_one = to_spectrum(values, outer_fwd, inner_fwd, turns)
        spec_two = to_spectrum(gated, outer_fwd, inner_fwd, turns)
        send_rows(out, 2, from_spectrum(conj_times(spec_one, held[0]), inner_inv, outer_inv, turns))
        send_rows(out, 3, from_spectrum(conj_times(spec_two, held[1]), inner_inv, outer_inv, turns))
        empty = [jnp.zeros((size, size), F32)] * per
        send_rows(out, 0, empty)
        send_rows(out, 1, empty)
        grad_one = [grad_held[pl.ds(k * size, size), :] for k in range(per)]
        skip_rows(per, (grad_one, signals(known, 3, per)), (values, gated), out)
        packed[...] = out[...].astype(BF)


def input_grad(inc, values, mix_one, conv_one, part_two, w_in):
    gate_one = mix_one.astype(F32) * conv_one.astype(F32)
    proj = jnp.concatenate([values.astype(BF), gate_one.astype(BF), part_two], axis=1)
    return (inc.astype(F32) + mm_t(proj, w_in)).astype(BF)


def hand_body(
    per,
    late,
    data,
    conv,
    part_two,
    inc,
    w_in,
    outer_fwd,
    inner_fwd,
    turns,
    result,
    spec,
    scratch,
):
    @pl.when(late[0] == 1)
    def _():
        scratch[...] = data[...].astype(F32)
        values = get_rows(scratch, 0, 2 * per, per)
        mix_one = get_rows(scratch, per, 2 * per, per)
        result[...] = input_grad(inc[...], values, mix_one, conv[0], part_two[...], w_in[...])

    @pl.when(late[0] == 0)
    def _():
        scratch[...] = data[...].astype(F32)
        for s in range(2):
            spec[s] = to_spectrum(signals(scratch, s, per), outer_fwd, inner_fwd, turns)
        result[...] = jnp.zeros_like(result)


def finish_body(
    per,
    rescale,
    late,
    data,
    conv,
    part_two,
    inc,
    w_in,
    result,
    filt_grads,
    skip_grads,
    scratch,
):
    size = data.shape[1]
    stride = data.shape[0] // size
    scratch[...] = data[...].astype(F32)

    @pl.when(late[0] == 0)
    def _():
        values = get_rows(scratch, 0, stride, per)
        mix_one = get_rows(scratch, per, stride, per)
        result[...] = input_grad(inc[...], values, mix_one, conv[0], part_two[...], w_in[...])

    @pl.when(late[0] == 1)
    def _():
        result[...] = inc[...]

    filt_grads[0] = (get_rows(scratch, 2 * per, stride, per).astype(F32) * rescale).astype(BF)
    filt_grads[1] = (get_rows(scratch, 3 * per, stride, per).astype(F32) * rescale).astype(BF)
    sums = scratch[pl.ds(4 * per, size, stride=stride), :].T
    sums = (sums[: 2 * per] + sums[2 * per : 4 * per]) * rescale
    for w in range(2):
        for k in range(per):
            row = w * per + k
            skip_grads[pl.ds(w, 1), pl.ds(k * size, size)] = sums[row : row + 1]


def call(body, out_shapes, scratch, *operands, smem=0, direct=(), direct_out=(), limit=VMEM_LIMIT):
    def space(i):
        if i < smem:
            return pltpu.SMEM
        return pltpu.HBM if i in direct else pltpu.VMEM

    return pl.pallas_call(
        body,
        out_shape=[
            (pltpu.HBM if i in direct_out else jax.ShapeDtypeStruct)(shape, dtype)
            for i, (shape, dtype) in enumerate(out_shapes)
        ],
        in_specs=[pl.BlockSpec(memory_space=space(i)) for i in range(len(operands))],
        out_specs=[
            pl.BlockSpec(memory_space=pltpu.HBM if i in direct_out else pltpu.VMEM)
            for i in range(len(out_shapes))
        ],
        scratch_shapes=[
            pltpu.VMEM(shape, F32) if isinstance(shape, tuple) else shape for shape in scratch
        ],
        compiler_params=pltpu.CompilerParams(vmem_limit_bytes=limit),
    )(
        *[
            pltpu.with_memory_space_constraint(x, pltpu.HBM) if i in direct else x
            for i, x in enumerate(operands)
        ]
    )


def exchange(rows, parts):
    per_part = rows.shape[0] // parts
    tile = math.gcd(per_part, 2)
    cut = rows.reshape(parts, per_part // tile, tile, rows.shape[1])
    return lax.all_to_all(cut, "seq", split_axis=0, concat_axis=0, tiled=True).reshape(rows.shape)


def on_device(layer_input, conv_out, filters, skip_gain, weight_in, weight_out, grad_output):
    tokens, channels = grad_output.shape
    parts = lax.axis_size("seq")
    per = channels // parts
    w_in, w_out, conv = weight_in[0], weight_out[0], conv_out[0]
    outer_fwd, inner_fwd, inner_inv, outer_inv, turns = transform_tables(parts, tokens)
    late = lax.axis_index("section").astype(jnp.int32).reshape(1)
    place = lax.axis_index("seq").astype(jnp.int32).reshape(1)

    def rows(count):
        return (parts * count, tokens)

    token_rows = ((tokens, channels), BF)
    spectra = ((2, per * parts, 2 * tokens), F32)

    packed, later, gate_two, part_two = call(
        prepare_body,
        [(rows(4 * per), BF), (rows(2 * per), BF), token_rows, token_rows],
        [
            pltpu.VMEM((tokens, channels), BF),
            pltpu.VMEM((2, tokens, channels), BF),
            pltpu.VMEM((2, tokens, channels), BF),
            pltpu.VMEM(w_in.shape, BF),
            pltpu.VMEM(w_out.shape, BF),
            pltpu.VMEM((tokens, channels), BF),
            rows(4 * per),
            rows(2 * per),
            pltpu.SemaphoreType.DMA((6,)),
        ],
        layer_input[0], conv, filters[0], w_in, w_out, grad_output,
        direct=range(6),
    )
    packed, late, place = lax.optimization_barrier((packed, late, place))
    first = exchange(packed, parts)
    packed, held, grad_held = call(
        functools.partial(early_body, per),
        [(rows(2 * per), BF), spectra, (rows(per), F32)],
        [rows(4 * per), rows(2 * per)],
        late, place, skip_gain[0], first, later, outer_fwd, inner_fwd, inner_inv, outer_inv, turns,
        smem=3,
    )
    second = exchange(packed, parts)
    done, spec = call(
        functools.partial(hand_body, per),
        [token_rows, spectra],
        [
            rows(2 * per),
        ],
        late, second, conv, part_two, grad_output, w_in, outer_fwd, inner_fwd, turns,
        smem=1,
    )
    handed = lax.ppermute(done, "section", [(0, 1), (1, 0)])
    packed, part_two, kept = call(
        regrad_body,
        [(rows(2 * per), BF), token_rows, token_rows],
        [rows(2 * per)],
        late, handed, done, w_out, gate_two, conv, later,
        smem=1,
    )
    third = exchange(packed, parts)
    out_rows = 4 * per + 2
    (packed,) = call(
        functools.partial(late_body, per),
        [(rows(out_rows), BF)],
        [
            rows(4 * per), rows(2 * per), rows(2 * per), rows(out_rows),
        ],
        late, place, skip_gain[0], first, second, third, held, grad_held, spec,
        outer_fwd, inner_fwd, inner_inv, outer_inv, turns,
        smem=3,
    )
    back = exchange(packed, parts)
    grad_rows, filter_grads, skip_grads = call(
        functools.partial(finish_body, per, 1.0 / math.sqrt(parts * tokens)),
        [token_rows, ((2, tokens, channels), BF), ((2, channels), F32)],
        [rows(out_rows)],
        late, back, conv, part_two, kept, w_in,
        smem=1,
    )
    return (grad_rows[None], filter_grads[None], skip_grads[None])


def solution(mesh):
    in_specs = (
        P("section", "seq", None),
        P("section", None, "seq", None),
        P("section", None, "seq", None),
        P("section", None, None),
        P("section", None, None),
        P("section", None, None),
        P("seq", None),
    )
    out_specs = (
        P("section", "seq", None),
        P("section", None, "seq", None),
        P("section", None, None),
    )
    return jax.shard_map(
        on_device, mesh=mesh, in_specs=in_specs, out_specs=out_specs, check_vma=False
    )
```

```python
import functools
import math

import jax
import jax.numpy as jnp
import ml_dtypes
import numpy as np
from jax import lax
from jax.experimental import pallas as pl
from jax.experimental.pallas import tpu as pltpu
from jax.sharding import PartitionSpec as P

BF = jnp.bfloat16
F32 = jnp.float32
VMEM_LIMIT = 20 * 1024 * 1024


def split_table(table, axis):
    high = table.astype(np.float32).astype(ml_dtypes.bfloat16)
    low = (table - high.astype(np.float64)).astype(np.float32).astype(ml_dtypes.bfloat16)
    return np.concatenate([high, low], axis=axis)


def transform_tables(blocks, width):
    period = 2 * blocks * width
    half = np.arange(blocks) + 0.5
    outer = 2.0 * np.pi * np.outer(half, np.arange(blocks)) / (2 * blocks)
    inner = 2.0 * np.pi * np.outer(np.arange(width), np.arange(width)) / width
    turn = 2.0 * np.pi * np.outer(half, np.arange(width)) / period
    cos_in, sin_in = np.cos(inner), np.sin(inner)
    outer_fwd = split_table(np.concatenate([np.cos(outer), -np.sin(outer)], 0), 1)
    inner_fwd = split_table(np.block([[cos_in, -sin_in], [sin_in, cos_in]]), 0)
    inner_inv = split_table(np.block([[cos_in, sin_in], [-sin_in, cos_in]]), 0)
    outer_inv = split_table(
        np.concatenate([np.cos(outer).T, -np.sin(outer).T], 1) * (2.0 / period), 1
    )
    turns = np.stack([np.cos(turn), np.sin(turn)]).astype(np.float32)
    return outer_fwd, inner_fwd, inner_inv, outer_inv, turns


def mm(left, right):
    return jnp.dot(left, right, preferred_element_type=F32)


def mm_t(left, right):
    return lax.dot_general(left, right, (((1,), (1,)), ((), ())), preferred_element_type=F32)


def to_spectrum(signals, outer, inner, turns):
    count = len(signals)
    size = signals[0].shape[0]
    width = signals[0].shape[1]
    data = jnp.concatenate([signal.astype(BF) for signal in signals], axis=1)
    mixed = mm(outer[...], jnp.concatenate([data, data], axis=0))
    turn_cos, turn_sin = turns[0], turns[1]
    rows = []
    for c in range(count):
        real = mixed[:size, c * width : (c + 1) * width]
        imag = mixed[size:, c * width : (c + 1) * width]
        rows.append(
            jnp.concatenate(
                [real * turn_cos + imag * turn_sin, imag * turn_cos - real * turn_sin], axis=1
            ).astype(BF)
        )
    turned = jnp.concatenate(rows, axis=0)
    return mm(jnp.concatenate([turned, turned], axis=1), inner[...])


def conj_times(left, right):
    width = left.shape[1] // 2
    left_real, left_imag = left[:, :width], left[:, width:]
    right_real, right_imag = right[:, :width], right[:, width:]
    return jnp.concatenate(
        [
            left_real * right_real + left_imag * right_imag,
            left_real * right_imag - left_imag * right_real,
        ],
        axis=1,
    )


def from_spectrum(product, inner, outer, turns):
    width = product.shape[1] // 2
    size = turns.shape[1]
    count = product.shape[0] // size
    data = product.astype(BF)
    mixed = mm(jnp.concatenate([data, data], axis=1), inner[...])
    turn_cos, turn_sin = turns[0], turns[1]
    reals, imags = [], []
    for c in range(count):
        real = mixed[c * size : (c + 1) * size, :width]
        imag = mixed[c * size : (c + 1) * size, width:]
        reals.append((real * turn_cos - imag * turn_sin).astype(BF))
        imags.append((imag * turn_cos + real * turn_sin).astype(BF))
    turned = jnp.concatenate(
        [jnp.concatenate(reals, axis=1), jnp.concatenate(imags, axis=1)], axis=0
    )
    result = mm(outer[...], jnp.concatenate([turned, turned], axis=0))
    return [result[:, c * width : (c + 1) * width] for c in range(count)]


def put_rows(scratch, value, first, stride):
    size = value.shape[0]
    for k in range(value.shape[1] // size):
        block = value[:, k * size : (k + 1) * size].astype(BF).T
        scratch[pl.ds(first + k, size, stride=stride), :] = block.astype(F32)


def get_rows(scratch, first, stride, count):
    size = scratch.shape[1]
    return jnp.concatenate(
        [scratch[pl.ds(first + k, size, stride=stride), :].astype(BF).T for k in range(count)],
        axis=1,
    )


def fetch(pairs, sems):
    copies = [
        pltpu.make_async_copy(source, target, sems.at[i])
        for i, (source, target) in enumerate(pairs)
    ]
    for copy in copies:
        copy.start()
    return copies


def prepare_body(
    rows_in,
    filt_in,
    w_in_in,
    w_out_in,
    inc_in,
    packed,
    projected,
    mix_two,
    rows,
    filt,
    w_in,
    w_out,
    inc,
    first,
    sems,
):
    channels = rows.shape[1]
    per = channels // rows.shape[0]
    blocks = [pl.ds(b * channels, channels) for b in (2, 1, 0)]
    copies = fetch(
        [(filt_in, filt), (inc_in, inc), (w_out_in, w_out), (rows_in, rows)]
        + [(w_in_in.at[:, block], w_in.at[:, block]) for block in blocks],
        sems,
    )
    copies[0].wait()
    put_rows(first, filt[0], 0, 4 * per)
    put_rows(first, filt[1], per, 4 * per)
    for copy in copies[1:3]:
        copy.wait()
    mixed = mm_t(inc[...], w_out[...])
    mix_two[...] = mixed
    for copy in copies[3:5]:
        copy.wait()
    gate_two = mm(rows[...], w_in[:, blocks[0]]).astype(BF)
    projected[:, blocks[0]] = gate_two
    put_rows(first, mixed * gate_two.astype(F32), 3 * per, 4 * per)
    copies[5].wait()
    gate_one = mm(rows[...], w_in[:, blocks[1]]).astype(BF)
    projected[:, blocks[1]] = gate_one
    put_rows(first, gate_one, 2 * per, 4 * per)
    packed[...] = first[...].astype(BF)
    copies[6].wait()
    projected[:, blocks[2]] = mm(rows[...], w_in[:, blocks[2]]).astype(BF)


def pack_known(scratch, projected, conv, packed):
    channels = conv.shape[2]
    per = channels // conv.shape[1]
    gate_one = projected[:, pl.ds(channels, channels)].astype(F32)
    put_rows(scratch, projected[:, pl.ds(0, channels)], 0, 2 * per)
    put_rows(scratch, gate_one * conv[0].astype(F32), per, 2 * per)
    packed[...] = scratch[...].astype(BF)


def regrad_body(late, inc, done, w_out, projected, conv, packed, part_two, kept, scratch):
    size = inc.shape[0]
    channels = inc.shape[1]
    per = channels // size

    @pl.when(late[0] == 0)
    def _():
        kept[...] = inc[...]
        mix_two = mm_t(inc[...], w_out[...])
        part_two[...] = (mix_two * conv[1].astype(F32)).astype(BF)
        gate_two = projected[:, pl.ds(2 * channels, channels)].astype(F32)
        put_rows(scratch, mix_two * gate_two, 0, 2 * per)
        for k in range(per):
            scratch[pl.ds(per + k, size, stride=2 * per), :] = jnp.zeros((size, size), F32)
        packed[...] = scratch[...].astype(BF)

    @pl.when(late[0] == 1)
    def _():
        kept[...] = done[...]
        part_two[...] = jnp.zeros_like(part_two)
        pack_known(scratch, projected, conv, packed)


def signals(scratch, s, per):
    size = scratch.shape[1]
    stride = scratch.shape[0] // size
    return [scratch[pl.ds(s * per + k, size, stride=stride), :] for k in range(per)]


def send_rows(scratch, s, values):
    size = scratch.shape[1]
    stride = scratch.shape[0] // size
    for k, value in enumerate(values):
        scratch[pl.ds(s * len(values) + k, size, stride=stride), :] = value


def early_body(
    per,
    late,
    place,
    gains,
    data,
    projected,
    conv,
    outer_fwd,
    inner_fwd,
    inner_inv,
    outer_inv,
    turns,
    packed,
    spec,
    grad,
    known,
    out,
):
    size = data.shape[1]

    @pl.when(late[0] == 1)
    def _():
        known[...] = data[...].astype(F32)
        filt_two = to_spectrum(signals(known, 1, per), outer_fwd, inner_fwd, turns)
        grad_two = signals(known, 3, per)
        spec_two = to_spectrum(grad_two, outer_fwd, inner_fwd, turns)
        spec[1] = spec_two
        mixed = from_spectrum(conj_times(filt_two, spec_two), inner_inv, outer_inv, turns)
        mix_one = [mixed[k] + gain_of(gains, 1, k, place, size) * grad_two[k] for k in range(per)]
        send_rows(out, 1, mix_one)
        gate_one = signals(known, 2, per)
        grad_one = [mix_one[k] * gate_one[k] for k in range(per)]
        for k in range(per):
            grad[pl.ds(k * size, size), :] = grad_one[k]
        filt_one = to_spectrum(signals(known, 0, per), outer_fwd, inner_fwd, turns)
        spec_one = to_spectrum(grad_one, outer_fwd, inner_fwd, turns)
        spec[0] = spec_one
        mixed = from_spectrum(conj_times(filt_one, spec_one), inner_inv, outer_inv, turns)
        send_rows(out, 0, [mixed[k] + gain_of(gains, 0, k, place, size) * grad_one[k] for k in range(per)])
        packed[...] = out[...].astype(BF)

    @pl.when(late[0] == 0)
    def _():
        pack_known(out, projected, conv, packed)
        known[...] = data[...].astype(F32)
        grad[...] = jnp.zeros_like(grad)
        spec[0] = to_spectrum(signals(known, 0, per), outer_fwd, inner_fwd, turns)
        spec[1] = to_spectrum(signals(known, 1, per), outer_fwd, inner_fwd, turns)


def gain_of(gains, w, k, place, size):
    row = gains[pl.ds(w, 1), k * size : (k + 1) * size]
    lane = lax.broadcasted_iota(jnp.int32, row.shape, 1)
    return jnp.sum(jnp.where(lane == place[0], row, 0.0), axis=1, keepdims=True)


def skip_rows(per, grads, others, out):
    size = out.shape[1]
    rows = out.shape[0] // size
    lane = lax.broadcasted_iota(jnp.int32, (1, size), 1)
    skip_row = jnp.zeros((1, size), F32)
    for w in range(2):
        for k in range(per):
            term = grads[w][k] * others[w][k]
            total = jnp.sum(jnp.sum(term, axis=0, keepdims=True), axis=1, keepdims=True)
            high = total.astype(BF).astype(F32)
            skip_row = jnp.where(lane == w * per + k, high, skip_row)
            skip_row = jnp.where(lane == (2 + w) * per + k, total - high, skip_row)
    out[pl.ds(4 * per, size, stride=rows), :] = jnp.broadcast_to(skip_row, (size, size))
    for r in range(4 * per + 1, rows):
        out[pl.ds(r, size, stride=rows), :] = jnp.zeros((size, size), F32)


def late_body(
    per,
    late,
    place,
    gains,
    first,
    second,
    third,
    held,
    grad_held,
    spec,
    outer_fwd,
    inner_fwd,
    inner_inv,
    outer_inv,
    turns,
    packed,
    known,
    other,
    fresh,
    out,
):
    size = first.shape[1]
    fresh[...] = third[...].astype(F32)
    known[...] = first[...].astype(F32)

    @pl.when(late[0] == 0)
    def _():
        grad_two = signals(fresh, 0, per)
        spec_two = to_spectrum(grad_two, outer_fwd, inner_fwd, turns)
        mixed = from_spectrum(conj_times(held[1], spec_two), inner_inv, outer_inv, turns)
        mix_one = [mixed[k] + gain_of(gains, 1, k, place, size) * grad_two[k] for k in range(per)]
        send_rows(out, 1, mix_one)
        gate_one = signals(known, 2, per)
        grad_one = [mix_one[k] * gate_one[k] for k in range(per)]
        spec_one = to_spectrum(grad_one, outer_fwd, inner_fwd, turns)
        products = [
            conj_times(held[0], spec_one),
            conj_times(spec[0], spec_one),
            conj_times(spec[1], spec_two),
        ]
        mixed = from_spectrum(jnp.concatenate(products, axis=0), inner_inv, outer_inv, turns)
        send_rows(out, 2, mixed[per : 2 * per])
        send_rows(out, 3, mixed[2 * per :])
        send_rows(out, 0, [mixed[k] + gain_of(gains, 0, k, place, size) * grad_one[k] for k in range(per)])
        other[...] = second[...].astype(F32)
        skip_rows(
            per, (grad_one, grad_two), (signals(other, 0, per), signals(other, 1, per)), out
        )
        packed[...] = out[...].astype(BF)

    @pl.when(late[0] == 1)
    def _():
        values, gated = signals(fresh, 0, per), signals(fresh, 1, per)
        spec_one = to_spectrum(values, outer_fwd, inner_fwd, turns)
        spec_two = to_spectrum(gated, outer_fwd, inner_fwd, turns)
        send_rows(out, 2, from_spectrum(conj_times(spec_one, held[0]), inner_inv, outer_inv, turns))
        send_rows(out, 3, from_spectrum(conj_times(spec_two, held[1]), inner_inv, outer_inv, turns))
        empty = [jnp.zeros((size, size), F32)] * per
        send_rows(out, 0, empty)
        send_rows(out, 1, empty)
        grad_one = [grad_held[pl.ds(k * size, size), :] for k in range(per)]
        skip_rows(per, (grad_one, signals(known, 3, per)), (values, gated), out)
        packed[...] = out[...].astype(BF)


def input_grad(inc, values, mix_one, conv_one, part_two, w_in):
    gate_one = mix_one.astype(F32) * conv_one.astype(F32)
    proj = jnp.concatenate([values.astype(BF), gate_one.astype(BF), part_two], axis=1)
    return (inc.astype(F32) + mm_t(proj, w_in)).astype(BF)


def hand_body(
    per,
    late,
    data,
    conv,
    mix_two,
    inc,
    w_in,
    outer_fwd,
    inner_fwd,
    turns,
    result,
    spec,
    scratch,
):
    @pl.when(late[0] == 1)
    def _():
        scratch[...] = data[...].astype(F32)
        values = get_rows(scratch, 0, 2 * per, per)
        mix_one = get_rows(scratch, per, 2 * per, per)
        part_two = (mix_two[...] * conv[1].astype(F32)).astype(BF)
        result[...] = input_grad(inc[...], values, mix_one, conv[0], part_two, w_in[...])

    @pl.when(late[0] == 0)
    def _():
        scratch[...] = data[...].astype(F32)
        for s in range(2):
            spec[s] = to_spectrum(signals(scratch, s, per), outer_fwd, inner_fwd, turns)
        result[...] = jnp.zeros_like(result)


def finish_body(
    per,
    rescale,
    late,
    data,
    conv,
    part_two,
    inc,
    w_in,
    result_out,
    filt_out,
    skip_grads,
    scratch,
    result,
    filt_grads,
    sems,
):
    size = data.shape[1]
    stride = data.shape[0] // size
    scratch[...] = data[...].astype(F32)
    copies = []
    for s in range(2):
        filt_grads[s] = (
            get_rows(scratch, (2 + s) * per, stride, per).astype(F32) * rescale
        ).astype(BF)
        copies.append(pltpu.make_async_copy(filt_grads.at[s], filt_out.at[s], sems.at[s]))
        copies[s].start()

    @pl.when(late[0] == 0)
    def _():
        values = get_rows(scratch, 0, stride, per)
        mix_one = get_rows(scratch, per, stride, per)
        result[...] = input_grad(inc[...], values, mix_one, conv[0], part_two[...], w_in[...])

    @pl.when(late[0] == 1)
    def _():
        result[...] = inc[...]

    copies.append(pltpu.make_async_copy(result, result_out, sems.at[2]))
    copies[2].start()
    sums = scratch[pl.ds(4 * per, size, stride=stride), :].T
    sums = (sums[: 2 * per] + sums[2 * per : 4 * per]) * rescale
    for w in range(2):
        for k in range(per):
            row = w * per + k
            skip_grads[pl.ds(w, 1), pl.ds(k * size, size)] = sums[row : row + 1]
    for copy in copies:
        copy.wait()


def call(body, out_shapes, scratch, *operands, smem=0, direct=(), direct_out=(), limit=VMEM_LIMIT):
    def space(i):
        if i < smem:
            return pltpu.SMEM
        return pltpu.HBM if i in direct else pltpu.VMEM

    return pl.pallas_call(
        body,
        out_shape=[
            (pltpu.HBM if i in direct_out else jax.ShapeDtypeStruct)(shape, dtype)
            for i, (shape, dtype) in enumerate(out_shapes)
        ],
        in_specs=[pl.BlockSpec(memory_space=space(i)) for i in range(len(operands))],
        out_specs=[
            pl.BlockSpec(memory_space=pltpu.HBM if i in direct_out else pltpu.VMEM)
            for i in range(len(out_shapes))
        ],
        scratch_shapes=[
            pltpu.VMEM(shape, F32) if isinstance(shape, tuple) else shape for shape in scratch
        ],
        compiler_params=pltpu.CompilerParams(vmem_limit_bytes=limit),
    )(
        *[
            pltpu.with_memory_space_constraint(x, pltpu.HBM) if i in direct else x
            for i, x in enumerate(operands)
        ]
    )


def exchange(rows, parts):
    per_part = rows.shape[0] // parts
    tile = math.gcd(per_part, 2)
    cut = rows.reshape(parts, per_part // tile, tile, rows.shape[1])
    return lax.all_to_all(cut, "seq", split_axis=0, concat_axis=0, tiled=True).reshape(rows.shape)


def on_device(layer_input, conv_out, filters, skip_gain, weight_in, weight_out, grad_output):
    tokens, channels = grad_output.shape
    parts = lax.axis_size("seq")
    per = channels // parts
    w_in, w_out, conv = weight_in[0], weight_out[0], conv_out[0]
    outer_fwd, inner_fwd, inner_inv, outer_inv, turns = transform_tables(parts, tokens)
    late = lax.axis_index("section").astype(jnp.int32).reshape(1)
    place = lax.axis_index("seq").astype(jnp.int32).reshape(1)

    def rows(count):
        return (parts * count, tokens)

    token_rows = ((tokens, channels), BF)
    spectra = ((2, per * parts, 2 * tokens), F32)

    packed, projected, mix_two = call(
        prepare_body,
        [(rows(4 * per), BF), ((tokens, 3 * channels), BF), ((tokens, channels), F32)],
        [
            pltpu.VMEM((tokens, channels), BF),
            pltpu.VMEM((2, tokens, channels), BF),
            pltpu.VMEM(w_in.shape, BF),
            pltpu.VMEM(w_out.shape, BF),
            pltpu.VMEM((tokens, channels), BF),
            rows(4 * per),
            pltpu.SemaphoreType.DMA((7,)),
        ],
        layer_input[0], filters[0], w_in, w_out, grad_output,
        direct=range(5),
    )
    packed, late, place = lax.optimization_barrier((packed, late, place))
    first = exchange(packed, parts)
    packed, held, grad_held = call(
        functools.partial(early_body, per),
        [(rows(2 * per), BF), spectra, (rows(per), F32)],
        [rows(4 * per), rows(2 * per)],
        late, place, skip_gain[0], first, projected, conv, outer_fwd, inner_fwd, inner_inv, outer_inv, turns,
        smem=2,
    )
    second = exchange(packed, parts)
    done, spec = call(
        functools.partial(hand_body, per),
        [token_rows, spectra],
        [
            rows(2 * per),
        ],
        late, second, conv, mix_two, grad_output, w_in, outer_fwd, inner_fwd, turns,
        smem=1,
    )
    handed = lax.ppermute(done, "section", [(0, 1), (1, 0)])
    packed, part_two, kept = call(
        regrad_body,
        [(rows(2 * per), BF), token_rows, token_rows],
        [rows(2 * per)],
        late, handed, done, w_out, projected, conv,
        smem=1,
    )
    third = exchange(packed, parts)
    out_rows = 4 * per + 2
    (packed,) = call(
        functools.partial(late_body, per),
        [(rows(out_rows), BF)],
        [
            rows(4 * per), rows(2 * per), rows(2 * per), rows(out_rows),
        ],
        late, place, skip_gain[0], first, second, third, held, grad_held, spec,
        outer_fwd, inner_fwd, inner_inv, outer_inv, turns,
        smem=2,
    )
    back = exchange(packed, parts)
    grad_rows, filter_grads, skip_grads = call(
        functools.partial(finish_body, per, 1.0 / math.sqrt(parts * tokens)),
        [token_rows, ((2, tokens, channels), BF), ((2, channels), F32)],
        [
            rows(out_rows), pltpu.VMEM((tokens, channels), BF),
            pltpu.VMEM((2, tokens, channels), BF), pltpu.SemaphoreType.DMA((3,)),
        ],
        late, back, conv, part_two, kept, w_in,
        smem=1, direct_out=(0, 1),
    )
    return (grad_rows[None], filter_grads[None], skip_grads[None])


def solution(mesh):
    in_specs = (
        P("section", "seq", None),
        P("section", None, "seq", None),
        P("section", None, "seq", None),
        P("section", None, None),
        P("section", None, None),
        P("section", None, None),
        P("seq", None),
    )
    out_specs = (
        P("section", "seq", None),
        P("section", None, "seq", None),
        P("section", None, None),
    )
    return jax.shard_map(
        on_device, mesh=mesh, in_specs=in_specs, out_specs=out_specs, check_vma=False
    )
```

```python
import functools
import math

import jax
import jax.numpy as jnp
import ml_dtypes
import numpy as np
from jax import lax
from jax.experimental import pallas as pl
from jax.experimental.pallas import tpu as pltpu
from jax.sharding import PartitionSpec as P

BF = jnp.bfloat16
F32 = jnp.float32
VMEM_LIMIT = 20 * 1024 * 1024


def split_table(table, axis):
    high = table.astype(np.float32).astype(ml_dtypes.bfloat16)
    low = (table - high.astype(np.float64)).astype(np.float32).astype(ml_dtypes.bfloat16)
    return np.concatenate([high, low], axis=axis)


def transform_tables(blocks, width):
    period = 2 * blocks * width
    half = np.arange(blocks) + 0.5
    outer = 2.0 * np.pi * np.outer(half, np.arange(blocks)) / (2 * blocks)
    inner = 2.0 * np.pi * np.outer(np.arange(width), np.arange(width)) / width
    turn = 2.0 * np.pi * np.outer(half, np.arange(width)) / period
    cos_in, sin_in = np.cos(inner), np.sin(inner)
    outer_fwd = split_table(np.concatenate([np.cos(outer), -np.sin(outer)], 0), 1)
    inner_fwd = split_table(np.block([[cos_in, -sin_in], [sin_in, cos_in]]), 0)
    inner_inv = np.block([[cos_in, sin_in], [-sin_in, cos_in]]).astype(ml_dtypes.bfloat16)
    outer_inv = split_table(
        np.concatenate([np.cos(outer).T, -np.sin(outer).T], 1) * (2.0 / period), 1
    )
    turns = np.stack([np.cos(turn), np.sin(turn)]).astype(np.float32)
    return outer_fwd, inner_fwd, inner_inv, outer_inv, turns


def mm(left, right):
    return jnp.dot(left, right, preferred_element_type=F32)


def mm_t(left, right):
    return lax.dot_general(left, right, (((1,), (1,)), ((), ())), preferred_element_type=F32)


def to_spectrum(signals, outer, inner, turns):
    count = len(signals)
    size = signals[0].shape[0]
    width = signals[0].shape[1]
    data = jnp.concatenate([signal.astype(BF) for signal in signals], axis=1)
    mixed = mm(outer[...], jnp.concatenate([data, data], axis=0))
    turn_cos, turn_sin = turns[0], turns[1]
    rows = []
    for c in range(count):
        real = mixed[:size, c * width : (c + 1) * width]
        imag = mixed[size:, c * width : (c + 1) * width]
        rows.append(
            jnp.concatenate(
                [real * turn_cos + imag * turn_sin, imag * turn_cos - real * turn_sin], axis=1
            ).astype(BF)
        )
    turned = jnp.concatenate(rows, axis=0)
    return mm(jnp.concatenate([turned, turned], axis=1), inner[...])


def conj_times(left, right):
    width = left.shape[1] // 2
    left_real, left_imag = left[:, :width], left[:, width:]
    right_real, right_imag = right[:, :width], right[:, width:]
    return jnp.concatenate(
        [
            left_real * right_real + left_imag * right_imag,
            left_real * right_imag - left_imag * right_real,
        ],
        axis=1,
    )


def from_spectrum(product, inner, outer, turns):
    width = product.shape[1] // 2
    size = turns.shape[1]
    count = product.shape[0] // size
    data = product.astype(BF)
    mixed = mm(data, inner[...])
    turn_cos, turn_sin = turns[0], turns[1]
    reals, imags = [], []
    for c in range(count):
        real = mixed[c * size : (c + 1) * size, :width]
        imag = mixed[c * size : (c + 1) * size, width:]
        reals.append((real * turn_cos - imag * turn_sin).astype(BF))
        imags.append((imag * turn_cos + real * turn_sin).astype(BF))
    turned = jnp.concatenate(
        [jnp.concatenate(reals, axis=1), jnp.concatenate(imags, axis=1)], axis=0
    )
    result = mm(outer[...], jnp.concatenate([turned, turned], axis=0))
    return [result[:, c * width : (c + 1) * width] for c in range(count)]


def put_rows(scratch, value, first, stride):
    size = value.shape[0]
    for k in range(value.shape[1] // size):
        block = value[:, k * size : (k + 1) * size].astype(BF).T
        scratch[pl.ds(first + k, size, stride=stride), :] = block.astype(F32)


def get_rows(scratch, first, stride, count):
    size = scratch.shape[1]
    return jnp.concatenate(
        [scratch[pl.ds(first + k, size, stride=stride), :].astype(BF).T for k in range(count)],
        axis=1,
    )


def fetch(pairs, sems):
    copies = [
        pltpu.make_async_copy(source, target, sems.at[i])
        for i, (source, target) in enumerate(pairs)
    ]
    for copy in copies:
        copy.start()
    return copies


def prepare_body(
    rows_in,
    filt_in,
    w_in_in,
    w_out_in,
    inc_in,
    packed,
    gates,
    mix_two,
    rows,
    w_in,
    w_out,
    inc,
    filt,
    first,
    sems,
):
    channels = rows.shape[1]
    per = channels // rows.shape[0]
    blocks = [pl.ds(b * channels, channels) for b in (2, 1, 0)]
    copies = fetch(
        [(filt_in, filt), (inc_in, inc), (w_out_in, w_out), (rows_in, rows)]
        + [(w_in_in.at[:, block], w_in.at[:, block]) for block in blocks],
        sems,
    )
    copies[0].wait()
    put_rows(first, filt[0], 0, 4 * per)
    put_rows(first, filt[1], per, 4 * per)
    for copy in copies[1:3]:
        copy.wait()
    mixed = mm_t(inc[...], w_out[...])
    mix_two[...] = mixed
    for copy in copies[3:5]:
        copy.wait()
    gate_two = mm(rows[...], w_in[:, blocks[0]]).astype(BF)
    gates[1] = gate_two
    put_rows(first, mixed * gate_two.astype(F32), 3 * per, 4 * per)
    copies[5].wait()
    gate_one = mm(rows[...], w_in[:, blocks[1]]).astype(BF)
    gates[0] = gate_one
    put_rows(first, gate_one, 2 * per, 4 * per)
    packed[...] = first[...].astype(BF)
    copies[6].wait()


def pack_known(scratch, rows, w_in, gates, conv, packed):
    channels = rows.shape[1]
    per = channels // rows.shape[0]
    values = mm(rows[...], w_in[:, pl.ds(0, channels)]).astype(BF)
    put_rows(scratch, values, 0, 2 * per)
    put_rows(scratch, gates[0].astype(F32) * conv[0].astype(F32), per, 2 * per)
    packed[...] = scratch[...].astype(BF)


def regrad_body(
    late, inc, done, w_out, rows, w_in, gates, conv, packed, part_two, kept, scratch
):
    size = inc.shape[0]
    channels = inc.shape[1]
    per = channels // size

    @pl.when(late[0] == 0)
    def _():
        kept[...] = inc[...]
        mix_two = mm_t(inc[...], w_out[...])
        part_two[...] = (mix_two * conv[1].astype(F32)).astype(BF)
        put_rows(scratch, mix_two * gates[1].astype(F32), 0, 2 * per)
        for k in range(per):
            scratch[pl.ds(per + k, size, stride=2 * per), :] = jnp.zeros((size, size), F32)
        packed[...] = scratch[...].astype(BF)

    @pl.when(late[0] == 1)
    def _():
        kept[...] = done[...]
        part_two[...] = jnp.zeros_like(part_two)
        pack_known(scratch, rows, w_in, gates, conv, packed)


def signals(scratch, s, per):
    size = scratch.shape[1]
    stride = scratch.shape[0] // size
    return [scratch[pl.ds(s * per + k, size, stride=stride), :] for k in range(per)]


def send_rows(scratch, s, values):
    size = scratch.shape[1]
    stride = scratch.shape[0] // size
    for k, value in enumerate(values):
        scratch[pl.ds(s * len(values) + k, size, stride=stride), :] = value


def early_body(
    per,
    late,
    place,
    gains,
    data,
    rows,
    w_in,
    gates,
    conv,
    outer_fwd,
    inner_fwd,
    inner_inv,
    outer_inv,
    turns,
    packed,
    spec,
    grad,
    known,
    out,
):
    size = data.shape[1]

    @pl.when(late[0] == 1)
    def _():
        known[...] = data[...].astype(F32)
        filt_two = to_spectrum(signals(known, 1, per), outer_fwd, inner_fwd, turns)
        grad_two = signals(known, 3, per)
        spec_two = to_spectrum(grad_two, outer_fwd, inner_fwd, turns)
        spec[1] = spec_two
        mixed = from_spectrum(conj_times(filt_two, spec_two), inner_inv, outer_inv, turns)
        mix_one = [mixed[k] + gain_of(gains, 1, k, place, size) * grad_two[k] for k in range(per)]
        send_rows(out, 1, mix_one)
        gate_one = signals(known, 2, per)
        grad_one = [mix_one[k] * gate_one[k] for k in range(per)]
        for k in range(per):
            grad[pl.ds(k * size, size), :] = grad_one[k]
        filt_one = to_spectrum(signals(known, 0, per), outer_fwd, inner_fwd, turns)
        spec_one = to_spectrum(grad_one, outer_fwd, inner_fwd, turns)
        spec[0] = spec_one
        mixed = from_spectrum(conj_times(filt_one, spec_one), inner_inv, outer_inv, turns)
        send_rows(out, 0, [mixed[k] + gain_of(gains, 0, k, place, size) * grad_one[k] for k in range(per)])
        packed[...] = out[...].astype(BF)

    @pl.when(late[0] == 0)
    def _():
        pack_known(out, rows, w_in, gates, conv, packed)
        known[...] = data[...].astype(F32)
        for k, gate_one in enumerate(signals(known, 2, per)):
            grad[pl.ds(k * size, size), :] = gate_one
        spec[0] = to_spectrum(signals(known, 0, per), outer_fwd, inner_fwd, turns)
        spec[1] = to_spectrum(signals(known, 1, per), outer_fwd, inner_fwd, turns)


def gain_of(gains, w, k, place, size):
    row = gains[pl.ds(w, 1), k * size : (k + 1) * size]
    lane = lax.broadcasted_iota(jnp.int32, row.shape, 1)
    return jnp.sum(jnp.where(lane == place[0], row, 0.0), axis=1, keepdims=True)


def skip_rows(per, grads, others, out):
    size = out.shape[1]
    rows = out.shape[0] // size
    lane = lax.broadcasted_iota(jnp.int32, (1, size), 1)
    skip_row = jnp.zeros((1, size), F32)
    for w in range(2):
        for k in range(per):
            term = grads[w][k] * others[w][k]
            total = jnp.sum(jnp.sum(term, axis=0, keepdims=True), axis=1, keepdims=True)
            high = total.astype(BF).astype(F32)
            skip_row = jnp.where(lane == w * per + k, high, skip_row)
            skip_row = jnp.where(lane == (2 + w) * per + k, total - high, skip_row)
    out[pl.ds(4 * per, size, stride=rows), :] = jnp.broadcast_to(skip_row, (size, size))
    for r in range(4 * per + 1, rows):
        out[pl.ds(r, size, stride=rows), :] = jnp.zeros((size, size), F32)


def late_body(
    per,
    late,
    place,
    gains,
    first,
    plain,
    third,
    held,
    grad_held,
    spec,
    outer_fwd,
    inner_fwd,
    inner_inv,
    outer_inv,
    turns,
    packed,
    known,
    fresh,
    out,
):
    size = first.shape[1]
    fresh[...] = third[...].astype(F32)

    @pl.when(late[0] == 0)
    def _():
        grad_two = signals(fresh, 0, per)
        spec_two = to_spectrum(grad_two, outer_fwd, inner_fwd, turns)
        mixed = from_spectrum(conj_times(held[1], spec_two), inner_inv, outer_inv, turns)
        send_rows(out, 3, from_spectrum(conj_times(spec[1], spec_two), inner_inv, outer_inv, turns))
        mix_one = [mixed[k] + gain_of(gains, 1, k, place, size) * grad_two[k] for k in range(per)]
        send_rows(out, 1, mix_one)
        gate_one = [grad_held[pl.ds(k * size, size), :] for k in range(per)]
        grad_one = [mix_one[k] * gate_one[k] for k in range(per)]
        spec_one = to_spectrum(grad_one, outer_fwd, inner_fwd, turns)
        mixed = from_spectrum(conj_times(held[0], spec_one), inner_inv, outer_inv, turns)
        send_rows(out, 2, from_spectrum(conj_times(spec[0], spec_one), inner_inv, outer_inv, turns))
        send_rows(out, 0, [mixed[k] + gain_of(gains, 0, k, place, size) * grad_one[k] for k in range(per)])
        others = [
            [plain[pl.ds((s * per + k) * size, size), :] for k in range(per)] for s in range(2)
        ]
        skip_rows(per, (grad_one, grad_two), others, out)
        packed[...] = out[...].astype(BF)

    @pl.when(late[0] == 1)
    def _():
        known[...] = first[...].astype(F32)
        values, gated = signals(fresh, 0, per), signals(fresh, 1, per)
        spec_one = to_spectrum(values, outer_fwd, inner_fwd, turns)
        spec_two = to_spectrum(gated, outer_fwd, inner_fwd, turns)
        send_rows(out, 2, from_spectrum(conj_times(spec_one, held[0]), inner_inv, outer_inv, turns))
        send_rows(out, 3, from_spectrum(conj_times(spec_two, held[1]), inner_inv, outer_inv, turns))
        empty = [jnp.zeros((size, size), F32)] * per
        send_rows(out, 0, empty)
        send_rows(out, 1, empty)
        grad_one = [grad_held[pl.ds(k * size, size), :] for k in range(per)]
        skip_rows(per, (grad_one, signals(known, 3, per)), (values, gated), out)
        packed[...] = out[...].astype(BF)


def input_grad(inc, values, mix_one, conv_one, part_two, w_in):
    gate_one = mix_one.astype(F32) * conv_one.astype(F32)
    proj = jnp.concatenate([values.astype(BF), gate_one.astype(BF), part_two], axis=1)
    return (inc.astype(F32) + mm_t(proj, w_in)).astype(BF)


def hand_body(
    per,
    late,
    data,
    conv,
    mix_two,
    inc,
    w_in,
    outer_fwd,
    inner_fwd,
    turns,
    result,
    spec,
    plain,
    scratch,
):
    @pl.when(late[0] == 1)
    def _():
        scratch[...] = data[...].astype(F32)
        values = get_rows(scratch, 0, 2 * per, per)
        mix_one = get_rows(scratch, per, 2 * per, per)
        part_two = (mix_two[...] * conv[1].astype(F32)).astype(BF)
        result[...] = input_grad(inc[...], values, mix_one, conv[0], part_two, w_in[...])

    @pl.when(late[0] == 0)
    def _():
        scratch[...] = data[...].astype(F32)
        size = data.shape[1]
        for s in range(2):
            blocks = signals(scratch, s, per)
            for k in range(per):
                plain[pl.ds((s * per + k) * size, size), :] = blocks[k]
            spec[s] = to_spectrum(blocks, outer_fwd, inner_fwd, turns)
        result[...] = jnp.zeros_like(result)


def finish_body(
    per,
    rescale,
    late,
    data,
    conv,
    part_two,
    inc,
    w_in,
    result,
    filt_grads,
    skip_grads,
    scratch,
):
    size = data.shape[1]
    stride = data.shape[0] // size
    scratch[...] = data[...].astype(F32)

    @pl.when(late[0] == 0)
    def _():
        values = get_rows(scratch, 0, stride, per)
        mix_one = get_rows(scratch, per, stride, per)
        result[...] = input_grad(inc[...], values, mix_one, conv[0], part_two[...], w_in[...])

    @pl.when(late[0] == 1)
    def _():
        result[...] = inc[...]

    filt_grads[0] = (get_rows(scratch, 2 * per, stride, per).astype(F32) * rescale).astype(BF)
    filt_grads[1] = (get_rows(scratch, 3 * per, stride, per).astype(F32) * rescale).astype(BF)
    sums = scratch[pl.ds(4 * per, size, stride=stride), :].T
    sums = (sums[: 2 * per] + sums[2 * per : 4 * per]) * rescale
    for w in range(2):
        for k in range(per):
            row = w * per + k
            skip_grads[pl.ds(w, 1), pl.ds(k * size, size)] = sums[row : row + 1]


def call(body, out_shapes, scratch, *operands, smem=0, direct=(), direct_out=(), limit=VMEM_LIMIT):
    def space(i):
        if i < smem:
            return pltpu.SMEM
        return pltpu.HBM if i in direct else pltpu.VMEM

    return pl.pallas_call(
        body,
        out_shape=[
            (pltpu.HBM if i in direct_out else jax.ShapeDtypeStruct)(shape, dtype)
            for i, (shape, dtype) in enumerate(out_shapes)
        ],
        in_specs=[pl.BlockSpec(memory_space=space(i)) for i in range(len(operands))],
        out_specs=[
            pl.BlockSpec(memory_space=pltpu.HBM if i in direct_out else pltpu.VMEM)
            for i in range(len(out_shapes))
        ],
        scratch_shapes=[
            pltpu.VMEM(shape, F32) if isinstance(shape, tuple) else shape for shape in scratch
        ],
        compiler_params=pltpu.CompilerParams(vmem_limit_bytes=limit),
    )(
        *[
            pltpu.with_memory_space_constraint(x, pltpu.HBM) if i in direct else x
            for i, x in enumerate(operands)
        ]
    )


def exchange(rows, parts):
    per_part = rows.shape[0] // parts
    tile = math.gcd(per_part, 2)
    cut = rows.reshape(parts, per_part // tile, tile, rows.shape[1])
    return lax.all_to_all(cut, "seq", split_axis=0, concat_axis=0, tiled=True).reshape(rows.shape)


def on_device(layer_input, conv_out, filters, skip_gain, weight_in, weight_out, grad_output):
    tokens, channels = grad_output.shape
    parts = lax.axis_size("seq")
    per = channels // parts
    w_in, w_out, conv = weight_in[0], weight_out[0], conv_out[0]
    outer_fwd, inner_fwd, inner_inv, outer_inv, turns = transform_tables(parts, tokens)
    late = lax.axis_index("section").astype(jnp.int32).reshape(1)
    place = lax.axis_index("seq").astype(jnp.int32).reshape(1)

    def rows(count):
        return (parts * count, tokens)

    token_rows = ((tokens, channels), BF)
    spectra = ((2, per * parts, 2 * tokens), F32)

    packed, gates, mix_two, rows_in, w_in, w_out, incoming = call(
        prepare_body,
        [
            (rows(4 * per), BF), ((2, tokens, channels), BF), ((tokens, channels), F32),
            token_rows, (w_in.shape, BF), (w_out.shape, BF), token_rows,
        ],
        [
            pltpu.VMEM((2, tokens, channels), BF), rows(4 * per), pltpu.SemaphoreType.DMA((7,)),
        ],
        layer_input[0], filters[0], w_in, w_out, grad_output,
        direct=range(5),
    )
    packed, late, place = lax.optimization_barrier((packed, late, place))
    first = exchange(packed, parts)
    packed, held, grad_held = call(
        functools.partial(early_body, per),
        [(rows(2 * per), BF), spectra, (rows(per), F32)],
        [rows(4 * per), rows(2 * per)],
        late, place, skip_gain[0], first, rows_in, w_in, gates, conv,
        outer_fwd, inner_fwd, inner_inv, outer_inv, turns,
        smem=2,
    )
    second = exchange(packed, parts)
    done, spec, plain = call(
        functools.partial(hand_body, per),
        [token_rows, spectra, (rows(2 * per), F32)],
        [
            rows(2 * per),
        ],
        late, second, conv, mix_two, incoming, w_in, outer_fwd, inner_fwd, turns,
        smem=1,
    )
    handed = lax.ppermute(done, "section", [(0, 1), (1, 0)])
    packed, part_two, kept = call(
        regrad_body,
        [(rows(2 * per), BF), token_rows, token_rows],
        [rows(2 * per)],
        late, handed, done, w_out, rows_in, w_in, gates, conv,
        smem=1,
    )
    third = exchange(packed, parts)
    out_rows = 4 * per + 2
    (packed,) = call(
        functools.partial(late_body, per),
        [(rows(out_rows), BF)],
        [
            rows(4 * per), rows(2 * per), rows(out_rows),
        ],
        late, place, skip_gain[0], first, plain, third, held, grad_held, spec,
        outer_fwd, inner_fwd, inner_inv, outer_inv, turns,
        smem=2,
    )
    back = exchange(packed, parts)
    grad_rows, filter_grads, skip_grads = call(
        functools.partial(finish_body, per, 1.0 / math.sqrt(parts * tokens)),
        [token_rows, ((2, tokens, channels), BF), ((2, channels), F32)],
        [rows(out_rows)],
        late, back, conv, part_two, kept, w_in,
        smem=1,
    )
    return (grad_rows[None], filter_grads[None], skip_grads[None])


def solution(mesh):
    in_specs = (
        P("section", "seq", None),
        P("section", None, "seq", None),
        P("section", None, "seq", None),
        P("section", None, None),
        P("section", None, None),
        P("section", None, None),
        P("seq", None),
    )
    out_specs = (
        P("section", "seq", None),
        P("section", None, "seq", None),
        P("section", None, None),
    )
    return jax.shard_map(
        on_device, mesh=mesh, in_specs=in_specs, out_specs=out_specs, check_vma=False
    )
```

```python
import functools
import math

import jax
import jax.numpy as jnp
import ml_dtypes
import numpy as np
from jax import lax
from jax.experimental import pallas as pl
from jax.experimental.pallas import tpu as pltpu
from jax.sharding import PartitionSpec as P

BF = jnp.bfloat16
F32 = jnp.float32
VMEM_LIMIT = 20 * 1024 * 1024


def split_table(table, axis):
    high = table.astype(np.float32).astype(ml_dtypes.bfloat16)
    low = (table - high.astype(np.float64)).astype(np.float32).astype(ml_dtypes.bfloat16)
    return np.concatenate([high, low], axis=axis)


def transform_tables(blocks, width):
    period = 2 * blocks * width
    half = np.arange(blocks) + 0.5
    outer = 2.0 * np.pi * np.outer(half, np.arange(blocks)) / (2 * blocks)
    inner = 2.0 * np.pi * np.outer(np.arange(width), np.arange(width)) / width
    turn = 2.0 * np.pi * np.outer(half, np.arange(width)) / period
    cos_in, sin_in = np.cos(inner), np.sin(inner)
    outer_fwd = split_table(np.concatenate([np.cos(outer), -np.sin(outer)], 0), 1)
    inner_fwd = split_table(np.block([[cos_in, -sin_in], [sin_in, cos_in]]), 0)
    inner_inv = np.block([[cos_in, sin_in], [-sin_in, cos_in]]).astype(ml_dtypes.bfloat16)
    outer_inv = split_table(
        np.concatenate([np.cos(outer).T, -np.sin(outer).T], 1) * (2.0 / period), 1
    )
    turns = np.stack([np.cos(turn), np.sin(turn)]).astype(np.float32)
    return outer_fwd, inner_fwd, inner_inv, outer_inv, turns


def mm(left, right):
    return jnp.dot(left, right, preferred_element_type=F32)


def mm_t(left, right):
    return lax.dot_general(left, right, (((1,), (1,)), ((), ())), preferred_element_type=F32)


def to_spectrum(signals, outer, inner, turns):
    count = len(signals)
    size = signals[0].shape[0]
    width = signals[0].shape[1]
    data = jnp.concatenate([signal.astype(BF) for signal in signals], axis=1)
    mixed = mm(outer[...], jnp.concatenate([data, data], axis=0))
    turn_cos, turn_sin = turns[0], turns[1]
    rows = []
    for c in range(count):
        real = mixed[:size, c * width : (c + 1) * width]
        imag = mixed[size:, c * width : (c + 1) * width]
        rows.append(
            jnp.concatenate(
                [real * turn_cos + imag * turn_sin, imag * turn_cos - real * turn_sin], axis=1
            ).astype(BF)
        )
    turned = jnp.concatenate(rows, axis=0)
    return mm(jnp.concatenate([turned, turned], axis=1), inner[...])


def conj_times(left, right):
    width = left.shape[1] // 2
    left_real, left_imag = left[:, :width], left[:, width:]
    right_real, right_imag = right[:, :width], right[:, width:]
    return jnp.concatenate(
        [
            left_real * right_real + left_imag * right_imag,
            left_real * right_imag - left_imag * right_real,
        ],
        axis=1,
    )


def from_spectrum(product, inner, outer, turns):
    width = product.shape[1] // 2
    size = turns.shape[1]
    count = product.shape[0] // size
    data = product.astype(BF)
    mixed = mm(data, inner[...])
    turn_cos, turn_sin = turns[0], turns[1]
    reals, imags = [], []
    for c in range(count):
        real = mixed[c * size : (c + 1) * size, :width]
        imag = mixed[c * size : (c + 1) * size, width:]
        reals.append((real * turn_cos - imag * turn_sin).astype(BF))
        imags.append((imag * turn_cos + real * turn_sin).astype(BF))
    turned = jnp.concatenate(
        [jnp.concatenate(reals, axis=1), jnp.concatenate(imags, axis=1)], axis=0
    )
    result = mm(outer[...], jnp.concatenate([turned, turned], axis=0))
    return [result[:, c * width : (c + 1) * width] for c in range(count)]


def put_rows(scratch, value, first, stride):
    size = value.shape[0]
    for k in range(value.shape[1] // size):
        block = value[:, k * size : (k + 1) * size].astype(BF).T
        scratch[pl.ds(first + k, size, stride=stride), :] = block.astype(F32)


def get_rows(scratch, first, stride, count):
    size = scratch.shape[1]
    return jnp.concatenate(
        [scratch[pl.ds(first + k, size, stride=stride), :].astype(BF).T for k in range(count)],
        axis=1,
    )


def fetch(pairs, sems):
    copies = [
        pltpu.make_async_copy(source, target, sems.at[i])
        for i, (source, target) in enumerate(pairs)
    ]
    for copy in copies:
        copy.start()
    return copies


def prepare_body(
    rows_in,
    filt_in,
    w_in_in,
    w_out_in,
    inc_in,
    packed,
    gates,
    mix_two,
    rows,
    w_in,
    w_out,
    inc,
    filt,
    first,
    sems,
):
    channels = rows.shape[1]
    per = channels // rows.shape[0]
    blocks = [pl.ds(b * channels, channels) for b in (2, 1, 0)]
    copies = fetch(
        [(filt_in, filt), (inc_in, inc), (w_out_in, w_out), (rows_in, rows)]
        + [(w_in_in.at[:, block], w_in.at[:, block]) for block in blocks],
        sems,
    )
    copies[0].wait()
    put_rows(first, filt[0], 0, 4 * per)
    put_rows(first, filt[1], per, 4 * per)
    for copy in copies[1:3]:
        copy.wait()
    mixed = mm_t(inc[...], w_out[...])
    mix_two[...] = mixed
    for copy in copies[3:5]:
        copy.wait()
    gate_two = mm(rows[...], w_in[:, blocks[0]]).astype(BF)
    gates[1] = gate_two
    put_rows(first, mixed * gate_two.astype(F32), 3 * per, 4 * per)
    copies[5].wait()
    gate_one = mm(rows[...], w_in[:, blocks[1]]).astype(BF)
    gates[0] = gate_one
    put_rows(first, gate_one, 2 * per, 4 * per)
    packed[...] = first[...].astype(BF)
    copies[6].wait()


def pack_known(scratch, rows, w_in, gates, conv, packed):
    channels = rows.shape[1]
    per = channels // rows.shape[0]
    values = mm(rows[...], w_in[:, pl.ds(0, channels)]).astype(BF)
    put_rows(scratch, values, 0, 2 * per)
    put_rows(scratch, gates[0].astype(F32) * conv[0].astype(F32), per, 2 * per)
    packed[...] = scratch[...].astype(BF)


def regrad_body(
    late, inc, done, w_out, rows, w_in, gates, conv, packed, part_two, kept, scratch
):
    size = inc.shape[0]
    channels = inc.shape[1]
    per = channels // size

    @pl.when(late[0] == 0)
    def _():
        kept[...] = inc[...]
        mix_two = mm_t(inc[...], w_out[...])
        part_two[...] = (mix_two * conv[1].astype(F32)).astype(BF)
        put_rows(scratch, mix_two * gates[1].astype(F32), 0, 2 * per)
        for k in range(per):
            scratch[pl.ds(per + k, size, stride=2 * per), :] = jnp.zeros((size, size), F32)
        packed[...] = scratch[...].astype(BF)

    @pl.when(late[0] == 1)
    def _():
        kept[...] = done[...]
        part_two[...] = jnp.zeros_like(part_two)
        pack_known(scratch, rows, w_in, gates, conv, packed)


def signals(scratch, s, per):
    size = scratch.shape[1]
    stride = scratch.shape[0] // size
    return [scratch[pl.ds(s * per + k, size, stride=stride), :] for k in range(per)]


def send_rows(scratch, s, values):
    size = scratch.shape[1]
    stride = scratch.shape[0] // size
    for k, value in enumerate(values):
        scratch[pl.ds(s * len(values) + k, size, stride=stride), :] = value


def early_body(
    per,
    late,
    place,
    gains,
    data,
    rows,
    w_in,
    gates,
    conv,
    outer_fwd,
    inner_fwd,
    inner_inv,
    outer_inv,
    turns,
    packed,
    spec,
    grad,
    known,
    out,
):
    size = data.shape[1]

    @pl.when(late[0] == 1)
    def _():
        known[...] = data[...].astype(F32)
        filt_two = to_spectrum(signals(known, 1, per), outer_fwd, inner_fwd, turns)
        grad_two = signals(known, 3, per)
        spec_two = to_spectrum(grad_two, outer_fwd, inner_fwd, turns)
        spec[1] = spec_two
        mixed = from_spectrum(conj_times(filt_two, spec_two), inner_inv, outer_inv, turns)
        mix_one = [mixed[k] + gain_of(gains, 1, k, place, size) * grad_two[k] for k in range(per)]
        send_rows(out, 1, mix_one)
        gate_one = signals(known, 2, per)
        grad_one = [mix_one[k] * gate_one[k] for k in range(per)]
        for k in range(per):
            grad[pl.ds(k * size, size), :] = grad_one[k]
        filt_one = to_spectrum(signals(known, 0, per), outer_fwd, inner_fwd, turns)
        spec_one = to_spectrum(grad_one, outer_fwd, inner_fwd, turns)
        spec[0] = spec_one
        mixed = from_spectrum(conj_times(filt_one, spec_one), inner_inv, outer_inv, turns)
        send_rows(out, 0, [mixed[k] + gain_of(gains, 0, k, place, size) * grad_one[k] for k in range(per)])
        packed[...] = out[...].astype(BF)

    @pl.when(late[0] == 0)
    def _():
        pack_known(out, rows, w_in, gates, conv, packed)
        known[...] = data[...].astype(F32)
        for k, gate_one in enumerate(signals(known, 2, per)):
            grad[pl.ds(k * size, size), :] = gate_one
        spec[0] = to_spectrum(signals(known, 0, per), outer_fwd, inner_fwd, turns)
        spec[1] = to_spectrum(signals(known, 1, per), outer_fwd, inner_fwd, turns)


def gain_of(gains, w, k, place, size):
    row = gains[pl.ds(w, 1), k * size : (k + 1) * size]
    lane = lax.broadcasted_iota(jnp.int32, row.shape, 1)
    return jnp.sum(jnp.where(lane == place[0], row, 0.0), axis=1, keepdims=True)


def skip_rows(per, grads, others, out):
    size = out.shape[1]
    rows = out.shape[0] // size
    lane = lax.broadcasted_iota(jnp.int32, (1, size), 1)
    skip_row = jnp.zeros((1, size), F32)
    for w in range(2):
        for k in range(per):
            term = grads[w][k] * others[w][k]
            total = jnp.sum(jnp.sum(term, axis=0, keepdims=True), axis=1, keepdims=True)
            high = total.astype(BF).astype(F32)
            skip_row = jnp.where(lane == w * per + k, high, skip_row)
            skip_row = jnp.where(lane == (2 + w) * per + k, total - high, skip_row)
    out[pl.ds(4 * per, size, stride=rows), :] = jnp.broadcast_to(skip_row, (size, size))
    for r in range(4 * per + 1, rows):
        out[pl.ds(r, size, stride=rows), :] = jnp.zeros((size, size), F32)


def late_body(
    per,
    late,
    place,
    gains,
    first,
    plain,
    third,
    held,
    grad_held,
    spec,
    outer_fwd,
    inner_fwd,
    inner_inv,
    outer_inv,
    turns,
    packed,
    known,
    fresh,
    out,
):
    size = first.shape[1]
    fresh[...] = third[...].astype(F32)

    @pl.when(late[0] == 0)
    def _():
        grad_two = signals(fresh, 0, per)
        spec_two = to_spectrum(grad_two, outer_fwd, inner_fwd, turns)
        mixed = from_spectrum(conj_times(held[1], spec_two), inner_inv, outer_inv, turns)
        send_rows(out, 3, from_spectrum(conj_times(spec[1], spec_two), inner_inv, outer_inv, turns))
        mix_one = [mixed[k] + gain_of(gains, 1, k, place, size) * grad_two[k] for k in range(per)]
        send_rows(out, 1, mix_one)
        gate_one = [grad_held[pl.ds(k * size, size), :] for k in range(per)]
        grad_one = [mix_one[k] * gate_one[k] for k in range(per)]
        spec_one = to_spectrum(grad_one, outer_fwd, inner_fwd, turns)
        mixed = from_spectrum(conj_times(held[0], spec_one), inner_inv, outer_inv, turns)
        send_rows(out, 2, from_spectrum(conj_times(spec[0], spec_one), inner_inv, outer_inv, turns))
        send_rows(out, 0, [mixed[k] + gain_of(gains, 0, k, place, size) * grad_one[k] for k in range(per)])
        others = [
            [plain[pl.ds((s * per + k) * size, size), :] for k in range(per)] for s in range(2)
        ]
        skip_rows(per, (grad_one, grad_two), others, out)
        packed[...] = out[...].astype(BF)

    @pl.when(late[0] == 1)
    def _():
        known[...] = first[...].astype(F32)
        values, gated = signals(fresh, 0, per), signals(fresh, 1, per)
        spec_one = to_spectrum(values, outer_fwd, inner_fwd, turns)
        spec_two = to_spectrum(gated, outer_fwd, inner_fwd, turns)
        send_rows(out, 2, from_spectrum(conj_times(spec_one, held[0]), inner_inv, outer_inv, turns))
        send_rows(out, 3, from_spectrum(conj_times(spec_two, held[1]), inner_inv, outer_inv, turns))
        empty = [jnp.zeros((size, size), F32)] * per
        send_rows(out, 0, empty)
        send_rows(out, 1, empty)
        grad_one = [grad_held[pl.ds(k * size, size), :] for k in range(per)]
        skip_rows(per, (grad_one, signals(known, 3, per)), (values, gated), out)
        packed[...] = out[...].astype(BF)


def input_grad(inc, values, mix_one, conv_one, part_two, w_in):
    gate_one = mix_one.astype(F32) * conv_one.astype(F32)
    proj = jnp.concatenate([values.astype(BF), gate_one.astype(BF), part_two], axis=1)
    return (inc.astype(F32) + mm_t(proj, w_in)).astype(BF)


def hand_body(
    per,
    late,
    data,
    conv,
    mix_two,
    inc,
    w_in,
    outer_fwd,
    inner_fwd,
    turns,
    result,
    spec,
    plain,
    scratch,
):
    @pl.when(late[0] == 1)
    def _():
        scratch[...] = data[...].astype(F32)
        values = get_rows(scratch, 0, 2 * per, per)
        mix_one = get_rows(scratch, per, 2 * per, per)
        part_two = (mix_two[...] * conv[1].astype(F32)).astype(BF)
        result[...] = input_grad(inc[...], values, mix_one, conv[0], part_two, w_in[...])

    @pl.when(late[0] == 0)
    def _():
        scratch[...] = data[...].astype(F32)
        size = data.shape[1]
        for s in range(2):
            blocks = signals(scratch, s, per)
            for k in range(per):
                plain[pl.ds((s * per + k) * size, size), :] = blocks[k]
            spec[s] = to_spectrum(blocks, outer_fwd, inner_fwd, turns)
        result[...] = jnp.zeros_like(result)


def finish_body(
    per,
    rescale,
    late,
    data,
    conv,
    part_two,
    inc,
    w_in,
    result_out,
    filt_out,
    skip_out,
    scratch,
    result,
    filt_grads,
    skip_grads,
    sems,
):
    size = data.shape[1]
    stride = data.shape[0] // size
    scratch[...] = data[...].astype(F32)
    sums = scratch[pl.ds(4 * per, size, stride=stride), :].T
    sums = (sums[: 2 * per] + sums[2 * per : 4 * per]) * rescale
    for w in range(2):
        for k in range(per):
            row = w * per + k
            skip_grads[pl.ds(w, 1), pl.ds(k * size, size)] = sums[row : row + 1]
    copies = [pltpu.make_async_copy(skip_grads, skip_out, sems.at[0])]
    copies[0].start()
    for s in range(2):
        filt_grads[s] = (
            get_rows(scratch, (2 + s) * per, stride, per).astype(F32) * rescale
        ).astype(BF)
        copies.append(pltpu.make_async_copy(filt_grads.at[s], filt_out.at[s], sems.at[1 + s]))
        copies[1 + s].start()

    @pl.when(late[0] == 0)
    def _():
        values = get_rows(scratch, 0, stride, per)
        mix_one = get_rows(scratch, per, stride, per)
        result[...] = input_grad(inc[...], values, mix_one, conv[0], part_two[...], w_in[...])

    @pl.when(late[0] == 1)
    def _():
        result[...] = inc[...]

    copies.append(pltpu.make_async_copy(result, result_out, sems.at[3]))
    copies[3].start()
    for copy in copies:
        copy.wait()


def call(body, out_shapes, scratch, *operands, smem=0, direct=(), direct_out=(), limit=VMEM_LIMIT):
    def space(i):
        if i < smem:
            return pltpu.SMEM
        return pltpu.HBM if i in direct else pltpu.VMEM

    return pl.pallas_call(
        body,
        out_shape=[
            (pltpu.HBM if i in direct_out else jax.ShapeDtypeStruct)(shape, dtype)
            for i, (shape, dtype) in enumerate(out_shapes)
        ],
        in_specs=[pl.BlockSpec(memory_space=space(i)) for i in range(len(operands))],
        out_specs=[
            pl.BlockSpec(memory_space=pltpu.HBM if i in direct_out else pltpu.VMEM)
            for i in range(len(out_shapes))
        ],
        scratch_shapes=[
            pltpu.VMEM(shape, F32) if isinstance(shape, tuple) else shape for shape in scratch
        ],
        compiler_params=pltpu.CompilerParams(vmem_limit_bytes=limit),
    )(
        *[
            pltpu.with_memory_space_constraint(x, pltpu.HBM) if i in direct else x
            for i, x in enumerate(operands)
        ]
    )


def exchange(rows, parts):
    per_part = rows.shape[0] // parts
    tile = math.gcd(per_part, 2)
    cut = rows.reshape(parts, per_part // tile, tile, rows.shape[1])
    return lax.all_to_all(cut, "seq", split_axis=0, concat_axis=0, tiled=True).reshape(rows.shape)


def on_device(layer_input, conv_out, filters, skip_gain, weight_in, weight_out, grad_output):
    tokens, channels = grad_output.shape
    parts = lax.axis_size("seq")
    per = channels // parts
    w_in, w_out, conv = weight_in[0], weight_out[0], conv_out[0]
    outer_fwd, inner_fwd, inner_inv, outer_inv, turns = transform_tables(parts, tokens)
    late = lax.axis_index("section").astype(jnp.int32).reshape(1)
    place = lax.axis_index("seq").astype(jnp.int32).reshape(1)

    def rows(count):
        return (parts * count, tokens)

    token_rows = ((tokens, channels), BF)
    spectra = ((2, per * parts, 2 * tokens), F32)

    packed, gates, mix_two, rows_in, w_in, w_out, incoming = call(
        prepare_body,
        [
            (rows(4 * per), BF), ((2, tokens, channels), BF), ((tokens, channels), F32),
            token_rows, (w_in.shape, BF), (w_out.shape, BF), token_rows,
        ],
        [
            pltpu.VMEM((2, tokens, channels), BF), rows(4 * per), pltpu.SemaphoreType.DMA((7,)),
        ],
        layer_input[0], filters[0], w_in, w_out, grad_output,
        direct=range(5),
    )
    packed, late, place = lax.optimization_barrier((packed, late, place))
    first = exchange(packed, parts)
    packed, held, grad_held = call(
        functools.partial(early_body, per),
        [(rows(2 * per), BF), spectra, (rows(per), F32)],
        [rows(4 * per), rows(2 * per)],
        late, place, skip_gain[0], first, rows_in, w_in, gates, conv,
        outer_fwd, inner_fwd, inner_inv, outer_inv, turns,
        smem=2,
    )
    second = exchange(packed, parts)
    done, spec, plain = call(
        functools.partial(hand_body, per),
        [token_rows, spectra, (rows(2 * per), F32)],
        [
            rows(2 * per),
        ],
        late, second, conv, mix_two, incoming, w_in, outer_fwd, inner_fwd, turns,
        smem=1,
    )
    handed = lax.ppermute(done, "section", [(0, 1), (1, 0)])
    packed, part_two, kept = call(
        regrad_body,
        [(rows(2 * per), BF), token_rows, token_rows],
        [rows(2 * per)],
        late, handed, done, w_out, rows_in, w_in, gates, conv,
        smem=1,
    )
    third = exchange(packed, parts)
    out_rows = 4 * per + 2
    (packed,) = call(
        functools.partial(late_body, per),
        [(rows(out_rows), BF)],
        [
            rows(4 * per), rows(2 * per), rows(out_rows),
        ],
        late, place, skip_gain[0], first, plain, third, held, grad_held, spec,
        outer_fwd, inner_fwd, inner_inv, outer_inv, turns,
        smem=2,
    )
    back = exchange(packed, parts)
    grad_rows, filter_grads, skip_grads = call(
        functools.partial(finish_body, per, 1.0 / math.sqrt(parts * tokens)),
        [token_rows, ((2, tokens, channels), BF), ((2, channels), F32)],
        [
            rows(out_rows), pltpu.VMEM((tokens, channels), BF),
            pltpu.VMEM((2, tokens, channels), BF), (2, channels), pltpu.SemaphoreType.DMA((4,)),
        ],
        late, back, conv, part_two, kept, w_in,
        smem=1, direct_out=range(3),
    )
    return (grad_rows[None], filter_grads[None], skip_grads[None])


def solution(mesh):
    in_specs = (
        P("section", "seq", None),
        P("section", None, "seq", None),
        P("section", None, "seq", None),
        P("section", None, None),
        P("section", None, None),
        P("section", None, None),
        P("seq", None),
    )
    out_specs = (
        P("section", "seq", None),
        P("section", None, "seq", None),
        P("section", None, None),
    )
    return jax.shard_map(
        on_device, mesh=mesh, in_specs=in_specs, out_specs=out_specs, check_vma=False
    )
```

```python
import functools
import math

import jax
import jax.numpy as jnp
import ml_dtypes
import numpy as np
from jax import lax
from jax.experimental import pallas as pl
from jax.experimental.pallas import tpu as pltpu
from jax.sharding import PartitionSpec as P

BF = jnp.bfloat16
F32 = jnp.float32
VMEM_LIMIT = 20 * 1024 * 1024


def split_table(table, axis):
    high = table.astype(np.float32).astype(ml_dtypes.bfloat16)
    low = (table - high.astype(np.float64)).astype(np.float32).astype(ml_dtypes.bfloat16)
    return np.concatenate([high, low], axis=axis)


def transform_tables(blocks, width):
    period = 2 * blocks * width
    half = np.arange(blocks) + 0.5
    outer = 2.0 * np.pi * np.outer(half, np.arange(blocks)) / (2 * blocks)
    inner = 2.0 * np.pi * np.outer(np.arange(width), np.arange(width)) / width
    turn = 2.0 * np.pi * np.outer(half, np.arange(width)) / period
    cos_in, sin_in = np.cos(inner), np.sin(inner)
    outer_fwd = split_table(np.concatenate([np.cos(outer), -np.sin(outer)], 0), 1)
    inner_fwd = split_table(np.block([[cos_in, -sin_in], [sin_in, cos_in]]), 0)
    inner_inv = np.block([[cos_in, sin_in], [-sin_in, cos_in]]).astype(ml_dtypes.bfloat16)
    outer_inv = split_table(
        np.concatenate([np.cos(outer).T, -np.sin(outer).T], 1) * (2.0 / period), 1
    )
    turns = np.stack([np.cos(turn), np.sin(turn)]).astype(np.float32)
    return outer_fwd, inner_fwd, inner_inv, outer_inv, turns


def mm(left, right):
    return jnp.dot(left, right, preferred_element_type=F32)


def mm_t(left, right):
    return lax.dot_general(left, right, (((1,), (1,)), ((), ())), preferred_element_type=F32)


def to_spectrum(signals, outer, inner, turns):
    count = len(signals)
    size = signals[0].shape[0]
    width = signals[0].shape[1]
    data = jnp.concatenate([signal.astype(BF) for signal in signals], axis=1)
    mixed = mm(outer[...], jnp.concatenate([data, data], axis=0))
    turn_cos, turn_sin = turns[0], turns[1]
    rows = []
    for c in range(count):
        real = mixed[:size, c * width : (c + 1) * width]
        imag = mixed[size:, c * width : (c + 1) * width]
        rows.append(
            jnp.concatenate(
                [real * turn_cos + imag * turn_sin, imag * turn_cos - real * turn_sin], axis=1
            ).astype(BF)
        )
    turned = jnp.concatenate(rows, axis=0)
    return mm(jnp.concatenate([turned, turned], axis=1), inner[...])


def conj_times(left, right):
    width = left.shape[1] // 2
    left_real, left_imag = left[:, :width], left[:, width:]
    right_real, right_imag = right[:, :width], right[:, width:]
    return jnp.concatenate(
        [
            left_real * right_real + left_imag * right_imag,
            left_real * right_imag - left_imag * right_real,
        ],
        axis=1,
    )


def from_spectrum(product, inner, outer, turns):
    width = product.shape[1] // 2
    size = turns.shape[1]
    count = product.shape[0] // size
    data = product.astype(BF)
    mixed = mm(data, inner[...])
    turn_cos, turn_sin = turns[0], turns[1]
    reals, imags = [], []
    for c in range(count):
        real = mixed[c * size : (c + 1) * size, :width]
        imag = mixed[c * size : (c + 1) * size, width:]
        reals.append((real * turn_cos - imag * turn_sin).astype(BF))
        imags.append((imag * turn_cos + real * turn_sin).astype(BF))
    turned = jnp.concatenate(
        [jnp.concatenate(reals, axis=1), jnp.concatenate(imags, axis=1)], axis=0
    )
    result = mm(outer[...], jnp.concatenate([turned, turned], axis=0))
    return [result[:, c * width : (c + 1) * width] for c in range(count)]


def put_rows(scratch, value, first, stride):
    size = value.shape[0]
    for k in range(value.shape[1] // size):
        block = value[:, k * size : (k + 1) * size].astype(BF).T
        scratch[pl.ds(first + k, size, stride=stride), :] = block.astype(F32)


def get_rows(scratch, first, stride, count):
    size = scratch.shape[1]
    return jnp.concatenate(
        [scratch[pl.ds(first + k, size, stride=stride), :].astype(BF).T for k in range(count)],
        axis=1,
    )


def fetch(pairs, sems):
    copies = [
        pltpu.make_async_copy(source, target, sems.at[i])
        for i, (source, target) in enumerate(pairs)
    ]
    for copy in copies:
        copy.start()
    return copies


def prepare_body(
    late,
    place,
    rows_in,
    filt_in,
    w_in_in,
    w_out_in,
    inc_in,
    packed,
    gates,
    mix_two,
    rows,
    w_in,
    w_out,
    inc,
    filt,
    first,
    sems,
):
    channels = rows.shape[1]
    per = channels // rows.shape[0]
    blocks = [pl.ds(b * channels, channels) for b in (2, 1, 0)]
    copies = fetch(
        [(filt_in, filt), (inc_in, inc), (w_out_in, w_out), (rows_in, rows)]
        + [(w_in_in.at[:, block], w_in.at[:, block]) for block in blocks],
        sems,
    )
    copies[0].wait()
    put_rows(first, filt[0], 0, 4 * per)
    put_rows(first, filt[1], per, 4 * per)
    for copy in copies[1:3]:
        copy.wait()
    mixed = mm_t(inc[...], w_out[...])
    mix_two[...] = mixed
    for copy in copies[3:5]:
        copy.wait()
    gate_two = mm(rows[...], w_in[:, blocks[0]]).astype(BF)
    gates[1] = gate_two
    put_rows(first, mixed * gate_two.astype(F32), 3 * per, 4 * per)
    copies[5].wait()
    gate_one = mm(rows[...], w_in[:, blocks[1]]).astype(BF)
    gates[0] = gate_one
    put_rows(first, gate_one, 2 * per, 4 * per)
    packed[...] = first[...].astype(BF)
    copies[6].wait()


def pack_known(scratch, rows, w_in, gates, conv, packed):
    channels = rows.shape[1]
    per = channels // rows.shape[0]
    values = mm(rows[...], w_in[:, pl.ds(0, channels)]).astype(BF)
    put_rows(scratch, values, 0, 2 * per)
    put_rows(scratch, gates[0].astype(F32) * conv[0].astype(F32), per, 2 * per)
    packed[...] = scratch[...].astype(BF)


def regrad_body(
    late, inc, done, w_out, rows, w_in, gates, conv, packed, part_two, kept, scratch
):
    size = inc.shape[0]
    channels = inc.shape[1]
    per = channels // size

    @pl.when(late[0] == 0)
    def _():
        kept[...] = inc[...]
        mix_two = mm_t(inc[...], w_out[...])
        part_two[...] = (mix_two * conv[1].astype(F32)).astype(BF)
        put_rows(scratch, mix_two * gates[1].astype(F32), 0, 2 * per)
        for k in range(per):
            scratch[pl.ds(per + k, size, stride=2 * per), :] = jnp.zeros((size, size), F32)
        packed[...] = scratch[...].astype(BF)

    @pl.when(late[0] == 1)
    def _():
        kept[...] = done[...]
        part_two[...] = jnp.zeros_like(part_two)
        pack_known(scratch, rows, w_in, gates, conv, packed)


def signals(scratch, s, per):
    size = scratch.shape[1]
    stride = scratch.shape[0] // size
    return [scratch[pl.ds(s * per + k, size, stride=stride), :] for k in range(per)]


def send_rows(scratch, s, values):
    size = scratch.shape[1]
    stride = scratch.shape[0] // size
    for k, value in enumerate(values):
        scratch[pl.ds(s * len(values) + k, size, stride=stride), :] = value


def early_body(
    per,
    late,
    place,
    gains,
    data,
    rows,
    w_in,
    gates,
    conv,
    outer_fwd,
    inner_fwd,
    inner_inv,
    outer_inv,
    turns,
    packed,
    spec,
    grad,
    known,
    out,
):
    size = data.shape[1]

    @pl.when(late[0] == 1)
    def _():
        known[...] = data[...].astype(F32)
        filt_two = to_spectrum(signals(known, 1, per), outer_fwd, inner_fwd, turns)
        grad_two = signals(known, 3, per)
        spec_two = to_spectrum(grad_two, outer_fwd, inner_fwd, turns)
        spec[1] = spec_two
        mixed = from_spectrum(conj_times(filt_two, spec_two), inner_inv, outer_inv, turns)
        mix_one = [mixed[k] + gain_of(gains, 1, k, place, size) * grad_two[k] for k in range(per)]
        send_rows(out, 1, mix_one)
        gate_one = signals(known, 2, per)
        grad_one = [mix_one[k] * gate_one[k] for k in range(per)]
        for k in range(per):
            grad[pl.ds(k * size, size), :] = grad_one[k]
        filt_one = to_spectrum(signals(known, 0, per), outer_fwd, inner_fwd, turns)
        spec_one = to_spectrum(grad_one, outer_fwd, inner_fwd, turns)
        spec[0] = spec_one
        mixed = from_spectrum(conj_times(filt_one, spec_one), inner_inv, outer_inv, turns)
        send_rows(out, 0, [mixed[k] + gain_of(gains, 0, k, place, size) * grad_one[k] for k in range(per)])
        packed[...] = out[...].astype(BF)

    @pl.when(late[0] == 0)
    def _():
        pack_known(out, rows, w_in, gates, conv, packed)
        known[...] = data[...].astype(F32)
        for k, gate_one in enumerate(signals(known, 2, per)):
            grad[pl.ds(k * size, size), :] = gate_one
        spec[0] = to_spectrum(signals(known, 0, per), outer_fwd, inner_fwd, turns)
        spec[1] = to_spectrum(signals(known, 1, per), outer_fwd, inner_fwd, turns)


def gain_of(gains, w, k, place, size):
    row = gains[pl.ds(w, 1), k * size : (k + 1) * size]
    lane = lax.broadcasted_iota(jnp.int32, row.shape, 1)
    return jnp.sum(jnp.where(lane == place[0], row, 0.0), axis=1, keepdims=True)


def skip_rows(per, first, grads, others, out):
    size = out.shape[1]
    rows = out.shape[0] // size
    lane = lax.broadcasted_iota(jnp.int32, (1, size), 1)
    skip_row = jnp.zeros((1, size), F32)
    for w in range(2):
        for k in range(per):
            term = grads[w][k] * others[w][k]
            total = jnp.sum(jnp.sum(term, axis=0, keepdims=True), axis=1, keepdims=True)
            high = total.astype(BF).astype(F32)
            skip_row = jnp.where(lane == w * per + k, high, skip_row)
            skip_row = jnp.where(lane == (2 + w) * per + k, total - high, skip_row)
    out[pl.ds(first, size, stride=rows), :] = jnp.broadcast_to(skip_row, (size, size))
    for r in range(first + 1, rows):
        out[pl.ds(r, size, stride=rows), :] = jnp.zeros((size, size), F32)


def late_body(
    per,
    late,
    place,
    gains,
    first,
    plain,
    third,
    held,
    grad_held,
    spec,
    outer_fwd,
    inner_fwd,
    inner_inv,
    outer_inv,
    turns,
    packed,
    packed_late,
    known,
    fresh,
    out,
    out_late,
):
    size = first.shape[1]
    fresh[...] = third[...].astype(F32)

    @pl.when(late[0] == 0)
    def _():
        grad_two = signals(fresh, 0, per)
        spec_two = to_spectrum(grad_two, outer_fwd, inner_fwd, turns)
        mixed = from_spectrum(conj_times(held[1], spec_two), inner_inv, outer_inv, turns)
        send_rows(out, 3, from_spectrum(conj_times(spec[1], spec_two), inner_inv, outer_inv, turns))
        mix_one = [mixed[k] + gain_of(gains, 1, k, place, size) * grad_two[k] for k in range(per)]
        send_rows(out, 1, mix_one)
        gate_one = [grad_held[pl.ds(k * size, size), :] for k in range(per)]
        grad_one = [mix_one[k] * gate_one[k] for k in range(per)]
        spec_one = to_spectrum(grad_one, outer_fwd, inner_fwd, turns)
        mixed = from_spectrum(conj_times(held[0], spec_one), inner_inv, outer_inv, turns)
        send_rows(out, 2, from_spectrum(conj_times(spec[0], spec_one), inner_inv, outer_inv, turns))
        send_rows(out, 0, [mixed[k] + gain_of(gains, 0, k, place, size) * grad_one[k] for k in range(per)])
        others = [
            [plain[pl.ds((s * per + k) * size, size), :] for k in range(per)] for s in range(2)
        ]
        skip_rows(per, 4 * per, (grad_one, grad_two), others, out)
        packed[...] = out[...].astype(BF)

    @pl.when(late[0] == 1)
    def _():
        known[...] = first[...].astype(F32)
        values, gated = signals(fresh, 0, per), signals(fresh, 1, per)
        spec_one = to_spectrum(values, outer_fwd, inner_fwd, turns)
        spec_two = to_spectrum(gated, outer_fwd, inner_fwd, turns)
        for s, spec_in in enumerate((spec_one, spec_two)):
            product = conj_times(spec_in, held[s])
            send_rows(out_late, s, from_spectrum(product, inner_inv, outer_inv, turns))
        grad_one = [grad_held[pl.ds(k * size, size), :] for k in range(per)]
        grads = (grad_one, signals(known, 3, per))
        skip_rows(per, 2 * per, grads, (values, gated), out_late)
        packed_late[...] = out_late[...].astype(BF)


def input_grad(inc, values, mix_one, conv_one, part_two, w_in):
    gate_one = mix_one.astype(F32) * conv_one.astype(F32)
    proj = jnp.concatenate([values.astype(BF), gate_one.astype(BF), part_two], axis=1)
    return (inc.astype(F32) + mm_t(proj, w_in)).astype(BF)


def hand_body(
    per,
    late,
    data,
    conv,
    mix_two,
    inc,
    w_in,
    outer_fwd,
    inner_fwd,
    turns,
    result,
    spec,
    plain,
    scratch,
):
    @pl.when(late[0] == 1)
    def _():
        scratch[...] = data[...].astype(F32)
        values = get_rows(scratch, 0, 2 * per, per)
        mix_one = get_rows(scratch, per, 2 * per, per)
        part_two = (mix_two[...] * conv[1].astype(F32)).astype(BF)
        result[...] = input_grad(inc[...], values, mix_one, conv[0], part_two, w_in[...])

    @pl.when(late[0] == 0)
    def _():
        scratch[...] = data[...].astype(F32)
        size = data.shape[1]
        for s in range(2):
            blocks = signals(scratch, s, per)
            for k in range(per):
                plain[pl.ds((s * per + k) * size, size), :] = blocks[k]
            spec[s] = to_spectrum(blocks, outer_fwd, inner_fwd, turns)
        result[...] = jnp.zeros_like(result)


def filter_and_skip(per, first, rescale, scratch, filt_grads, skip_grads):
    size = scratch.shape[1]
    stride = scratch.shape[0] // size
    for s in range(2):
        rows = get_rows(scratch, first + s * per, stride, per).astype(F32)
        filt_grads[s] = (rows * rescale).astype(BF)
    sums = scratch[pl.ds(first + 2 * per, size, stride=stride), :].T
    sums = (sums[: 2 * per] + sums[2 * per : 4 * per]) * rescale
    for w in range(2):
        for k in range(per):
            row = w * per + k
            skip_grads[pl.ds(w, 1), pl.ds(k * size, size)] = sums[row : row + 1]


def finish_early_body(
    per, rescale, data, conv, part_two, inc, w_in, result, filt_grads, skip_grads, scratch
):
    stride = data.shape[0] // data.shape[1]
    scratch[...] = data[...].astype(F32)
    values = get_rows(scratch, 0, stride, per)
    mix_one = get_rows(scratch, per, stride, per)
    result[...] = input_grad(inc[...], values, mix_one, conv[0], part_two[...], w_in[...])
    filter_and_skip(per, 2 * per, rescale, scratch, filt_grads, skip_grads)


def finish_late_body(per, rescale, data, inc, result, filt_grads, skip_grads, scratch):
    scratch[...] = data[...].astype(F32)
    result[...] = inc[...]
    filter_and_skip(per, 0, rescale, scratch, filt_grads, skip_grads)


def call(body, out_shapes, scratch, *operands, smem=0, direct=(), direct_out=(), limit=VMEM_LIMIT):
    def space(i):
        if i < smem:
            return pltpu.SMEM
        return pltpu.HBM if i in direct else pltpu.VMEM

    return pl.pallas_call(
        body,
        out_shape=[
            (pltpu.HBM if i in direct_out else jax.ShapeDtypeStruct)(shape, dtype)
            for i, (shape, dtype) in enumerate(out_shapes)
        ],
        in_specs=[pl.BlockSpec(memory_space=space(i)) for i in range(len(operands))],
        out_specs=[
            pl.BlockSpec(memory_space=pltpu.HBM if i in direct_out else pltpu.VMEM)
            for i in range(len(out_shapes))
        ],
        scratch_shapes=[
            pltpu.VMEM(shape, F32) if isinstance(shape, tuple) else shape for shape in scratch
        ],
        compiler_params=pltpu.CompilerParams(vmem_limit_bytes=limit),
    )(
        *[
            pltpu.with_memory_space_constraint(x, pltpu.HBM) if i in direct else x
            for i, x in enumerate(operands)
        ]
    )


def exchange(rows, parts):
    per_part = rows.shape[0] // parts
    tile = math.gcd(per_part, 2)
    cut = rows.reshape(parts, per_part // tile, tile, rows.shape[1])
    return lax.all_to_all(cut, "seq", split_axis=0, concat_axis=0, tiled=True).reshape(rows.shape)


def on_device(layer_input, conv_out, filters, skip_gain, weight_in, weight_out, grad_output):
    tokens, channels = grad_output.shape
    parts = lax.axis_size("seq")
    per = channels // parts
    w_in, w_out, conv = weight_in[0], weight_out[0], conv_out[0]
    outer_fwd, inner_fwd, inner_inv, outer_inv, turns = transform_tables(parts, tokens)
    is_late = lax.axis_index("section") == 1
    late = is_late.astype(jnp.int32).reshape(1)
    place = lax.axis_index("seq").astype(jnp.int32).reshape(1)

    def rows(count):
        return (parts * count, tokens)

    token_rows = ((tokens, channels), BF)
    spectra = ((2, per * parts, 2 * tokens), F32)

    packed, gates, mix_two, rows_in, w_in, w_out, incoming = call(
        prepare_body,
        [
            (rows(4 * per), BF), ((2, tokens, channels), BF), ((tokens, channels), F32),
            token_rows, (w_in.shape, BF), (w_out.shape, BF), token_rows,
        ],
        [
            pltpu.VMEM((2, tokens, channels), BF), rows(4 * per), pltpu.SemaphoreType.DMA((7,)),
        ],
        late, place, layer_input[0], filters[0], w_in, w_out, grad_output,
        smem=2, direct=range(2, 7),
    )
    first = exchange(packed, parts)
    packed, held, grad_held = call(
        functools.partial(early_body, per),
        [(rows(2 * per), BF), spectra, (rows(per), F32)],
        [rows(4 * per), rows(2 * per)],
        late, place, skip_gain[0], first, rows_in, w_in, gates, conv,
        outer_fwd, inner_fwd, inner_inv, outer_inv, turns,
        smem=2,
    )
    second = exchange(packed, parts)
    done, spec, plain = call(
        functools.partial(hand_body, per),
        [token_rows, spectra, (rows(2 * per), F32)],
        [
            rows(2 * per),
        ],
        late, second, conv, mix_two, incoming, w_in, outer_fwd, inner_fwd, turns,
        smem=1,
    )
    handed = lax.ppermute(done, "section", [(0, 1), (1, 0)])
    packed, part_two, kept = call(
        regrad_body,
        [(rows(2 * per), BF), token_rows, token_rows],
        [rows(2 * per)],
        late, handed, done, w_out, rows_in, w_in, gates, conv,
        smem=1,
    )
    third = exchange(packed, parts)
    out_rows = 4 * per + 2
    late_rows = 2 * per + 2
    packed, packed_late = call(
        functools.partial(late_body, per),
        [(rows(out_rows), BF), (rows(late_rows), BF)],
        [
            rows(4 * per), rows(2 * per), rows(out_rows), rows(late_rows),
        ],
        late, place, skip_gain[0], first, plain, third, held, grad_held, spec,
        outer_fwd, inner_fwd, inner_inv, outer_inv, turns,
        smem=2,
    )
    rescale = 1.0 / math.sqrt(parts * tokens)
    outputs = [token_rows, ((2, tokens, channels), BF), ((2, channels), F32)]

    def finish_early(packed, packed_late, conv, part_two, kept, w_in):
        return call(
            functools.partial(finish_early_body, per, rescale),
            outputs,
            [rows(out_rows)],
            exchange(packed, parts), conv, part_two, kept, w_in,
        )

    def finish_late(packed, packed_late, conv, part_two, kept, w_in):
        return call(
            functools.partial(finish_late_body, per, rescale),
            outputs,
            [rows(late_rows)],
            exchange(packed_late, parts), kept,
        )

    grad_rows, filter_grads, skip_grads = lax.cond(
        is_late, finish_late, finish_early, packed, packed_late, conv, part_two, kept, w_in
    )
    return (grad_rows[None], filter_grads[None], skip_grads[None])


def solution(mesh):
    in_specs = (
        P("section", "seq", None),
        P("section", None, "seq", None),
        P("section", None, "seq", None),
        P("section", None, None),
        P("section", None, None),
        P("section", None, None),
        P("seq", None),
    )
    out_specs = (
        P("section", "seq", None),
        P("section", None, "seq", None),
        P("section", None, None),
    )
    return jax.shard_map(
        on_device, mesh=mesh, in_specs=in_specs, out_specs=out_specs, check_vma=False
    )
```

```python
import functools
import math

import jax
import jax.numpy as jnp
import ml_dtypes
import numpy as np
from jax import lax
from jax.experimental import pallas as pl
from jax.experimental.pallas import tpu as pltpu
from jax.sharding import PartitionSpec as P

BF = jnp.bfloat16
F32 = jnp.float32
VMEM_LIMIT = 20 * 1024 * 1024


def split_table(table, axis):
    high = table.astype(np.float32).astype(ml_dtypes.bfloat16)
    low = (table - high.astype(np.float64)).astype(np.float32).astype(ml_dtypes.bfloat16)
    return np.concatenate([high, low], axis=axis)


def transform_tables(blocks, width):
    period = 2 * blocks * width
    half = np.arange(blocks) + 0.5
    outer = 2.0 * np.pi * np.outer(half, np.arange(blocks)) / (2 * blocks)
    inner = 2.0 * np.pi * np.outer(np.arange(width), np.arange(width)) / width
    turn = 2.0 * np.pi * np.outer(half, np.arange(width)) / period
    cos_in, sin_in = np.cos(inner), np.sin(inner)
    outer_fwd = split_table(np.concatenate([np.cos(outer), -np.sin(outer)], 0), 1)
    inner_fwd = split_table(np.block([[cos_in, -sin_in], [sin_in, cos_in]]), 0)
    inner_inv = np.block([[cos_in, sin_in], [-sin_in, cos_in]]).astype(ml_dtypes.bfloat16)
    outer_inv = split_table(
        np.concatenate([np.cos(outer).T, -np.sin(outer).T], 1) * (2.0 / period), 1
    )
    turns = np.stack([np.cos(turn), np.sin(turn)]).astype(np.float32)
    return outer_fwd, inner_fwd, inner_inv, outer_inv, turns


def mm(left, right):
    return jnp.dot(left, right, preferred_element_type=F32)


def mm_t(left, right):
    return lax.dot_general(left, right, (((1,), (1,)), ((), ())), preferred_element_type=F32)


def to_spectrum(signals, outer, inner, turns):
    count = len(signals)
    size = signals[0].shape[0]
    width = signals[0].shape[1]
    data = jnp.concatenate([signal.astype(BF) for signal in signals], axis=1)
    mixed = mm(outer[...], jnp.concatenate([data, data], axis=0))
    turn_cos, turn_sin = turns[0], turns[1]
    rows = []
    for c in range(count):
        real = mixed[:size, c * width : (c + 1) * width]
        imag = mixed[size:, c * width : (c + 1) * width]
        rows.append(
            jnp.concatenate(
                [real * turn_cos + imag * turn_sin, imag * turn_cos - real * turn_sin], axis=1
            ).astype(BF)
        )
    turned = jnp.concatenate(rows, axis=0)
    return mm(jnp.concatenate([turned, turned], axis=1), inner[...])


def conj_times(left, right):
    width = left.shape[1] // 2
    left_real, left_imag = left[:, :width], left[:, width:]
    right_real, right_imag = right[:, :width], right[:, width:]
    return jnp.concatenate(
        [
            left_real * right_real + left_imag * right_imag,
            left_real * right_imag - left_imag * right_real,
        ],
        axis=1,
    )


def from_spectrum(product, inner, outer, turns):
    width = product.shape[1] // 2
    size = turns.shape[1]
    count = product.shape[0] // size
    data = product.astype(BF)
    mixed = mm(data, inner[...])
    turn_cos, turn_sin = turns[0], turns[1]
    reals, imags = [], []
    for c in range(count):
        real = mixed[c * size : (c + 1) * size, :width]
        imag = mixed[c * size : (c + 1) * size, width:]
        reals.append((real * turn_cos - imag * turn_sin).astype(BF))
        imags.append((imag * turn_cos + real * turn_sin).astype(BF))
    turned = jnp.concatenate(
        [jnp.concatenate(reals, axis=1), jnp.concatenate(imags, axis=1)], axis=0
    )
    result = mm(outer[...], jnp.concatenate([turned, turned], axis=0))
    return [result[:, c * width : (c + 1) * width] for c in range(count)]


def put_rows(scratch, value, first, stride):
    size = value.shape[0]
    for k in range(value.shape[1] // size):
        block = value[:, k * size : (k + 1) * size].astype(BF).T
        scratch[pl.ds(first + k, size, stride=stride), :] = block.astype(F32)


def get_rows(scratch, first, stride, count):
    size = scratch.shape[1]
    return jnp.concatenate(
        [scratch[pl.ds(first + k, size, stride=stride), :].astype(BF).T for k in range(count)],
        axis=1,
    )


def fetch(pairs, sems):
    copies = [
        pltpu.make_async_copy(source, target, sems.at[i])
        for i, (source, target) in enumerate(pairs)
    ]
    for copy in copies:
        copy.start()
    return copies


def prepare_body(
    late,
    place,
    rows_in,
    filt_in,
    w_in_in,
    w_out_in,
    inc_in,
    packed,
    gates,
    mix_two,
    rows,
    w_in,
    w_out,
    inc,
    filt,
    first,
    sems,
):
    channels = rows.shape[1]
    per = channels // rows.shape[0]
    blocks = [pl.ds(b * channels, channels) for b in (2, 1, 0)]
    copies = fetch(
        [(filt_in, filt), (inc_in, inc), (w_out_in, w_out), (rows_in, rows)]
        + [(w_in_in.at[:, block], w_in.at[:, block]) for block in blocks],
        sems,
    )
    copies[0].wait()
    put_rows(first, filt[0], 0, 4 * per)
    put_rows(first, filt[1], per, 4 * per)
    for copy in copies[1:3]:
        copy.wait()
    mixed = mm_t(inc[...], w_out[...])
    mix_two[...] = mixed
    for copy in copies[3:5]:
        copy.wait()
    gate_two = mm(rows[...], w_in[:, blocks[0]]).astype(BF)
    gates[1] = gate_two
    put_rows(first, mixed * gate_two.astype(F32), 3 * per, 4 * per)
    copies[5].wait()
    gate_one = mm(rows[...], w_in[:, blocks[1]]).astype(BF)
    gates[0] = gate_one
    put_rows(first, gate_one, 2 * per, 4 * per)
    packed[...] = first[...].astype(BF)
    copies[6].wait()


def pack_known(scratch, rows, w_in, gates, conv, packed):
    channels = rows.shape[1]
    per = channels // rows.shape[0]
    values = mm(rows[...], w_in[:, pl.ds(0, channels)]).astype(BF)
    put_rows(scratch, values, 0, 2 * per)
    put_rows(scratch, gates[0].astype(F32) * conv[0].astype(F32), per, 2 * per)
    packed[...] = scratch[...].astype(BF)


def regrad_body(inc, w_out, gates, conv, packed, part_two, scratch):
    per = inc.shape[1] // inc.shape[0]
    mix_two = mm_t(inc[...], w_out[...])
    part_two[...] = (mix_two * conv[1].astype(F32)).astype(BF)
    put_rows(scratch, mix_two * gates[1].astype(F32), 0, per)
    packed[...] = scratch[...].astype(BF)


def known_body(rows, w_in, gates, conv, packed, scratch):
    pack_known(scratch, rows, w_in, gates, conv, packed)


def signals(scratch, s, per):
    size = scratch.shape[1]
    stride = scratch.shape[0] // size
    return [scratch[pl.ds(s * per + k, size, stride=stride), :] for k in range(per)]


def send_rows(scratch, s, values):
    size = scratch.shape[1]
    stride = scratch.shape[0] // size
    for k, value in enumerate(values):
        scratch[pl.ds(s * len(values) + k, size, stride=stride), :] = value


def early_body(
    per,
    late,
    place,
    gains,
    data,
    rows,
    w_in,
    gates,
    conv,
    outer_fwd,
    inner_fwd,
    inner_inv,
    outer_inv,
    turns,
    packed,
    spec,
    grad,
    known,
    out,
):
    size = data.shape[1]

    @pl.when(late[0] == 1)
    def _():
        known[...] = data[...].astype(F32)
        filt_two = to_spectrum(signals(known, 1, per), outer_fwd, inner_fwd, turns)
        grad_two = signals(known, 3, per)
        spec_two = to_spectrum(grad_two, outer_fwd, inner_fwd, turns)
        spec[1] = spec_two
        mixed = from_spectrum(conj_times(filt_two, spec_two), inner_inv, outer_inv, turns)
        mix_one = [mixed[k] + gain_of(gains, 1, k, place, size) * grad_two[k] for k in range(per)]
        send_rows(out, 1, mix_one)
        gate_one = signals(known, 2, per)
        grad_one = [mix_one[k] * gate_one[k] for k in range(per)]
        for k in range(per):
            grad[pl.ds(k * size, size), :] = grad_one[k]
        filt_one = to_spectrum(signals(known, 0, per), outer_fwd, inner_fwd, turns)
        spec_one = to_spectrum(grad_one, outer_fwd, inner_fwd, turns)
        spec[0] = spec_one
        mixed = from_spectrum(conj_times(filt_one, spec_one), inner_inv, outer_inv, turns)
        send_rows(out, 0, [mixed[k] + gain_of(gains, 0, k, place, size) * grad_one[k] for k in range(per)])
        packed[...] = out[...].astype(BF)

    @pl.when(late[0] == 0)
    def _():
        pack_known(out, rows, w_in, gates, conv, packed)
        known[...] = data[...].astype(F32)
        for k, gate_one in enumerate(signals(known, 2, per)):
            grad[pl.ds(k * size, size), :] = gate_one
        spec[0] = to_spectrum(signals(known, 0, per), outer_fwd, inner_fwd, turns)
        spec[1] = to_spectrum(signals(known, 1, per), outer_fwd, inner_fwd, turns)


def gain_of(gains, w, k, place, size):
    row = gains[pl.ds(w, 1), k * size : (k + 1) * size]
    lane = lax.broadcasted_iota(jnp.int32, row.shape, 1)
    return jnp.sum(jnp.where(lane == place[0], row, 0.0), axis=1, keepdims=True)


def skip_rows(per, first, grads, others, out):
    size = out.shape[1]
    rows = out.shape[0] // size
    lane = lax.broadcasted_iota(jnp.int32, (1, size), 1)
    skip_row = jnp.zeros((1, size), F32)
    for w in range(2):
        for k in range(per):
            term = grads[w][k] * others[w][k]
            total = jnp.sum(jnp.sum(term, axis=0, keepdims=True), axis=1, keepdims=True)
            high = total.astype(BF).astype(F32)
            skip_row = jnp.where(lane == w * per + k, high, skip_row)
            skip_row = jnp.where(lane == (2 + w) * per + k, total - high, skip_row)
    out[pl.ds(first, size, stride=rows), :] = jnp.broadcast_to(skip_row, (size, size))
    for r in range(first + 1, rows):
        out[pl.ds(r, size, stride=rows), :] = jnp.zeros((size, size), F32)


def early_tick_body(
    per,
    place,
    gains,
    plain,
    third,
    held,
    grad_held,
    spec,
    outer_fwd,
    inner_fwd,
    inner_inv,
    outer_inv,
    turns,
    packed,
    fresh,
    out,
):
    size = third.shape[1]
    fresh[...] = third[...].astype(F32)
    grad_two = signals(fresh, 0, per)
    spec_two = to_spectrum(grad_two, outer_fwd, inner_fwd, turns)
    mixed = from_spectrum(conj_times(held[1], spec_two), inner_inv, outer_inv, turns)
    send_rows(out, 3, from_spectrum(conj_times(spec[1], spec_two), inner_inv, outer_inv, turns))
    mix_one = [mixed[k] + gain_of(gains, 1, k, place, size) * grad_two[k] for k in range(per)]
    send_rows(out, 1, mix_one)
    gate_one = [grad_held[pl.ds(k * size, size), :] for k in range(per)]
    grad_one = [mix_one[k] * gate_one[k] for k in range(per)]
    spec_one = to_spectrum(grad_one, outer_fwd, inner_fwd, turns)
    mixed = from_spectrum(conj_times(held[0], spec_one), inner_inv, outer_inv, turns)
    send_rows(out, 2, from_spectrum(conj_times(spec[0], spec_one), inner_inv, outer_inv, turns))
    send_rows(out, 0, [mixed[k] + gain_of(gains, 0, k, place, size) * grad_one[k] for k in range(per)])
    others = [
        [plain[pl.ds((s * per + k) * size, size), :] for k in range(per)] for s in range(2)
    ]
    skip_rows(per, 4 * per, (grad_one, grad_two), others, out)
    packed[...] = out[...].astype(BF)


def late_tick_body(
    per,
    first,
    third,
    held,
    grad_held,
    outer_fwd,
    inner_fwd,
    inner_inv,
    outer_inv,
    turns,
    packed,
    known,
    fresh,
    out,
):
    size = third.shape[1]
    fresh[...] = third[...].astype(F32)
    known[...] = first[...].astype(F32)
    values, gated = signals(fresh, 0, per), signals(fresh, 1, per)
    spec_one = to_spectrum(values, outer_fwd, inner_fwd, turns)
    spec_two = to_spectrum(gated, outer_fwd, inner_fwd, turns)
    for s, spec_in in enumerate((spec_one, spec_two)):
        product = conj_times(spec_in, held[s])
        send_rows(out, s, from_spectrum(product, inner_inv, outer_inv, turns))
    grad_one = [grad_held[pl.ds(k * size, size), :] for k in range(per)]
    grads = (grad_one, signals(known, 3, per))
    skip_rows(per, 2 * per, grads, (values, gated), out)
    packed[...] = out[...].astype(BF)


def input_grad(inc, values, mix_one, conv_one, part_two, w_in):
    gate_one = mix_one.astype(F32) * conv_one.astype(F32)
    proj = jnp.concatenate([values.astype(BF), gate_one.astype(BF), part_two], axis=1)
    return (inc.astype(F32) + mm_t(proj, w_in)).astype(BF)


def hand_body(
    per,
    late,
    data,
    conv,
    mix_two,
    inc,
    w_in,
    outer_fwd,
    inner_fwd,
    turns,
    result,
    spec,
    plain,
    scratch,
):
    @pl.when(late[0] == 1)
    def _():
        scratch[...] = data[...].astype(F32)
        values = get_rows(scratch, 0, 2 * per, per)
        mix_one = get_rows(scratch, per, 2 * per, per)
        part_two = (mix_two[...] * conv[1].astype(F32)).astype(BF)
        result[...] = input_grad(inc[...], values, mix_one, conv[0], part_two, w_in[...])

    @pl.when(late[0] == 0)
    def _():
        scratch[...] = data[...].astype(F32)
        size = data.shape[1]
        for s in range(2):
            blocks = signals(scratch, s, per)
            for k in range(per):
                plain[pl.ds((s * per + k) * size, size), :] = blocks[k]
            spec[s] = to_spectrum(blocks, outer_fwd, inner_fwd, turns)
        result[...] = jnp.zeros_like(result)


def filter_and_skip(per, first, rescale, scratch, filt_grads, skip_grads):
    size = scratch.shape[1]
    stride = scratch.shape[0] // size
    for s in range(2):
        rows = get_rows(scratch, first + s * per, stride, per).astype(F32)
        filt_grads[s] = (rows * rescale).astype(BF)
    sums = scratch[pl.ds(first + 2 * per, size, stride=stride), :].T
    sums = (sums[: 2 * per] + sums[2 * per : 4 * per]) * rescale
    for w in range(2):
        for k in range(per):
            row = w * per + k
            skip_grads[pl.ds(w, 1), pl.ds(k * size, size)] = sums[row : row + 1]


def finish_early_body(
    per, rescale, data, conv, part_two, inc, w_in, result, filt_grads, skip_grads, scratch
):
    stride = data.shape[0] // data.shape[1]
    scratch[...] = data[...].astype(F32)
    values = get_rows(scratch, 0, stride, per)
    mix_one = get_rows(scratch, per, stride, per)
    result[...] = input_grad(inc[...], values, mix_one, conv[0], part_two[...], w_in[...])
    filter_and_skip(per, 2 * per, rescale, scratch, filt_grads, skip_grads)


def finish_late_body(per, rescale, data, inc, result, filt_grads, skip_grads, scratch):
    scratch[...] = data[...].astype(F32)
    result[...] = inc[...]
    filter_and_skip(per, 0, rescale, scratch, filt_grads, skip_grads)


def call(body, out_shapes, scratch, *operands, smem=0, direct=(), direct_out=(), limit=VMEM_LIMIT):
    def space(i):
        if i < smem:
            return pltpu.SMEM
        return pltpu.HBM if i in direct else pltpu.VMEM

    return pl.pallas_call(
        body,
        out_shape=[
            (pltpu.HBM if i in direct_out else jax.ShapeDtypeStruct)(shape, dtype)
            for i, (shape, dtype) in enumerate(out_shapes)
        ],
        in_specs=[pl.BlockSpec(memory_space=space(i)) for i in range(len(operands))],
        out_specs=[
            pl.BlockSpec(memory_space=pltpu.HBM if i in direct_out else pltpu.VMEM)
            for i in range(len(out_shapes))
        ],
        scratch_shapes=[
            pltpu.VMEM(shape, F32) if isinstance(shape, tuple) else shape for shape in scratch
        ],
        compiler_params=pltpu.CompilerParams(vmem_limit_bytes=limit),
    )(
        *[
            pltpu.with_memory_space_constraint(x, pltpu.HBM) if i in direct else x
            for i, x in enumerate(operands)
        ]
    )


def exchange(rows, parts):
    per_part = rows.shape[0] // parts
    tile = math.gcd(per_part, 2)
    cut = rows.reshape(parts, per_part // tile, tile, rows.shape[1])
    return lax.all_to_all(cut, "seq", split_axis=0, concat_axis=0, tiled=True).reshape(rows.shape)


def on_device(layer_input, conv_out, filters, skip_gain, weight_in, weight_out, grad_output):
    tokens, channels = grad_output.shape
    parts = lax.axis_size("seq")
    per = channels // parts
    w_in, w_out, conv = weight_in[0], weight_out[0], conv_out[0]
    outer_fwd, inner_fwd, inner_inv, outer_inv, turns = transform_tables(parts, tokens)
    is_late = lax.axis_index("section") == 1
    late = is_late.astype(jnp.int32).reshape(1)
    place = lax.axis_index("seq").astype(jnp.int32).reshape(1)

    def rows(count):
        return (parts * count, tokens)

    token_rows = ((tokens, channels), BF)
    spectra = ((2, per * parts, 2 * tokens), F32)

    packed, gates, mix_two, rows_in, w_in, w_out, incoming = call(
        prepare_body,
        [
            (rows(4 * per), BF), ((2, tokens, channels), BF), ((tokens, channels), F32),
            token_rows, (w_in.shape, BF), (w_out.shape, BF), token_rows,
        ],
        [
            pltpu.VMEM((2, tokens, channels), BF), rows(4 * per), pltpu.SemaphoreType.DMA((7,)),
        ],
        late, place, layer_input[0], filters[0], w_in, w_out, grad_output,
        smem=2, direct=range(2, 7),
    )
    first = exchange(packed, parts)
    packed, held, grad_held = call(
        functools.partial(early_body, per),
        [(rows(2 * per), BF), spectra, (rows(per), F32)],
        [rows(4 * per), rows(2 * per)],
        late, place, skip_gain[0], first, rows_in, w_in, gates, conv,
        outer_fwd, inner_fwd, inner_inv, outer_inv, turns,
        smem=2,
    )
    second = exchange(packed, parts)
    done, spec, plain = call(
        functools.partial(hand_body, per),
        [token_rows, spectra, (rows(2 * per), F32)],
        [
            rows(2 * per),
        ],
        late, second, conv, mix_two, incoming, w_in, outer_fwd, inner_fwd, turns,
        smem=1,
    )
    handed = lax.ppermute(done, "section", [(0, 1), (1, 0)])
    rescale = 1.0 / math.sqrt(parts * tokens)
    outputs = [token_rows, ((2, tokens, channels), BF), ((2, channels), F32)]
    tables = (outer_fwd, inner_fwd, inner_inv, outer_inv, turns)
    gains = skip_gain[0]

    def early_section():
        count = 4 * per + 2
        packed, part_two = call(
            regrad_body,
            [(rows(per), BF), token_rows],
            [rows(per)],
            handed, w_out, gates, conv,
        )
        third = exchange(packed, parts)
        (packed,) = call(
            functools.partial(early_tick_body, per),
            [(rows(count), BF)],
            [rows(per), rows(count)],
            place, gains, plain, third, held, grad_held, spec, *tables,
            smem=1,
        )
        return call(
            functools.partial(finish_early_body, per, rescale),
            outputs,
            [rows(count)],
            exchange(packed, parts), conv, part_two, handed, w_in,
        )

    def late_section():
        count = 2 * per + 2
        (packed,) = call(
            known_body,
            [(rows(2 * per), BF)],
            [rows(2 * per)],
            rows_in, w_in, gates, conv,
        )
        third = exchange(packed, parts)
        (packed,) = call(
            functools.partial(late_tick_body, per),
            [(rows(count), BF)],
            [rows(4 * per), rows(2 * per), rows(count)],
            first, third, held, grad_held, *tables,
        )
        return call(
            functools.partial(finish_late_body, per, rescale),
            outputs,
            [rows(count)],
            exchange(packed, parts), done,
        )

    grad_rows, filter_grads, skip_grads = lax.cond(is_late, late_section, early_section)
    return (grad_rows[None], filter_grads[None], skip_grads[None])


def solution(mesh):
    in_specs = (
        P("section", "seq", None),
        P("section", None, "seq", None),
        P("section", None, "seq", None),
        P("section", None, None),
        P("section", None, None),
        P("section", None, None),
        P("seq", None),
    )
    out_specs = (
        P("section", "seq", None),
        P("section", None, "seq", None),
        P("section", None, None),
    )
    return jax.shard_map(
        on_device, mesh=mesh, in_specs=in_specs, out_specs=out_specs, check_vma=False
    )
```
